32 devices in a mesh: dp: 2 (over y), fsdp: 16 (over z, x, core).
Axes of the slice: x: 2, y: 2, z: 4, core: 2. Of those that a mesh axis runs over, the one named last changes fastest.
Arguments:
- frames: bfloat16 [16, 2048, 1024], P('fsdp', 'dp'), may hold values from -6 to 6
- skip_in: bfloat16 [16, 2048, 1024], P('fsdp', 'dp'), may hold values from -6 to 6
- cond_in: bfloat16 [16, 2048, 1024], P('fsdp', 'dp'), may hold values from -6 to 6
- lengths: int32 [16, 8], P('fsdp'), may hold values from 1 to 1536, 2048 in all within a row
- drop_mask: int32 [16, 8], P('fsdp'), may hold values 0 or 1
- time_index: int32 [16, 8], P('fsdp'), may hold values from 0 to 999
- w_skip: bfloat16 [2048, 1024], P('dp', 'fsdp'), may hold values from -0.125 to 0.125
- w_qkv: bfloat16 [1024, 3072], P('dp', 'fsdp'), may hold values from -0.1875 to 0.1875
- w_out: bfloat16 [1024, 1024], P('dp', 'fsdp'), may hold values from -0.75 to 0.75
- w_up: bfloat16 [1024, 4096], P('dp', 'fsdp'), may hold values from -0.1875 to 0.1875
- w_down: bfloat16 [4096, 1024], P('dp', 'fsdp'), may hold values from -0.09375 to 0.09375
- w_mod: bfloat16 [1024, 4096], P('dp', 'fsdp'), may hold values from -0.1875 to 0.1875
- d_out: bfloat16 [16, 2048, 1024], P('fsdp', 'dp'), may hold values from -6 to 6
Outputs:
- output: bfloat16 [16, 2048, 1024], P('fsdp', 'dp')
- grad_frames: float32 [16, 2048, 1024], P('fsdp', 'dp')
- grad_skip: float32 [16, 2048, 1024], P('fsdp', 'dp')
- grad_w_skip: float32 [2048, 1024], P('dp', 'fsdp')
- grad_w_qkv: float32 [1024, 3072], P('dp', 'fsdp')
- grad_w_out: float32 [1024, 1024], P('dp', 'fsdp')
- grad_w_up: float32 [1024, 4096], P('dp', 'fsdp')
- grad_w_down: float32 [4096, 1024], P('dp', 'fsdp')
- grad_w_mod: float32 [1024, 4096], P('dp', 'fsdp')
The draws below stay inside these ranges and needn't reach their ends.
Inputs may be any that keep to these rules, and one draw needn't show every extreme that they name: `lengths`: each row sums to 2048; the largest length of every row is 1536.
All inputs are finite; a program needn't handle non-finite values. No bound on the sum of `drop_mask` on one device may be relied on, other than what follows from the above.
Results may differ from the reference program's by a relative error of at most 0.02.
Values may be sent and summed in bfloat16 or wider, within the bound.
No kernel may reach another device: no remote copies, remote signals or barrier semaphores. Data moves between devices by JAX's collectives and lax.ppermute only.
A program may use at most 384 MiB of HBM per device.

```python
import math
from functools import partial
import jax
import jax.numpy as jnp
import numpy as np
from jax import lax

D = 1024
FF = 4096
HD = 64
GROUP_TOK = 2048
UTT = 8
STEPS = 1000
GROUPS = 16
LONG = 1536


def touch_ends(drawn, rng, low, high):
    longest = drawn.shape.index(max(drawn.shape))
    spots = []
    for shift in (0, 1):
        where = [jax.random.randint(jax.random.fold_in(rng, axis), (), 0, length) for axis, length in enumerate(drawn.shape)]
        where[longest] = (where[longest] + shift) % drawn.shape[longest]
        spots.append(tuple(where))
    return drawn.at[spots[0]].set(low).at[spots[1]].set(high)


def levels(own_key, extent, pieces, smallest, largest):
    factor_of = 1.0
    for position, shards_of in pieces:
        draws = jax.random.uniform(jax.random.fold_in(jax.random.fold_in(own_key, 6), position), (shards_of,), jnp.float32, smallest / len(pieces), largest / len(pieces))
        factor_of = factor_of * jnp.repeat(jnp.exp(draws), extent[position] // shards_of).reshape((-1,) + (1,) * (len(extent) - 1 - position))
    return factor_of


def profile(amount, total, reach, slope):
    loads = [(1 << 20) // math.isqrt(standing ** slope) + 1 for standing in range(2, amount + 1)]
    surplus, given = total - reach - (amount - 1), [1] * (amount - 1)
    while surplus > 0:
        movable = [i for i in range(amount - 1) if given[i] < reach]
        whole, left = sum([loads[i] for i in movable]), surplus
        for i in movable:
            more = min(reach - given[i], max(1, left * loads[i] // whole), surplus)
            given[i] = given[i] + more
            surplus = surplus - more
    return np.array([reach] + given)


def uneven_parts(rng, amount, total, reach, skew):
    if amount == 2:
        one = jax.random.randint(rng, (), max(1, total - reach), min(reach, total - 1) + 1)
        return jnp.stack([one, total - one])
    sizes = jnp.asarray(profile(amount, total, reach, skew), jnp.int32)
    couples = (amount - 1) // 2
    source_of, taker = sizes[1:1 + 2 * couples:2], sizes[2:2 + 2 * couples:2]
    room = jnp.minimum(source_of - 1, reach - taker)
    passed = jax.random.randint(jax.random.fold_in(rng, 1), (couples,), 0, 1 << 20) % (room + 1)
    sizes = sizes.at[1:1 + 2 * couples:2].set(source_of - passed).at[2:2 + 2 * couples:2].set(taker + passed)
    return sizes[jax.random.permutation(jax.random.fold_in(rng, 2), amount)]


def normal_values(rng, shape, deviation, limit, pieces=(), kind=jnp.bfloat16):
    result = jax.random.normal(rng, shape, jnp.float32) * deviation
    if len(pieces) > 0:
        result = levels(rng, shape, pieces, -0.22, 0.18) * result
    return jnp.clip(result, min=-limit, max=limit).astype(kind)


def setup_inputs(seed: int = 0) -> dict:
    streams_of = jax.random.split(jax.random.key(seed), 14)
    frames = normal_values(streams_of[0], (GROUPS, GROUP_TOK, D), 1.0, 6.0, ((0, 16), (1, 2)))
    skip_in = normal_values(streams_of[1], (GROUPS, GROUP_TOK, D), 1.0, 6.0, ((0, 16), (1, 2)))
    cond_in = normal_values(streams_of[2], (GROUPS, GROUP_TOK, D), 1.0, 6.0, ((0, 16), (1, 2)))
    lengths = jax.vmap(lambda own: uneven_parts(own, UTT, GROUP_TOK, LONG, 2))(jax.random.split(streams_of[3], GROUPS)).reshape((GROUPS, UTT)).astype(jnp.int32)
    drop_mask = touch_ends((jax.random.randint(streams_of[4], (GROUPS, UTT), 0, 4) < 1).astype(jnp.int32), jax.random.fold_in(streams_of[4], 1), 0, 1)
    time_index = touch_ends(jax.random.randint(streams_of[5], (GROUPS, UTT), 0, STEPS), jax.random.fold_in(streams_of[5], 1), 0, STEPS - 1).astype(jnp.int32)
    w_skip = normal_values(streams_of[6], (2 * D, D), (2 * D) ** -0.5, 0.125, ((0, 2), (1, 16)))
    w_qkv = normal_values(streams_of[7], (D, 3 * D), D ** -0.5, 0.1875, ((0, 2), (1, 16)))
    w_out = normal_values(streams_of[8], (D, D), (D // 16) ** -0.5, 0.75, ((0, 2), (1, 16)))
    w_up = normal_values(streams_of[9], (D, FF), D ** -0.5, 0.1875, ((0, 2), (1, 16)))
    w_down = normal_values(streams_of[10], (FF, D), FF ** -0.5, 0.09375, ((0, 2), (1, 16)))
    w_mod = normal_values(streams_of[11], (D, 4 * D), D ** -0.5, 0.1875, ((0, 2), (1, 16)))
    d_out = normal_values(streams_of[12], (GROUPS, GROUP_TOK, D), 1.0, 6.0, ((0, 16), (1, 2)))
    return dict(frames=frames, skip_in=skip_in, cond_in=cond_in, lengths=lengths, drop_mask=drop_mask, time_index=time_index, w_skip=w_skip, w_qkv=w_qkv, w_out=w_out, w_up=w_up, w_down=w_down, w_mod=w_mod, d_out=d_out)


@jax.custom_vjp
def low(v):
    return lax.optimization_barrier(v.astype(jnp.bfloat16)).astype(jnp.float32)

@jax.custom_vjp
def low_back(v):
    return v

def low_keep(v):
    return (low(v), None)

def low_pass(kept, grad):
    return (grad,)

def back_keep(v):
    return (v, None)

def back_low(kept, grad):
    return (low(grad),)
low.defvjp(low_keep, low_pass)
low_back.defvjp(back_keep, back_low)
highest = lax.Precision.HIGHEST
epsilon = 1e-06

def round_both(values):
    return low(low_back(values))

def layer_norm_mod(hidden, mod_scale, mod_shift):
    row_mean = lax.optimization_barrier(jnp.mean(hidden, axis=-1, keepdims=True))
    centered = hidden - row_mean
    row_var = lax.optimization_barrier(jnp.mean(centered * centered, axis=-1, keepdims=True))
    return centered * lax.rsqrt(row_var + epsilon) * (1.0 + mod_scale) + mod_shift

def membership(utt_lengths, row_first, row_count):
    utt_ends = jnp.cumsum(utt_lengths).astype(jnp.int32)
    utt_starts = (utt_ends - utt_lengths).astype(jnp.int32)
    positions = (row_first + jnp.arange(row_count, dtype=jnp.int32)).astype(jnp.int32)
    inside = (positions[:, None] >= utt_starts[None, :]) & (positions[:, None] < utt_ends[None, :])
    member = inside.astype(jnp.float32)
    offsets = lax.optimization_barrier(jnp.sum(jnp.where(inside, utt_starts[None, :], 0), axis=1)).astype(jnp.int32)
    rel_pos = (positions - offsets).astype(jnp.float32)
    utt_numbers = jnp.arange(utt_lengths.shape[0], dtype=jnp.int32)
    seg_ids = lax.optimization_barrier(jnp.sum(jnp.where(inside, utt_numbers[None, :], 0), axis=1)).astype(jnp.int32)
    return (member, rel_pos, seg_ids)

def rope_tables(rel_pos, head_dim):
    half_dim = head_dim // 2
    frequency = jnp.exp(-math.log(10000.0) * jnp.arange(half_dim, dtype=jnp.float32) / half_dim)
    angles = rel_pos[:, None] * frequency[None, :]
    return (jnp.cos(angles), jnp.sin(angles))

def rotate(vector, cos_table, sin_table):
    half_dim = vector.shape[-1] // 2
    first_half = vector[..., :half_dim]
    second_half = vector[..., half_dim:]
    cos_rows = cos_table[:, None, :]
    sin_rows = sin_table[:, None, :]
    return jnp.concatenate([first_half * cos_rows - second_half * sin_rows, second_half * cos_rows + first_half * sin_rows], axis=-1)

def time_embed(step_index, model_width):
    flow_time = step_index.astype(jnp.float32) / STEPS
    half_dim = model_width // 2
    frequency = jnp.exp(-math.log(10000.0) * jnp.arange(half_dim, dtype=jnp.float32) / half_dim)
    angles = 1000.0 * flow_time[:, None] * frequency[None, :]
    return jnp.concatenate([jnp.sin(angles), jnp.cos(angles)], axis=-1)

def group_forward(params, group_items):
    skip_weight, qkv_weight, out_weight, up_weight, down_weight, mod_weight = params
    frames_wide, skip_wide, cond_wide, utt_lengths, kept_mask, step_index = group_items
    frame_count = frames_wide.shape[0]
    model_width = frames_wide.shape[1]
    member, rel_pos, seg_ids = membership(utt_lengths, 0, frame_count)
    keep_row = jnp.dot(member, kept_mask, precision=highest)
    mixed_in = frames_wide + keep_row[:, None] * cond_wide
    joined = low(jnp.concatenate([mixed_in, skip_wide], axis=1))
    hidden = low_back(jnp.dot(joined, skip_weight, precision=highest))
    smooth = low(jax.nn.silu(time_embed(step_index, model_width)))
    modulation = jnp.dot(smooth, mod_weight, precision=highest)
    row_mod = jnp.dot(member, modulation, precision=highest)
    shift_attn, scale_attn, shift_ff, scale_ff = jnp.split(row_mod, 4, axis=1)
    normed_attn = low(layer_norm_mod(hidden, scale_attn, shift_attn))
    qkv_rows = low_back(jnp.dot(normed_attn, qkv_weight, precision=highest))
    cos_table, sin_table = rope_tables(rel_pos, HD)
    head_shape = (frame_count, model_width // HD, HD)
    query_rows = round_both(rotate(qkv_rows[:, :model_width].reshape(head_shape), cos_table, sin_table))
    key_rows = round_both(rotate(qkv_rows[:, model_width:2 * model_width].reshape(head_shape), cos_table, sin_table))
    value_rows = round_both(qkv_rows[:, 2 * model_width:].reshape(head_shape))
    score_scale = 1.0 / math.sqrt(HD)
    block_rows = min(512, frame_count)

    def attend(block_index):
        row_start = block_index * block_rows
        query_block = lax.dynamic_slice_in_dim(query_rows, row_start, block_rows, 0)
        seg_query = lax.dynamic_slice_in_dim(seg_ids, row_start, block_rows, 0)
        raw_scores = low_back(score_scale * jnp.einsum('qhd,khd->hqk', query_block, key_rows, precision=highest))
        same_utt = seg_query[:, None] == seg_ids[None, :]
        masked = jnp.where(same_utt[None], raw_scores, -1e+30)
        row_top = lax.optimization_barrier(jnp.max(masked, axis=-1, keepdims=True))
        exp_scores = jnp.exp(masked - row_top)
        attn_probs = exp_scores / lax.optimization_barrier(jnp.sum(exp_scores, axis=-1, keepdims=True))
        return jnp.einsum('hqk,khd->qhd', low(attn_probs), value_rows, precision=highest)
    attn_blocks = lax.map(jax.checkpoint(attend), jnp.arange(frame_count // block_rows, dtype=jnp.int32))
    attn_rows = round_both(attn_blocks.reshape(frame_count, model_width))
    hidden_two = hidden + low_back(jnp.dot(attn_rows, out_weight, precision=highest))
    normed_ff = low(layer_norm_mod(hidden_two, scale_ff, shift_ff))
    up_proj = low_back(jnp.dot(normed_ff, up_weight, precision=highest))
    activated = low(jax.nn.gelu(up_proj, approximate=True))
    return hidden_two + low_back(jnp.dot(activated, down_weight, precision=highest))

def reference(frames, skip_in, cond_in, lengths, drop_mask, time_index, w_skip, w_qkv, w_out, w_up, w_down, w_mod, d_out):
    kept_mask = 1.0 - drop_mask.astype(jnp.float32)
    grad_scale = GROUPS * UTT / jnp.maximum(jnp.sum(kept_mask), 1.0)
    cond_wide = cond_in.astype(jnp.float32)
    params = (w_skip.astype(jnp.float32), w_qkv.astype(jnp.float32), w_out.astype(jnp.float32), w_up.astype(jnp.float32), w_down.astype(jnp.float32), w_mod.astype(jnp.float32))

    def forward(frames_wide, skip_wide, weight_set):
        step_fn = jax.checkpoint(partial(group_forward, weight_set))
        return lax.map(step_fn, (frames_wide, skip_wide, cond_wide, lengths, kept_mask, time_index))
    output, pullback = jax.vjp(forward, frames.astype(jnp.float32), skip_in.astype(jnp.float32), params)
    d_frames, d_skip, weight_grads = pullback(d_out.astype(jnp.float32) * grad_scale)
    return (output.astype(jnp.bfloat16), d_frames, d_skip, weight_grads[0], weight_grads[1], weight_grads[2], weight_grads[3], weight_grads[4], weight_grads[5])
```

```python
from functools import partial
import math

import jax
import jax.numpy as jnp
from jax import lax
from jax.experimental import pallas as pl
from jax.experimental.pallas import tpu as pltpu
from jax.sharding import PartitionSpec as P

HD = 64
LANES = 128
STEPS = 1000
LONG_PART = 0.75
NEG = -1e30
GELU_C = math.sqrt(2.0 / math.pi)
VMEM_MIB = 60

bf16 = jnp.bfloat16
f32 = jnp.float32
highest = lax.Precision.HIGHEST
epsilon = 1e-06


def dot(a, b, ca, cb):
    return lax.dot_general(a, b, (((ca,), (cb,)), ((), ())), preferred_element_type=f32)


def params(mib=VMEM_MIB):
    return pltpu.CompilerParams(vmem_limit_bytes=mib * 2**20)


def cost(flops, nbytes, trans=0):
    return pl.CostEstimate(flops=int(flops), bytes_accessed=int(nbytes), transcendentals=int(trans))


def shape(dims, dtype):
    return jax.ShapeDtypeStruct(dims, dtype)


class Net:
    def __init__(self, mesh):
        self.nd = mesh.shape["dp"]
        self.nf = mesh.shape["fsdp"]
        self.fb = self.nf.bit_length() - 1
        self.db = self.nd.bit_length() - 1
        common = [("fsdp", 1 << b) for b in range(self.fb - 1, 1, -1)]
        common += [("dp", 1 << b) for b in range(self.db - 1, 0, -1)]
        x, y, core = ("fsdp", 2), ("dp", 1), ("fsdp", 1)
        self.orders = (common + [x, y, core], common + [y, x, core])
        self.regroup = self.nd == 2
        self.attn_axis = "core" if self.regroup else "dp"
        self.na = 2 if self.regroup else self.nd

    def swap(self, x, bit):
        axis, mask = bit
        size = self.nf if axis == "fsdp" else self.nd
        return lax.ppermute(x, axis, [(i, i ^ mask) for i in range(size)])

    def attn_swap(self, x, r):
        return self.swap(x, ("fsdp", r) if self.regroup else ("dp", r))

    def attn_index(self):
        return lax.axis_index("fsdp") & 1 if self.regroup else lax.axis_index("dp")

    def group_of(self, f, y):
        return (f & ~1) | y if self.regroup else f

    def trade(self, x):
        if not self.regroup:
            return x
        perm = []
        for y in range(self.nd):
            for f in range(self.nf):
                c = f & 1
                perm.append((y * self.nf + f, c * self.nf + (f & ~1 | y)))
        return lax.ppermute(x, ("dp", "fsdp"), perm)

    def offsets(self, order):
        out = []
        for s in range(self.nd * self.nf):
            d = f = 0
            for j, (axis, mask) in enumerate(order):
                if s >> j & 1:
                    if axis == "dp":
                        d ^= mask
                    else:
                        f ^= mask
            out.append((d, f))
        return out

    def gather(self, x, order):
        for bit in order[:-2]:
            x = jnp.concatenate([x, self.swap(x, bit)], axis=0)
        y = self.swap(x, order[-2])
        return [x, y, self.swap(x, order[-1]), self.swap(y, order[-1])]

    def scatter_rest(self, x, order):
        for bit in reversed(order):
            half = x.shape[0] // 2
            got = self.swap(x[half:], bit)
            x = (x[:half].astype(f32) + got.astype(f32)).astype(bf16)
        return x

    def scatter_canonical(self, g, n, kd):
        f, d = lax.axis_index("fsdp"), lax.axis_index("dp")
        g = g.reshape((2,) * self.fb + (n, g.shape[1]))

        def split(x, bit, axes):
            axis, mask = bit
            if axis == "fsdp":
                at = axes.index(mask)
                b = jnp.where(f & mask != 0, 1, 0)
                keep = lax.dynamic_index_in_dim(x, b, at, keepdims=False)
                send = lax.dynamic_index_in_dim(x, 1 - b, at, keepdims=False)
                axes = axes[:at] + axes[at + 1 :]
            else:
                half = x.shape[-1] // 2
                b = jnp.where(d & mask != 0, 1, 0)
                keep = lax.dynamic_slice_in_dim(x, b * half, half, x.ndim - 1)
                send = lax.dynamic_slice_in_dim(x, (1 - b) * half, half, x.ndim - 1)
            got = self.swap(send, bit)
            return (keep.astype(f32) + got.astype(f32)).astype(bf16), axes

        axes = [1 << b for b in range(self.fb - 1, -1, -1)]
        g, axes = split(g, ("fsdp", 1), axes)
        rows = []
        dps = [("dp", 1 << b) for b in range(self.db - 1, -1, -1)]
        fs = [("fsdp", 1 << b) for b in range(1, self.fb)]
        for part, order in enumerate((dps + fs, fs[:1] + dps + fs[1:])):
            x = lax.slice_in_dim(g, part * n // 2, (part + 1) * n // 2, axis=g.ndim - 2)
            left = axes
            for bit in order:
                x, left = split(x, bit, left)
            rows.append(x)
        return jnp.concatenate(rows, axis=0)


def place_kernel(idx, *refs, plans, n):
    count = len(plans)
    srcs, out, sems = refs[:count], refs[count], refs[count + 1]
    copies = []
    for ref, plan in zip(srcs, plans):
        for slot, (d, f, first) in enumerate(plan):
            rows = ref.shape[0] // len(plan)
            kd = ref.shape[1]
            row = pl.multiple_of((idx[1] ^ f) * n + first, 16)
            col = pl.multiple_of((idx[0] ^ d) * kd, LANES)
            copies.append(
                pltpu.make_async_copy(
                    ref.at[pl.ds(slot * rows, rows), :],
                    out.at[pl.ds(row, rows), pl.ds(col, kd)],
                    sems.at[len(copies)],
                )
            )
    for c in copies:
        c.start()
    for c in copies:
        c.wait()


def gather_weight(net, block, idx):
    turned = block.T
    n, kd = turned.shape
    half = n // 2
    pieces, plans = [], []
    for part, order in enumerate(net.orders):
        got = net.gather(turned[part * half : (part + 1) * half], order)
        offs = net.offsets(order)
        quarter = len(offs) // 4
        for q, piece in enumerate(got):
            pieces.append(piece)
            plans.append([(d, f, part * half) for d, f in offs[q * quarter : (q + 1) * quarter]])
    big = (n * net.nf, kd * net.nd)
    return pl.pallas_call(
        partial(place_kernel, plans=plans, n=n),
        grid_spec=pltpu.PrefetchScalarGridSpec(
            num_scalar_prefetch=1,
            grid=(1,),
            in_specs=[pl.BlockSpec(memory_space=pl.ANY)] * len(pieces),
            out_specs=pl.BlockSpec(memory_space=pl.ANY),
            scratch_shapes=[pltpu.SemaphoreType.DMA((sum(len(p) for p in plans),))],
        ),
        out_shape=shape(big, bf16),
        compiler_params=params(16),
        cost_estimate=cost(0, 4 * big[0] * big[1]),
        name="place",
    )(idx, *pieces)


def norm_stats(x):
    mean = jnp.mean(x, axis=-1, keepdims=True)
    centered = x - mean
    var = jnp.mean(centered * centered, axis=-1, keepdims=True)
    rstd = lax.rsqrt(var + epsilon)
    return centered * rstd, rstd


def seg_sums(pick, x):
    top = x.astype(bf16)
    low = (x - top.astype(f32)).astype(bf16)
    return (dot(pick, top, 0, 0) + dot(pick, low, 0, 0))[:8]


def skip_fwd_kernel(frames, skip, cond, keep, w, hidden, mixed):
    d = frames.shape[1]
    m = (frames[...].astype(f32) + keep[:, :1] * cond[...].astype(f32)).astype(bf16)
    mixed[...] = m
    hidden[...] = (dot(m, w[:, :d], 1, 1) + dot(skip[...], w[:, d:], 1, 1)).astype(bf16)


def skip_fwd(frames, skip, cond, keep, w):
    r, d = frames.shape
    rb = min(256, r)
    row = pl.BlockSpec((rb, d), lambda i: (i, 0))
    return pl.pallas_call(
        skip_fwd_kernel,
        grid=(r // rb,),
        in_specs=[row, row, row, pl.BlockSpec((rb, LANES), lambda i: (i, 0)), pl.BlockSpec(w.shape, lambda i: (0, 0))],
        out_specs=[row, row],
        out_shape=[shape((r, d), bf16)] * 2,
        compiler_params=params(),
        cost_estimate=cost(4 * r * d * d, 10 * r * d + 4 * d * d),
        name="skip_fwd",
    )(frames, skip, cond, keep, w)


def turn(x, cos, sin, sign):
    width = x.shape[1]
    reps = width // LANES
    if reps > 1:
        cos = jnp.concatenate([cos] * reps, axis=1)
        sin = jnp.concatenate([sin] * reps, axis=1)
    lane = lax.broadcasted_iota(jnp.int32, (1, width), 1)
    other = jnp.where(lane % HD < HD // 2, pltpu.roll(x, width - HD // 2, 1), pltpu.roll(x, HD // 2, 1))
    return x * cos + other * sin if sign > 0 else x * cos - other * sin


def qkv_fwd_kernel(idx, hidden, pick, mod, w, cos, sin, normed, *pieces):
    d = hidden.shape[1]
    na = len(pieces)
    hw = d // na
    xh, _ = norm_stats(hidden[...].astype(f32))
    pk = pick[...]
    y = (xh * (1.0 + dot(pk, mod[:, d:], 1, 0)) + dot(pk, mod[:, :d], 1, 0)).astype(bf16)
    normed[...] = y
    for part in range(3):
        for r in range(na):
            at = pl.multiple_of(part * d + (idx[0] ^ r) * hw, hw)
            z = dot(y, w[pl.ds(at, hw), :], 1, 1)
            if part < 2:
                z = turn(z, cos[...], sin[...], 1)
            if part == 0:
                z = z * (1.0 / math.sqrt(HD))
            pieces[r][part] = z.astype(bf16)


def qkv_fwd(net, idx, hidden, pick, mod, w, cos, sin):
    r, d = hidden.shape
    rb = min(256, r)
    hw = d // net.na
    row = pl.BlockSpec((rb, d), lambda i, s: (i, 0))
    narrow = pl.BlockSpec((rb, LANES), lambda i, s: (i, 0))
    out = pl.BlockSpec((3, rb, hw), lambda i, s: (0, i, 0))
    res = pl.pallas_call(
        qkv_fwd_kernel,
        grid_spec=pltpu.PrefetchScalarGridSpec(
            num_scalar_prefetch=1,
            grid=(r // rb,),
            in_specs=[
                row,
                narrow,
                pl.BlockSpec(mod.shape, lambda i, s: (0, 0)),
                pl.BlockSpec(w.shape, lambda i, s: (0, 0)),
                narrow,
                narrow,
            ],
            out_specs=[row] + [out] * net.na,
        ),
        out_shape=[shape((r, d), bf16)] + [shape((3, r, hw), bf16)] * net.na,
        compiler_params=params(),
        cost_estimate=cost(6 * r * d * d, 12 * r * d + 6 * d * d),
        name="qkv_fwd",
    )(idx, hidden, pick, mod, w, cos, sin)
    return res[0], res[1:]


def out_fwd_kernel(idx, *refs, na):
    pieces = refs[:na]
    hidden, pick, mod, w, attn, hidden2, normed = refs[na:]
    d = hidden.shape[1]
    hw = d // na
    for r in range(na):
        attn[:, pl.ds(pl.multiple_of((idx[0] ^ r) * hw, hw), hw)] = pieces[r][...]
    h2 = hidden[...].astype(f32) + dot(attn[...], w[...], 1, 1)
    hidden2[...] = h2
    xh, _ = norm_stats(h2)
    pk = pick[...]
    normed[...] = (xh * (1.0 + dot(pk, mod[:, d:], 1, 0)) + dot(pk, mod[:, :d], 1, 0)).astype(bf16)


def out_fwd(net, idx, pieces, hidden, pick, mod, w):
    r, d = hidden.shape
    rb = min(256, r)
    hw = d // net.na
    row = pl.BlockSpec((rb, d), lambda i, s: (i, 0))
    narrow = pl.BlockSpec((rb, LANES), lambda i, s: (i, 0))
    return pl.pallas_call(
        partial(out_fwd_kernel, na=net.na),
        grid_spec=pltpu.PrefetchScalarGridSpec(
            num_scalar_prefetch=1,
            grid=(r // rb,),
            in_specs=[pl.BlockSpec((rb, hw), lambda i, s: (i, 0))] * net.na
            + [
                row,
                narrow,
                pl.BlockSpec(mod.shape, lambda i, s: (0, 0)),
                pl.BlockSpec(w.shape, lambda i, s: (0, 0)),
            ],
            out_specs=[row, row, row],
        ),
        out_shape=[shape((r, d), bf16), shape((r, d), f32), shape((r, d), bf16)],
        compiler_params=params(),
        cost_estimate=cost(2 * r * d * d, 12 * r * d + 2 * d * d),
        name="out_fwd",
    )(idx, *pieces, hidden, pick, mod, w)


def norm_back(x, grad, pick, scale):
    xh, rstd = norm_stats(x)
    g = grad * (1.0 + dot(pick, scale, 1, 0))
    dx = rstd * (
        g
        - jnp.mean(g, axis=-1, keepdims=True)
        - xh * jnp.mean(g * xh, axis=-1, keepdims=True)
    )
    return dx, seg_sums(pick, grad * xh), seg_sums(pick, grad)


def out_bwd_kernel(idx, gs, grad, hidden2, d_out, pick, scale, w, d_h2, d_att, sums, *outs):
    refs, hold = outs[:-1], outs[-1]
    i = pl.program_id(0)
    na = len(refs)
    d = grad.shape[1]
    hw = d // na
    dx, d_scale, d_shift = norm_back(hidden2[...], grad[...], pick[...], scale[...])
    dh = d_out[...].astype(f32) * gs[0] + dx
    d_h2[...] = dh
    low = dh.astype(bf16)
    d_att[...] = low
    hold[...] = dot(low, w[...], 1, 0).astype(bf16)
    for r in range(na):
        refs[r][...] = hold[:, pl.ds(pl.multiple_of((idx[0] ^ r) * hw, hw), hw)]
    both = jnp.concatenate([d_shift, d_scale], axis=1)

    @pl.when(i == 0)
    def _():
        sums[...] = both

    @pl.when(i > 0)
    def _():
        sums[...] += both


def out_bwd(net, idx, gs, grad, hidden2, d_out, pick, scale, w):
    r, d = grad.shape
    rb = min(256, r)
    hw = d // net.na
    row = pl.BlockSpec((rb, d), lambda i, s, t: (i, 0))
    narrow = pl.BlockSpec((rb, LANES), lambda i, s, t: (i, 0))
    whole = lambda a: pl.BlockSpec(a.shape, lambda i, s, t: (0, 0))
    res = pl.pallas_call(
        out_bwd_kernel,
        grid_spec=pltpu.PrefetchScalarGridSpec(
            num_scalar_prefetch=2,
            grid=(r // rb,),
            in_specs=[row, row, row, narrow, whole(scale), whole(w)],
            out_specs=[row, row, pl.BlockSpec((8, 2 * d), lambda i, s, t: (0, 0))]
            + [pl.BlockSpec((rb, hw), lambda i, s, t: (i, 0))] * net.na,
            scratch_shapes=[pltpu.VMEM((rb, d), bf16)],
        ),
        out_shape=[shape((r, d), f32), shape((r, d), bf16), shape((8, 2 * d), f32)]
        + [shape((r, hw), bf16)] * net.na,
        compiler_params=params(),
        cost_estimate=cost(2 * r * d * d, 20 * r * d + 2 * d * d),
        name="out_bwd",
    )(idx, gs, grad, hidden2, d_out, pick, scale, w)
    return res[0], res[1], res[2], res[3:]


def qkv_bwd_kernel(idx, *refs, na):
    pieces = refs[:na]
    cos, sin, hidden, d_h2, pick, scale, w, d_qkv, d_h, sums = refs[na:]
    i = pl.program_id(0)
    d = hidden.shape[1]
    hw = d // na
    for part in range(3):
        for r in range(na):
            z = pieces[r][part]
            if part < 2:
                z = turn(z.astype(f32), cos[...], sin[...], -1).astype(bf16)
            d_qkv[:, pl.ds(pl.multiple_of(part * d + (idx[0] ^ r) * hw, hw), hw)] = z
    grad = dot(d_qkv[...], w[...], 1, 0)
    dx, d_scale, d_shift = norm_back(hidden[...].astype(f32), grad, pick[...], scale[...])
    d_h[...] = (d_h2[...] + dx).astype(bf16)
    both = jnp.concatenate([d_shift, d_scale], axis=1)

    @pl.when(i == 0)
    def _():
        sums[...] = both

    @pl.when(i > 0)
    def _():
        sums[...] += both


def qkv_bwd(net, idx, pieces, cos, sin, hidden, d_h2, pick, scale, w):
    r, d = hidden.shape
    rb = min(256, r)
    hw = d // net.na
    row = pl.BlockSpec((rb, d), lambda i, s: (i, 0))
    narrow = pl.BlockSpec((rb, LANES), lambda i, s: (i, 0))
    whole = lambda a: pl.BlockSpec(a.shape, lambda i, s: (0, 0))
    return pl.pallas_call(
        partial(qkv_bwd_kernel, na=net.na),
        grid_spec=pltpu.PrefetchScalarGridSpec(
            num_scalar_prefetch=1,
            grid=(r // rb,),
            in_specs=[pl.BlockSpec((3, rb, hw), lambda i, s: (0, i, 0))] * net.na
            + [narrow, narrow, row, row, narrow, whole(scale), whole(w)],
            out_specs=[
                pl.BlockSpec((rb, 3 * d), lambda i, s: (i, 0)),
                row,
                pl.BlockSpec((8, 2 * d), lambda i, s: (0, 0)),
            ],
        ),
        out_shape=[shape((r, 3 * d), bf16), shape((r, d), bf16), shape((8, 2 * d), f32)],
        compiler_params=params(),
        cost_estimate=cost(6 * r * d * d, 22 * r * d + 6 * d * d),
        name="qkv_bwd",
    )(idx, *pieces, cos, sin, hidden, d_h2, pick, scale, w)


def skip_bwd_kernel(d_h, w, d_frames, d_skip):
    d = d_h.shape[1]
    g = d_h[...]
    d_frames[...] = dot(g, w[:, :d], 1, 0)
    d_skip[...] = dot(g, w[:, d:], 1, 0)


def skip_bwd(d_h, w):
    r, d = d_h.shape
    rb = min(256, r)
    row = pl.BlockSpec((rb, d), lambda i: (i, 0))
    return pl.pallas_call(
        skip_bwd_kernel,
        grid=(r // rb,),
        in_specs=[row, pl.BlockSpec(w.shape, lambda i: (0, 0))],
        out_specs=[row, row],
        out_shape=[shape((r, d), f32)] * 2,
        compiler_params=params(),
        cost_estimate=cost(4 * r * d * d, 10 * r * d + 4 * d * d),
        name="skip_bwd",
    )(d_h, w)


def outer_kernel(g, *refs):
    xs, out = refs[:-1], refs[-1]
    at = 0
    for x in xs:
        width = x.shape[1]
        out[:, at : at + width] = dot(g[...], x[...], 0, 0).astype(bf16)
        at += width


def outer(g, *xs):
    r, n = g.shape
    nb = min(512, n)
    k = sum(x.shape[1] for x in xs)
    return pl.pallas_call(
        outer_kernel,
        grid=(n // nb,),
        in_specs=[pl.BlockSpec((r, nb), lambda i: (0, i))] + [pl.BlockSpec(x.shape, lambda i: (0, 0)) for x in xs],
        out_specs=pl.BlockSpec((nb, k), lambda i: (i, 0)),
        out_shape=shape((n, k), bf16),
        compiler_params=params(),
        cost_estimate=cost(2 * r * n * k, 2 * (r * n + r * k + n * k)),
        name="outer",
    )(g, *xs)


def gelu_both(u):
    u2 = u * u
    t = jnp.tanh(GELU_C * u * (1.0 + 0.044715 * u2))
    half = 0.5 * (1.0 + t)
    return u * half, half + 0.5 * u * (1.0 - t * t) * (GELU_C * (1.0 + 3 * 0.044715 * u2))


def ffn_kernel(*refs, second):
    n = 12 if second else 7
    ins, outs = refs[:n], refs[n:]
    x_ref, df_ref, o_in = ins[:3]
    up_a, up_b, dn_a, dn_b = ins[3:7]
    o_out, dx_out, gu1, gu0, gd1, gd0, o_acc, sems = outs
    s = pl.program_id(0)
    loads = [pltpu.make_async_copy(o_in, o_acc, sems.at[0])]
    if second:
        loads.append(pltpu.make_async_copy(ins[7], dx_out, sems.at[1]))

    @pl.when(s == 0)
    def _():
        for load in loads:
            load.start()
        if not second:
            dx_out[...] = jnp.zeros_like(dx_out)

    has_y = s >= 2
    has_x = (s == 1) | (s == 2)
    wu = jnp.where(has_y, up_b[...], up_a[...])
    wd = jnp.where(has_x, dn_b[...], dn_a[...])
    x, df = x_ref[...], df_ref[...]
    g, dg = gelu_both(dot(x, wu, 1, 1))
    act = g.astype(bf16)
    du = (dot(df, wd, 1, 1) * dg).astype(bf16)

    @pl.when(s == 0)
    def _():
        for load in loads:
            load.wait()

    o_acc[...] += dot(act, wd, 1, 0)
    dx_out[...] += dot(du, wu, 1, 0)
    gd = dot(act, df, 0, 0)
    gu = dot(du, x, 0, 0)

    def put(cond, grad, ref, add):
        @pl.when(cond)
        def _():
            ref[...] = (grad + add[...].astype(f32) if second else grad).astype(bf16)

    adds = ins[8:12] if second else (None,) * 4
    put(has_y, gu, gu1, adds[0])
    put(jnp.logical_not(has_y), gu, gu0, adds[1])
    put(has_x, gd, gd1, adds[2])
    put(jnp.logical_not(has_x), gd, gd0, adds[3])

    @pl.when(s == 3)
    def _():
        o_out[...] = o_acc[...].astype(o_out.dtype)


def ffn(x, df, o_in, ups, dns, dx_in=None, adds=None):
    second = dx_in is not None
    r, d = x.shape
    u = ups[0].shape[0] // 2
    one = pl.Buffered(1)
    full = pl.BlockSpec((r, d), lambda s: (0, 0), pipeline_mode=one)
    whole = pl.BlockSpec((r, d), lambda s: (0, 0))
    up_a = pl.BlockSpec((u, d), lambda s: (jnp.minimum(s, 1), 0))
    up_b = pl.BlockSpec((u, d), lambda s: (jnp.where(s <= 2, 1, 0), 0))
    dn_a = pl.BlockSpec((u, d), lambda s: (jnp.where(s >= 1, 1, 0), 0))
    dn_b = pl.BlockSpec((u, d), lambda s: (jnp.where(s >= 2, 1, 0), 0))
    far = pl.BlockSpec(memory_space=pl.ANY)
    in_specs = [full, full, far, up_a, up_b, dn_a, dn_b]
    args = [x, df, o_in, *ups, *dns]
    if second:
        in_specs += [far, up_b, up_a, dn_b, dn_a]
        args += [dx_in, *adds]
    half = shape(ups[0].shape, bf16)
    return pl.pallas_call(
        partial(ffn_kernel, second=second),
        grid=(4,),
        in_specs=in_specs,
        out_specs=[whole, whole, up_b, up_a, dn_b, dn_a],
        out_shape=[shape((r, d), bf16 if second else f32), shape((r, d), f32)] + [half] * 4,
        scratch_shapes=[pltpu.VMEM((r, d), f32), pltpu.SemaphoreType.DMA((2,))],
        compiler_params=params(),
        cost_estimate=cost(12 * r * d * 4 * u, 16 * r * d + 20 * u * d, 4 * u * r),
        name="ffn",
    )(*args)


def head_sel(h):
    lane = lax.broadcasted_iota(jnp.int32, (1, LANES), 1)
    return lane < HD if h == 0 else lane >= HD


def load_rolled(idx, hold, refs, part, rest):
    rows = refs[0].shape[-2]
    t = rows * len(refs)
    for r, ref in enumerate(refs):
        x = ref[part] if part is not None else ref[...]
        hold[pl.ds(pl.multiple_of((idx[0] ^ r) * rows, rows), rows), :] = x.astype(f32)
    hold[t : t + rest, :] = hold[0:rest, :]
    return hold[pl.ds(idx[1], t), :]


def store_unrolled(idx, hold, t, rest):
    row = lax.broadcasted_iota(jnp.int32, (rest, 1), 0)
    hold[0:rest, :] = jnp.where(row < idx[1], hold[t : t + rest, :], hold[0:rest, :])


def attn_fwd_kernel(idx, *refs, na, long):
    pieces = refs[:na]
    segr, segc = refs[na : na + 2]
    outs = refs[na + 2 : 2 * na + 2]
    lse_ref, hold, ql, kl, vt = refs[2 * na + 2 :]
    rows = outs[0].shape[0]
    t = rows * na
    rest = t - long
    ql[...] = load_rolled(idx, hold, pieces, 0, rest).astype(bf16)
    kl[...] = load_rolled(idx, hold, pieces, 1, rest).astype(bf16)
    vt[...] = jnp.transpose(load_rolled(idx, hold, pieces, 2, rest)).astype(bf16)

    def pair(r0, n, c0, cn, mask):
        q = ql[pl.ds(r0, n), :]
        k = kl[c0 : c0 + cn, :]
        got, lses = [], []
        for h in range(2):
            qh = jnp.where(head_sel(h), q, jnp.zeros_like(q))
            s = dot(k, qh, 1, 1)
            if mask is not None:
                s = jnp.where(mask, s, NEG)
            top = jnp.max(s, axis=0, keepdims=True)
            p = jnp.exp(s - top)
            total = jnp.sum(p, axis=0, keepdims=True)
            got.append(dot(vt[HD * h : HD * h + HD, c0 : c0 + cn], p.astype(bf16), 1, 0) / total)
            lses.append(top + jnp.log(total))
        lse_ref[0, :, pl.ds(r0, n)] = jnp.concatenate(lses, axis=0)
        hold[pl.ds(idx[1] + r0, n), :] = jnp.transpose(jnp.concatenate(got, axis=0))

    step = long // 2
    for i in range(2):
        pair(i * step, step, 0, long, None)
    pair(long, rest, long, rest, segc[:, :1] == segr[:1, :])
    store_unrolled(idx, hold, t, rest)
    for r in range(na):
        outs[r][...] = hold[pl.ds(pl.multiple_of((idx[0] ^ r) * rows, rows), rows), :].astype(bf16)


def attn_fwd(net, idx, pieces, segr, segc, long):
    na = net.na
    _, rows, hw = pieces[0].shape
    t = rows * na
    rest = t - long
    pairs = hw // LANES
    const = lambda a: pl.BlockSpec(a.shape, lambda j, s: (0, 0))
    work = pairs * 2 * (long * long + rest * rest)
    res = pl.pallas_call(
        partial(attn_fwd_kernel, na=na, long=long),
        grid_spec=pltpu.PrefetchScalarGridSpec(
            num_scalar_prefetch=1,
            grid=(pairs,),
            in_specs=[pl.BlockSpec((3, rows, LANES), lambda j, s: (0, 0, j))] * na + [const(segr), const(segc)],
            out_specs=[pl.BlockSpec((rows, LANES), lambda j, s: (0, j))] * na
            + [pl.BlockSpec((1, 2, t), lambda j, s: (j, 0, 0))],
            scratch_shapes=[
                pltpu.VMEM((t + rest, LANES), f32),
                pltpu.VMEM((t, LANES), bf16),
                pltpu.VMEM((t, LANES), bf16),
                pltpu.VMEM((LANES, t), bf16),
            ],
        ),
        out_shape=[shape((rows, hw), bf16)] * na + [shape((pairs, 2, t), f32)],
        compiler_params=params(),
        cost_estimate=cost(16 * HD * work, 8 * t * hw, work),
        name="attn_fwd",
    )(idx, *pieces, segr, segc)
    return res[:na], res[na]


def attn_bwd_kernel(idx, *refs, na, long):
    pieces, d_pieces = refs[:na], refs[na : 2 * na]
    lse_ref, segr, segc = refs[2 * na : 2 * na + 3]
    outs = refs[2 * na + 3 : 3 * na + 3]
    hold, ql, kl, vl, dl, kt, dqt, dka, dva = refs[3 * na + 3 :]
    rows = outs[0].shape[1]
    t = rows * na
    rest = t - long
    ql[...] = load_rolled(idx, hold, pieces, 0, rest).astype(bf16)
    kf = load_rolled(idx, hold, pieces, 1, rest)
    kl[...] = kf.astype(bf16)
    kt[...] = jnp.transpose(kf).astype(bf16)
    vl[...] = load_rolled(idx, hold, pieces, 2, rest).astype(bf16)
    dl[...] = load_rolled(idx, hold, d_pieces, None, rest).astype(bf16)
    dka[...] = jnp.zeros_like(dka)
    dva[...] = jnp.zeros_like(dva)

    def pair(r0, n, c0, cn, mask):
        q, do = ql[pl.ds(r0, n), :], dl[pl.ds(r0, n), :]
        k, v = kl[c0 : c0 + cn, :], vl[c0 : c0 + cn, :]
        dqs = []
        for h in range(2):
            qh = jnp.where(head_sel(h), q, jnp.zeros_like(q))
            dh = jnp.where(head_sel(h), do, jnp.zeros_like(do))
            s = dot(k, qh, 1, 1)
            if mask is not None:
                s = jnp.where(mask, s, NEG)
            p = jnp.exp(s - lse_ref[0, h : h + 1, pl.ds(r0, n)])
            dp = dot(v, dh, 1, 1)
            delta = jnp.sum(p * dp, axis=0, keepdims=True)
            ds = (p * (dp - delta)).astype(bf16)
            dqs.append(dot(kt[HD * h : HD * h + HD, c0 : c0 + cn], ds, 1, 0))
            dva[c0 : c0 + cn, :] += dot(p.astype(bf16), dh, 1, 0)
            dka[c0 : c0 + cn, :] += dot(ds, qh, 1, 0)
        dqt[pl.ds(r0, n), :] = jnp.transpose(jnp.concatenate(dqs, axis=0))

    step = long // 2

    def body(i, carry):
        pair(pl.multiple_of(i * step, step), step, 0, long, None)
        return carry

    lax.fori_loop(0, 2, body, 0)
    pair(long, rest, long, rest, segc[:, :1] == segr[:1, :])
    for part, src in enumerate((dqt, dka, dva)):
        x = src[...]
        if part == 0:
            x = x * (1.0 / math.sqrt(HD))
        hold[pl.ds(idx[1], t), :] = x
        store_unrolled(idx, hold, t, rest)
        for r in range(na):
            at = pl.multiple_of((idx[0] ^ r) * rows, rows)
            outs[r][part] = hold[pl.ds(at, rows), :].astype(bf16)


def attn_bwd(net, idx, pieces, d_pieces, lse, segr, segc, long):
    na = net.na
    _, rows, hw = pieces[0].shape
    t = rows * na
    rest = t - long
    pairs = hw // LANES
    const = lambda a: pl.BlockSpec(a.shape, lambda j, s: (0, 0))
    three = pl.BlockSpec((3, rows, LANES), lambda j, s: (0, 0, j))
    work = pairs * 2 * (long * long + rest * rest)
    return pl.pallas_call(
        partial(attn_bwd_kernel, na=na, long=long),
        grid_spec=pltpu.PrefetchScalarGridSpec(
            num_scalar_prefetch=1,
            grid=(pairs,),
            in_specs=[three] * na
            + [pl.BlockSpec((rows, LANES), lambda j, s: (0, j))] * na
            + [pl.BlockSpec((1, 2, t), lambda j, s: (j, 0, 0)), const(segr), const(segc)],
            out_specs=[three] * na,
            scratch_shapes=[pltpu.VMEM((t + rest, LANES), f32)]
            + [pltpu.VMEM((t, LANES), bf16)] * 4
            + [pltpu.VMEM((LANES, t), bf16)]
            + [pltpu.VMEM((t, LANES), f32)] * 3,
        ),
        out_shape=[shape((3, rows, hw), bf16)] * na,
        compiler_params=params(),
        cost_estimate=cost(40 * HD * work, 16 * t * hw, work),
        name="attn_bwd",
    )(idx, *pieces, *d_pieces, lse, segr, segc)


def members(utt_lengths, positions):
    ends = jnp.cumsum(utt_lengths)
    starts = ends - utt_lengths
    inside = (positions[:, None] >= starts[None, :]) & (positions[:, None] < ends[None, :])
    return inside, positions - jnp.sum(jnp.where(inside, starts[None, :], 0), axis=1)


def rope_tables(rel_pos):
    half = HD // 2
    frequency = jnp.exp(-math.log(10000.0) * jnp.arange(half, dtype=f32) / half)
    angles = rel_pos.astype(f32)[:, None] * frequency[None, :]
    c, s = jnp.cos(angles), jnp.sin(angles)
    return jnp.concatenate([c] * 4, axis=1), jnp.concatenate([-s, s, -s, s], axis=1)


def time_embed(step_index, model_width):
    flow_time = step_index.astype(f32) / STEPS
    half_dim = model_width // 2
    frequency = jnp.exp(-math.log(10000.0) * jnp.arange(half_dim, dtype=f32) / half_dim)
    angles = 1000.0 * flow_time[:, None] * frequency[None, :]
    return jnp.concatenate([jnp.sin(angles), jnp.cos(angles)], axis=-1)


def three_terms(x):
    a = lax.reduce_precision(x, 8, 7)
    b = lax.reduce_precision(x - a, 8, 7)
    c = x - a - b
    stacked = jnp.concatenate([a, b, c], axis=0).astype(bf16)
    return jnp.pad(stacked, ((0, LANES - stacked.shape[0]), (0, 0)))


def local(net, frames, skip_in, cond_in, lengths, drop_mask, time_index, w_skip, w_qkv, w_out, w_up, w_down, w_mod, d_out):
    frames, skip_in, cond_in, d_out = frames[0], skip_in[0], cond_in[0], d_out[0]
    rows, d = frames.shape
    nd, nf, na = net.nd, net.nf, net.na
    y, f = lax.axis_index("dp"), lax.axis_index("fsdp")
    utt = lengths.shape[1]
    group_len = rows * nd
    long = int(group_len * LONG_PART)
    rest = group_len - long
    me = jnp.stack([y, f]).astype(jnp.int32)

    skip_t = gather_weight(net, w_skip, me)
    small = lax.all_gather(jnp.concatenate([lengths, drop_mask, time_index], axis=1), "fsdp", axis=0, tiled=True)
    all_lengths, all_drop, all_time = jnp.split(small, 3, axis=1)
    qkv_t = gather_weight(net, w_qkv, me)
    out_t = gather_weight(net, w_out, me)

    units = w_down.shape[0] * nd // (nd * nf)
    down_mine = lax.all_to_all(w_down, "fsdp", split_axis=0, concat_axis=1, tiled=True)
    up_t = w_up.T
    up_parts = []
    for j in range(nd):
        perm = [(a * nf + b, nd * b + (a + j) % nd) for a in range(nd) for b in range(nf)]
        send = lax.dynamic_slice_in_dim(up_t, (y + j) % nd * units, units, 0)
        up_parts.append(lax.ppermute(send, ("dp", "fsdp"), perm))
    own = (y * nf + f) % nd
    up_stack = jnp.stack(up_parts)
    up_mine = jnp.concatenate([lax.dynamic_index_in_dim(up_stack, (own - a) % nd, 0, keepdims=False) for a in range(nd)], axis=1)
    ups = net.gather(up_mine, net.orders[0])
    dns = net.gather(down_mine, net.orders[1])

    smooth = jax.nn.silu(time_embed(all_time.reshape(-1), d)).astype(bf16)
    mine = lax.dynamic_slice_in_dim(smooth, y * (d // nd), d // nd, 1)
    part = jnp.dot(mine, w_mod, preferred_element_type=f32)
    for b in range(net.db):
        part = part + net.swap(part, ("dp", 1 << b))
    cols = w_mod.shape[1]
    part = part.reshape(nf, utt, cols)
    if net.regroup:
        by_pair = part.reshape(nf // 2, 2, utt, cols)
        picked = lax.dynamic_index_in_dim(by_pair, y, 1, keepdims=True)
        part = jnp.broadcast_to(picked, by_pair.shape).reshape(nf, utt, cols)
    mod = lax.all_to_all(part, "fsdp", split_axis=0, concat_axis=2, tiled=True).reshape(utt, nf * cols)
    mods = three_terms(mod)
    mod_a, mod_f = mods[:, : 2 * d], mods[:, 2 * d :]

    inside0, _ = members(lengths[0], y * rows + jnp.arange(rows, dtype=jnp.int32))
    kept0 = 1.0 - drop_mask[0].astype(f32)
    keep_row = jnp.sum(jnp.where(inside0, kept0[None, :], 0.0), axis=1)
    keep = jnp.broadcast_to(keep_row[:, None], (rows, LANES))
    grad_scale = all_lengths.size / jnp.maximum(jnp.sum(1.0 - all_drop.astype(f32)), 1.0)
    gs = grad_scale.reshape(1)

    group = net.group_of(f, y)
    my_lengths = lax.dynamic_index_in_dim(all_lengths, group, 0, keepdims=False)
    block = net.attn_index()
    inside, rel_pos = members(my_lengths, block * rows + jnp.arange(rows, dtype=jnp.int32))
    pick = jnp.pad(jnp.concatenate([inside] * 3, axis=1).astype(bf16), ((0, 0), (0, LANES - 3 * utt)))
    cos, sin = rope_tables(rel_pos)
    starts = jnp.cumsum(my_lengths) - my_lengths
    first = jnp.sum(jnp.where(my_lengths == long, starts, 0))
    rest_pos = (first + long + jnp.arange(rest, dtype=jnp.int32)) % group_len
    rest_in, _ = members(my_lengths, rest_pos)
    seg = jnp.sum(jnp.where(rest_in, jnp.arange(utt, dtype=jnp.int32)[None, :], 0), axis=1)
    segr = jnp.broadcast_to(seg[None, :], (8, rest))
    segc = jnp.broadcast_to(seg[:, None], (rest, LANES))
    idx = jnp.stack([block, first]).astype(jnp.int32)

    hidden0, mixed = skip_fwd(frames, skip_in, cond_in, keep, skip_t)
    hidden = net.trade(hidden0)
    d_out_t = net.trade(d_out)
    d_f = (d_out_t.astype(f32) * grad_scale).astype(bf16)
    normed_a, sent = qkv_fwd(net, idx, hidden, pick, mod_a, qkv_t, cos, sin)
    pieces = [sent[0]] + [net.attn_swap(sent[r], r) for r in range(1, na)]
    attn_p, lse = attn_fwd(net, idx, pieces, segr, segc, long)
    attn_p = [attn_p[0]] + [net.attn_swap(attn_p[r], r) for r in range(1, na)]
    attn, hidden2, normed_f = out_fwd(net, idx, attn_p, hidden, pick, mod_f, out_t)

    acc, dx, *theirs = ffn(normed_f, d_f, hidden2, ups[2:], dns[2:])
    theirs = [net.swap(g, ("fsdp", 1)) for g in theirs]
    out_b, dx, gu1, gu0, gd1, gd0 = ffn(normed_f, d_f, acc, ups[:2], dns[:2], dx, theirs)
    output = net.trade(out_b)

    def finish(order, far, near):
        got = net.swap(far, order[-2])
        near = (near.astype(f32) + got.astype(f32)).astype(bf16)
        return net.scatter_rest(near, order[:-2])

    g_up = finish(net.orders[0], gu1, gu0)
    g_down = finish(net.orders[1], gd1, gd0)
    grad_down = lax.all_to_all(g_down, "fsdp", split_axis=1, concat_axis=0, tiled=True).astype(f32)
    back = []
    for j in range(nd):
        perm = [(nd * b + (a + j) % nd, a * nf + b) for a in range(nd) for b in range(nf)]
        send = lax.dynamic_slice_in_dim(g_up, (own - j) % nd * (d // nd), d // nd, 1)
        back.append(lax.ppermute(send, ("dp", "fsdp"), perm))
    back = jnp.stack(back)
    grad_up = jnp.concatenate([lax.dynamic_index_in_dim(back, (h - y) % nd, 0, keepdims=False) for h in range(nd)], axis=0)
    grad_up = grad_up.T.astype(f32)

    d_h2, d_att, sums_f, d_attn_p = out_bwd(net, idx, gs, dx, hidden2, d_out_t, pick, mod_f[:, d:], out_t)
    d_attn_p = [d_attn_p[0]] + [net.attn_swap(d_attn_p[r], r) for r in range(1, na)]
    grad_out = net.scatter_canonical(outer(d_att, attn), w_out.shape[1], w_out.shape[0]).T.astype(f32)
    d_sent = attn_bwd(net, idx, pieces, d_attn_p, lse, segr, segc, long)
    d_pieces = [d_sent[0]] + [net.attn_swap(d_sent[r], r) for r in range(1, na)]
    d_qkv, d_h, sums_a = qkv_bwd(net, idx, d_pieces, cos, sin, hidden, d_h2, pick, mod_a[:, d:], qkv_t)
    d_h0 = net.trade(d_h)
    grad_qkv = net.scatter_canonical(outer(d_qkv, normed_a), w_qkv.shape[1], w_qkv.shape[0]).T.astype(f32)
    grad_skip = net.scatter_canonical(outer(d_h0, mixed, skip_in), w_skip.shape[1], w_skip.shape[0]).T.astype(f32)
    d_frames, d_skip = skip_bwd(d_h0, skip_t)

    d_mod = jnp.concatenate([sums_a, sums_f], axis=1).reshape(utt, nf, cols).transpose(1, 0, 2)
    d_mod = lax.all_to_all(d_mod, "fsdp", split_axis=0, concat_axis=0, tiled=True)
    if net.regroup:
        pair_sum = d_mod.reshape(nf // 2, 2, utt, cols).sum(axis=1)
        here = (jnp.arange(2) == y).astype(f32)
        d_mod = pair_sum[:, None] * here[None, :, None, None]
    d_mod = d_mod.reshape(nf * utt, cols)
    for b in range(net.db):
        d_mod = d_mod + net.swap(d_mod, ("dp", 1 << b))
    grad_mod = jnp.dot(mine.astype(f32).T, d_mod, precision=highest)

    return (output[None], d_frames[None], d_skip[None], grad_skip, grad_qkv, grad_out, grad_up, grad_down, grad_mod)


def solution(mesh):
    rows = P("fsdp", "dp", None)
    ints = P("fsdp", None)
    weight = P("dp", "fsdp")
    return jax.shard_map(
        partial(local, Net(mesh)),
        mesh=mesh,
        in_specs=(rows, rows, rows, ints, ints, ints, *([weight] * 6), rows),
        out_specs=(rows, rows, rows, *([weight] * 6)),
        check_vma=False,
    )
```

```python
from functools import partial
import math

import jax
import jax.numpy as jnp
from jax import lax
from jax.experimental import pallas as pl
from jax.experimental.pallas import tpu as pltpu
from jax.sharding import PartitionSpec as P

HD = 64
LANES = 128
STEPS = 1000
LONG_PART = 0.75
NEG = -1e30
GELU_C = math.sqrt(2.0 / math.pi)
VMEM_MIB = 60

bf16 = jnp.bfloat16
f32 = jnp.float32
highest = lax.Precision.HIGHEST
epsilon = 1e-06


def dot(a, b, ca, cb):
    return lax.dot_general(a, b, (((ca,), (cb,)), ((), ())), preferred_element_type=f32)


def params(mib=VMEM_MIB):
    return pltpu.CompilerParams(vmem_limit_bytes=mib * 2**20)


def cost(flops, nbytes, trans=0):
    return pl.CostEstimate(flops=int(flops), bytes_accessed=int(nbytes), transcendentals=int(trans))


def shape(dims, dtype):
    return jax.ShapeDtypeStruct(dims, dtype)


class Net:
    def __init__(self, mesh):
        self.nd = mesh.shape["dp"]
        self.nf = mesh.shape["fsdp"]
        self.fb = self.nf.bit_length() - 1
        self.db = self.nd.bit_length() - 1
        common = [("fsdp", 1 << b) for b in range(self.fb - 1, 1, -1)]
        common += [("dp", 1 << b) for b in range(self.db - 1, 0, -1)]
        x, y, core = ("fsdp", 2), ("dp", 1), ("fsdp", 1)
        self.orders = (common + [x, y, core], common + [y, x, core])
        self.regroup = self.nd == 2
        self.attn_axis = "core" if self.regroup else "dp"
        self.na = 2 if self.regroup else self.nd

    def swap(self, x, bit):
        axis, mask = bit
        size = self.nf if axis == "fsdp" else self.nd
        return lax.ppermute(x, axis, [(i, i ^ mask) for i in range(size)])

    def attn_swap(self, x, r):
        return self.swap(x, ("fsdp", r) if self.regroup else ("dp", r))

    def attn_index(self):
        return lax.axis_index("fsdp") & 1 if self.regroup else lax.axis_index("dp")

    def group_of(self, f, y):
        return (f & ~1) | y if self.regroup else f

    def trade(self, x):
        if not self.regroup:
            return x
        perm = []
        for y in range(self.nd):
            for f in range(self.nf):
                c = f & 1
                if c != y:
                    perm.append((y * self.nf + f, c * self.nf + (f & ~1 | y)))
        return lax.ppermute(x, ("dp", "fsdp"), perm)

    def traded(self, x, got):
        if not self.regroup:
            return x
        return jnp.where(lax.axis_index("fsdp") & 1 != lax.axis_index("dp"), got, x)

    def offsets(self, order):
        out = []
        for s in range(self.nd * self.nf):
            d = f = 0
            for j, (axis, mask) in enumerate(order):
                if s >> j & 1:
                    if axis == "dp":
                        d ^= mask
                    else:
                        f ^= mask
            out.append((d, f))
        return out

    def halves(self, x, bit, axes):
        axis, mask = bit
        b = jnp.where(lax.axis_index(axis) & mask != 0, 1, 0)
        if axis == "fsdp":
            at = axes.index(mask)
            keep = lax.dynamic_index_in_dim(x, b, at, keepdims=False)
            send = lax.dynamic_index_in_dim(x, 1 - b, at, keepdims=False)
            return keep, send, axes[:at] + axes[at + 1 :]
        half = x.shape[-1] // 2
        keep = lax.dynamic_slice_in_dim(x, b * half, half, x.ndim - 1)
        send = lax.dynamic_slice_in_dim(x, (1 - b) * half, half, x.ndim - 1)
        return keep, send, axes


def plus(*xs):
    total = xs[0].astype(f32)
    for x in xs[1:]:
        total = total + x.astype(f32)
    return total.astype(bf16)


def tie(*groups):
    flat = lax.optimization_barrier(tuple(x for g in groups for x in g))
    out, at = [], 0
    for g in groups:
        out.append(list(flat[at : at + len(g)]))
        at += len(g)
    return out


class Gather:
    def __init__(self, net, block, split):
        self.net = net
        rows = block.shape[0]
        cuts = [(0, split, net.orders[0]), (split, rows, net.orders[1])]
        cuts = [c for c in cuts if c[0] < c[1]]
        self.bounds = [c[:2] for c in cuts]
        self.orders = [c[2] for c in cuts]
        self.x = [block[None]]
        self.done = 0
        self.common = len(net.orders[0]) - 3

    def send(self):
        if self.done == self.common:
            self.x = [self.x[0][:, a:b] for a, b in self.bounds]
        self.raw = [self.net.swap(x, o[self.done]) for x, o in zip(self.x, self.orders)]

    def join(self):
        if self.done == self.common + 1:
            self.far = self.raw
        else:
            self.x = [jnp.concatenate([x, r], axis=0) for x, r in zip(self.x, self.raw)]
        self.done += 1

    def finish_common(self):
        while self.done < self.common:
            self.send()
            self.join()

    def core(self, which):
        return [self.net.swap(x, self.orders[0][-1]) for x in which]


class Sum:
    def __init__(self, net, x):
        self.net = net
        n = x.shape[1]
        x = x.reshape((2,) * (net.fb - 1) + x.shape[1:])
        axes = [1 << b for b in range(net.fb - 1, 0, -1)]
        dps = [("dp", 1 << b) for b in range(net.db - 1, -1, -1)]
        fs = [("fsdp", 1 << b) for b in range(1, net.fb)]
        half = n // 2
        self.parts = [
            [lax.slice_in_dim(x, p * half, p * half + half, axis=x.ndim - 2), axes, order]
            for p, order in enumerate((dps + fs[:1], fs[:1] + dps))
        ]
        self.tail = fs[1:]

    @property
    def left(self):
        return max(len(p[2]) for p in self.parts) + len(self.tail)

    def send(self):
        if not self.parts[0][2] and len(self.parts) > 1:
            self.parts = [[jnp.concatenate([p[0] for p in self.parts], axis=-2), self.parts[0][1], self.tail]]
            self.tail = []
        self.keeps, self.raw = [], []
        for p in self.parts:
            keep, send, p[1] = self.net.halves(p[0], p[2][0], p[1])
            self.keeps.append(keep)
            self.raw.append(self.net.swap(send, p[2][0]))

    def join(self):
        for p, keep, got in zip(self.parts, self.keeps, self.raw):
            p[0] = plus(keep, got)
            p[2] = p[2][1:]

    def finish(self):
        while self.left:
            self.send()
            self.join()
        return self.parts[0][0]


def place_kernel(idx, *refs, plans, count):
    srcs, outs, sems = refs[:count], refs[count:-1], refs[-1]
    copies = []
    for ref, plan in zip(srcs, plans):
        kd = ref.shape[2]
        for slot, ((d, f), moves) in enumerate(plan):
            for first, rows, which, n, start in moves:
                row = pl.multiple_of((idx[1] ^ f) * n + start, 16)
                col = pl.multiple_of((idx[0] ^ d) * kd, LANES)
                copies.append(
                    pltpu.make_async_copy(
                        ref.at[slot, pl.ds(first, rows), :],
                        outs[which].at[pl.ds(row, rows), pl.ds(col, kd)],
                        sems.at[len(copies)],
                    )
                )
    for c in copies:
        c.start()
    for c in copies:
        c.wait()


def place(net, idx, gather, theirs, sizes):
    pieces = gather.x + gather.far + theirs
    lanes = pieces[0].shape[-1]
    plans = []
    total = 0
    count = len(gather.bounds)
    for i in range(len(pieces)):
        quarter, part = divmod(i, count)
        offs = net.offsets(gather.orders[part])
        some = offs[quarter * len(offs) // 4 : (quarter + 1) * len(offs) // 4]
        lo, hi = gather.bounds[part]
        moves, at = [], 0
        for which, n in enumerate(sizes):
            a, b = max(lo, at), min(hi, at + n)
            if a < b:
                moves.append((a - lo, b - a, which, n, a - at))
            at += n
        plans.append([(o, moves) for o in some])
        total += len(some) * len(moves)
    shapes = [shape((n * net.nf, lanes * net.nd), bf16) for n in sizes]
    return pl.pallas_call(
        partial(place_kernel, plans=plans, count=len(pieces)),
        grid_spec=pltpu.PrefetchScalarGridSpec(
            num_scalar_prefetch=1,
            grid=(1,),
            in_specs=[pl.BlockSpec(memory_space=pl.ANY)] * len(pieces),
            out_specs=[pl.BlockSpec(memory_space=pl.ANY)] * len(sizes),
            scratch_shapes=[pltpu.SemaphoreType.DMA((total,))],
        ),
        out_shape=shapes,
        compiler_params=params(16),
        cost_estimate=cost(0, 4 * sum(sizes) * net.nf * lanes * net.nd),
        name="place",
    )(idx, *pieces)


def norm_stats(x):
    mean = jnp.mean(x, axis=-1, keepdims=True)
    centered = x - mean
    var = jnp.mean(centered * centered, axis=-1, keepdims=True)
    rstd = lax.rsqrt(var + epsilon)
    return centered * rstd, rstd


def seg_sums(pick, x):
    top = x.astype(bf16)
    low = (x - top.astype(f32)).astype(bf16)
    return (dot(pick, top, 0, 0) + dot(pick, low, 0, 0))[:8]


def flip_kernel(*refs):
    n = len(refs) // 2
    for src, dst in zip(refs[:n], refs[n:]):
        dst[...] = jnp.transpose(src[...].astype(f32)).astype(bf16)


def flip(*xs):
    return pl.pallas_call(
        flip_kernel,
        out_shape=[shape(x.shape[::-1], bf16) for x in xs],
        compiler_params=params(32),
        cost_estimate=cost(0, 4 * sum(x.size for x in xs)),
        name="flip",
    )(*xs)


def skip_fwd_kernel(idx, lens, frames, skip, cond, w, hidden, mixed):
    rb, d = frames.shape
    pos = idx[0] * (rb * pl.num_programs(0)) + pl.program_id(0) * rb + lax.broadcasted_iota(jnp.int32, (rb, 1), 0)
    keep = jnp.zeros((rb, 1), f32)
    end = 0
    for u in range(lens.shape[1]):
        start, end = end, end + lens[0, u]
        keep = jnp.where((pos >= start) & (pos < end), (1 - lens[1, u]).astype(f32), keep)
    m = (frames[...].astype(f32) + keep * cond[...].astype(f32)).astype(bf16)
    mixed[...] = m
    hidden[...] = (dot(m, w[:, :d], 1, 1) + dot(skip[...], w[:, d:], 1, 1)).astype(bf16)


def skip_fwd(idx, lens, frames, skip, cond, w):
    r, d = frames.shape
    rb = min(256, r)
    row = pl.BlockSpec((rb, d), lambda i, s, t: (i, 0))
    return pl.pallas_call(
        skip_fwd_kernel,
        grid_spec=pltpu.PrefetchScalarGridSpec(
            num_scalar_prefetch=2,
            grid=(r // rb,),
            in_specs=[row, row, row, pl.BlockSpec(w.shape, lambda i, s, t: (0, 0))],
            out_specs=[row, row],
        ),
        out_shape=[shape((r, d), bf16)] * 2,
        compiler_params=params(),
        cost_estimate=cost(4 * r * d * d, 10 * r * d + 4 * d * d),
        name="skip_fwd",
    )(idx, lens, frames, skip, cond, w)


def turn(x, cos, sin, sign):
    width = x.shape[1]
    reps = width // LANES
    if reps > 1:
        cos = jnp.concatenate([cos] * reps, axis=1)
        sin = jnp.concatenate([sin] * reps, axis=1)
    lane = lax.broadcasted_iota(jnp.int32, (1, width), 1)
    other = jnp.where(lane % HD < HD // 2, pltpu.roll(x, width - HD // 2, 1), pltpu.roll(x, HD // 2, 1))
    return x * cos + other * sin if sign > 0 else x * cos - other * sin


def chosen(idx, own, got):
    half = pl.program_id(0) * 2 < pl.num_programs(0)
    new = jnp.where(half, got[0][...], got[1][...]) if len(got) > 1 else got[0][...]
    return jnp.where(idx[2] > 0, new, own[...])


def chosen_specs(rb, d, steps, halves=2):
    row = pl.BlockSpec((rb, d), lambda i, s: (i, 0))
    if halves == 1:
        return [row, row]
    return [
        row,
        pl.BlockSpec((rb, d), lambda i, s: (jnp.minimum(i, steps // 2 - 1), 0)),
        pl.BlockSpec((rb, d), lambda i, s: (jnp.maximum(i - steps // 2, 0), 0)),
    ]


def qkv_fwd_kernel(idx, hidden0, got, pick, mod, w, cos, sin, hidden, normed, *pieces):
    d = hidden.shape[1]
    na = len(pieces)
    hw = d // na
    h = chosen(idx, hidden0, (got,))
    hidden[...] = h
    xh, _ = norm_stats(h.astype(f32))
    pk = pick[...]
    y = (xh * (1.0 + dot(pk, mod[:, d:], 1, 0)) + dot(pk, mod[:, :d], 1, 0)).astype(bf16)
    normed[...] = y
    for part in range(3):
        for r in range(na):
            at = pl.multiple_of(part * d + (idx[0] ^ r) * hw, hw)
            z = dot(y, w[pl.ds(at, hw), :], 1, 1)
            if part < 2:
                z = turn(z, cos[...], sin[...], 1)
            if part == 0:
                z = z * (1.0 / math.sqrt(HD))
            pieces[r][part] = z.astype(bf16)


def qkv_fwd(net, idx, hidden0, got, pick, mod, w, cos, sin):
    r, d = hidden0.shape
    rb = min(256, r // 2)
    hw = d // net.na
    row = pl.BlockSpec((rb, d), lambda i, s: (i, 0))
    narrow = pl.BlockSpec((rb, LANES), lambda i, s: (i, 0))
    out = pl.BlockSpec((3, rb, hw), lambda i, s: (0, i, 0))
    res = pl.pallas_call(
        qkv_fwd_kernel,
        grid_spec=pltpu.PrefetchScalarGridSpec(
            num_scalar_prefetch=1,
            grid=(r // rb,),
            in_specs=chosen_specs(rb, d, r // rb, 1)
            + [
                narrow,
                pl.BlockSpec(mod.shape, lambda i, s: (0, 0)),
                pl.BlockSpec(w.shape, lambda i, s: (0, 0)),
                narrow,
                narrow,
            ],
            out_specs=[row, row] + [out] * net.na,
        ),
        out_shape=[shape((r, d), bf16)] * 2 + [shape((3, r, hw), bf16)] * net.na,
        compiler_params=params(),
        cost_estimate=cost(6 * r * d * d, 14 * r * d + 6 * d * d),
        name="qkv_fwd",
    )(idx, hidden0, got, pick, mod, w, cos, sin)
    return res[0], res[1], res[2:]


def out_fwd_kernel(idx, *refs, na):
    pieces = refs[:na]
    hidden, pick, mod, w, d_f0, got0, got1, attn, hidden2, normed, d_f = refs[na:]
    d = hidden.shape[1]
    d_f[...] = chosen(idx, d_f0, (got0, got1))
    hw = d // na
    for r in range(na):
        attn[:, pl.ds(pl.multiple_of((idx[0] ^ r) * hw, hw), hw)] = pieces[r][...]
    h2 = hidden[...].astype(f32) + dot(attn[...], w[...], 1, 1)
    hidden2[...] = h2
    xh, _ = norm_stats(h2)
    pk = pick[...]
    normed[...] = (xh * (1.0 + dot(pk, mod[:, d:], 1, 0)) + dot(pk, mod[:, :d], 1, 0)).astype(bf16)


def out_fwd(net, idx, pieces, hidden, pick, mod, w, d_f0, d_f_got):
    r, d = hidden.shape
    rb = min(256, r // 2)
    hw = d // net.na
    row = pl.BlockSpec((rb, d), lambda i, s: (i, 0))
    narrow = pl.BlockSpec((rb, LANES), lambda i, s: (i, 0))
    return pl.pallas_call(
        partial(out_fwd_kernel, na=net.na),
        grid_spec=pltpu.PrefetchScalarGridSpec(
            num_scalar_prefetch=1,
            grid=(r // rb,),
            in_specs=[pl.BlockSpec((rb, hw), lambda i, s: (i, 0))] * net.na
            + [
                row,
                narrow,
                pl.BlockSpec(mod.shape, lambda i, s: (0, 0)),
                pl.BlockSpec(w.shape, lambda i, s: (0, 0)),
            ]
            + chosen_specs(rb, d, r // rb),
            out_specs=[row, row, row, row],
        ),
        out_shape=[shape((r, d), bf16), shape((r, d), f32)] + [shape((r, d), bf16)] * 2,
        compiler_params=params(),
        cost_estimate=cost(2 * r * d * d, 12 * r * d + 2 * d * d),
        name="out_fwd",
    )(idx, *pieces, hidden, pick, mod, w, d_f0, *d_f_got)


def norm_back(x, grad, pick, scale):
    xh, rstd = norm_stats(x)
    g = grad * (1.0 + dot(pick, scale, 1, 0))
    dx = rstd * (
        g
        - jnp.mean(g, axis=-1, keepdims=True)
        - xh * jnp.mean(g * xh, axis=-1, keepdims=True)
    )
    return dx, seg_sums(pick, grad * xh), seg_sums(pick, grad)


def out_bwd_kernel(idx, grad, hidden2, d_f, pick, scale, w, d_h2, d_att, sums, *outs):
    refs, hold = outs[:-1], outs[-1]
    i = pl.program_id(0)
    na = len(refs)
    d = grad.shape[1]
    hw = d // na
    dx, d_scale, d_shift = norm_back(hidden2[...], grad[...], pick[...], scale[...])
    dh = d_f[...].astype(f32) + dx
    d_h2[...] = dh
    low = dh.astype(bf16)
    d_att[...] = low
    hold[...] = dot(low, w[...], 1, 0).astype(bf16)
    for r in range(na):
        refs[r][...] = hold[:, pl.ds(pl.multiple_of((idx[0] ^ r) * hw, hw), hw)]
    both = jnp.concatenate([d_shift, d_scale], axis=1)

    @pl.when(i == 0)
    def _():
        sums[...] = both

    @pl.when(i > 0)
    def _():
        sums[...] += both


def out_bwd(net, idx, grad, hidden2, d_f, pick, scale, w):
    r, d = grad.shape
    rb = min(256, r)
    hw = d // net.na
    row = pl.BlockSpec((rb, d), lambda i, s: (i, 0))
    narrow = pl.BlockSpec((rb, LANES), lambda i, s: (i, 0))
    whole = lambda a: pl.BlockSpec(a.shape, lambda i, s: (0, 0))
    res = pl.pallas_call(
        out_bwd_kernel,
        grid_spec=pltpu.PrefetchScalarGridSpec(
            num_scalar_prefetch=1,
            grid=(r // rb,),
            in_specs=[row, row, row, narrow, whole(scale), whole(w)],
            out_specs=[row, row, pl.BlockSpec((8, 2 * d), lambda i, s: (0, 0))]
            + [pl.BlockSpec((rb, hw), lambda i, s: (i, 0))] * net.na,
            scratch_shapes=[pltpu.VMEM((rb, d), bf16)],
        ),
        out_shape=[shape((r, d), f32), shape((r, d), bf16), shape((8, 2 * d), f32)]
        + [shape((r, hw), bf16)] * net.na,
        compiler_params=params(),
        cost_estimate=cost(2 * r * d * d, 20 * r * d + 2 * d * d),
        name="out_bwd",
    )(idx, grad, hidden2, d_f, pick, scale, w)
    return res[0], res[1], res[2], res[3:]


def turn_back_kernel(idx, *refs, na):
    pieces = refs[:-3]
    cos, sin, d_qkv = refs[-3:]
    d = d_qkv.shape[1] // 3
    hw = d // na
    for part in range(3):
        first = 0
        for k, piece in enumerate(pieces):
            r = k % na
            wide = piece.shape[2]
            z = piece[part]
            if part < 2:
                z = turn(z.astype(f32), cos[...], sin[...], -1).astype(bf16)
            d_qkv[:, pl.ds(pl.multiple_of(part * d + (idx[0] ^ r) * hw + first, LANES), wide)] = z
            first += wide if r == na - 1 else 0


def turn_back(net, idx, pieces, cos, sin, d):
    r = cos.shape[0]
    rb = min(256, r)
    narrow = pl.BlockSpec((rb, LANES), lambda i, s: (i, 0))
    return pl.pallas_call(
        partial(turn_back_kernel, na=net.na),
        grid_spec=pltpu.PrefetchScalarGridSpec(
            num_scalar_prefetch=1,
            grid=(r // rb,),
            in_specs=[pl.BlockSpec((3, rb, p.shape[2]), lambda i, s: (0, i, 0)) for p in pieces] + [narrow, narrow],
            out_specs=pl.BlockSpec((rb, 3 * d), lambda i, s: (i, 0)),
        ),
        out_shape=shape((r, 3 * d), bf16),
        compiler_params=params(),
        cost_estimate=cost(12 * r * d, 12 * r * d),
        name="turn_back",
    )(idx, *pieces, cos, sin)


def qkv_bwd_kernel(d_qkv, hidden, d_h2, pick, scale, w, d_h, sums):
    i = pl.program_id(0)
    grad = dot(d_qkv[...], w[...], 1, 0)
    dx, d_scale, d_shift = norm_back(hidden[...].astype(f32), grad, pick[...], scale[...])
    d_h[...] = (d_h2[...] + dx).astype(bf16)
    both = jnp.concatenate([d_shift, d_scale], axis=1)

    @pl.when(i == 0)
    def _():
        sums[...] = both

    @pl.when(i > 0)
    def _():
        sums[...] += both


def qkv_bwd(d_qkv, hidden, d_h2, pick, scale, w):
    r, d = hidden.shape
    rb = min(256, r)
    row = pl.BlockSpec((rb, d), lambda i: (i, 0))
    narrow = pl.BlockSpec((rb, LANES), lambda i: (i, 0))
    whole = lambda a: pl.BlockSpec(a.shape, lambda i: (0, 0))
    return pl.pallas_call(
        qkv_bwd_kernel,
        grid=(r // rb,),
        in_specs=[pl.BlockSpec((rb, 3 * d), lambda i: (i, 0)), row, row, narrow, whole(scale), whole(w)],
        out_specs=[row, pl.BlockSpec((8, 2 * d), lambda i: (0, 0))],
        out_shape=[shape((r, d), bf16), shape((8, 2 * d), f32)],
        compiler_params=params(),
        cost_estimate=cost(6 * r * d * d, 16 * r * d + 6 * d * d),
        name="qkv_bwd",
    )(d_qkv, hidden, d_h2, pick, scale, w)


def skip_bwd_kernel(idx, d_h, d_h_got, w, d_frames, d_skip):
    d = d_h.shape[1]
    g = jnp.where(idx[2] > 0, d_h_got[...], d_h[...])
    d_frames[...] = dot(g, w[:, :d], 1, 0)
    d_skip[...] = dot(g, w[:, d:], 1, 0)


def skip_bwd(idx, d_h, d_h_got, w):
    r, d = d_h.shape
    rb = min(256, r)
    row = pl.BlockSpec((rb, d), lambda i, s: (i, 0))
    return pl.pallas_call(
        skip_bwd_kernel,
        grid_spec=pltpu.PrefetchScalarGridSpec(
            num_scalar_prefetch=1,
            grid=(r // rb,),
            in_specs=[row, row, pl.BlockSpec(w.shape, lambda i, s: (0, 0))],
            out_specs=[row, row],
        ),
        out_shape=[shape((r, d), f32)] * 2,
        compiler_params=params(),
        cost_estimate=cost(4 * r * d * d, 12 * r * d + 4 * d * d),
        name="skip_bwd",
    )(idx, d_h, d_h_got, w)


def outer_kernel(idx, g, *refs, n, own, choose):
    xs = refs[:own]
    keep, send = refs[-2:]
    pairs = keep.shape[0]
    at = 0
    low = idx[1] & 1 == 0
    for k in range(0, own, 2 if choose else 1):
        x = jnp.where(idx[2] > 0, xs[k + 1][...], xs[k][...]) if choose else xs[k][...]
        width = x.shape[1]
        z = dot(g[...], x, 0, 0).astype(bf16).reshape(pairs, 2, n, width)
        keep[:, :, at : at + width] = jnp.where(low, z[:, 0], z[:, 1])
        send[:, :, at : at + width] = jnp.where(low, z[:, 1], z[:, 0])
        at += width


def outer(net, idx, g, xs, n, rows, first, into=None, choose=False):
    r, wide = g.shape
    per = max(1, 512 // (2 * n))
    while net.nf // 2 % per:
        per -= 1
    k = sum(x.shape[1] for x in xs) // (2 if choose else 1)
    out = pl.BlockSpec((per, n, k), lambda i, s: (i, first // n, 0))
    big = shape((net.nf // 2, rows, k), bf16)
    extra = list(into) if into is not None else []
    return pl.pallas_call(
        partial(outer_kernel, n=n, own=len(xs), choose=choose),
        grid_spec=pltpu.PrefetchScalarGridSpec(
            num_scalar_prefetch=1,
            grid=(wide // (2 * n * per),),
            in_specs=[pl.BlockSpec((r, 2 * n * per), lambda i, s: (0, i))]
            + [pl.BlockSpec(x.shape, lambda i, s: (0, 0)) for x in xs]
            + [pl.BlockSpec(memory_space=pl.ANY)] * len(extra),
            out_specs=[out, out],
        ),
        out_shape=[big, big],
        input_output_aliases={2 + len(xs) + i: i for i in range(len(extra))},
        compiler_params=params(),
        cost_estimate=cost(2 * r * wide * k, 2 * (r * wide + r * k + wide * k)),
        name="outer",
    )(idx, g, *xs, *extra)


def gelu_both(u):
    u2 = u * u
    t = jnp.tanh(GELU_C * u * (1.0 + 0.044715 * u2))
    half = 0.5 * (1.0 + t)
    return u * half, half + 0.5 * u * (1.0 - t * t) * (GELU_C * (1.0 + 3 * 0.044715 * u2))


def ffn_kernel(*refs, steps, second):
    x_ref, df_ref, o_in = refs[:3]
    at = 4 if second else 3
    ws = refs[at : at + steps]
    o_ref, dx_ref = refs[at + steps : at + steps + 2]
    gs = refs[at + steps + 2 : at + 2 * steps + 2]
    o_acc, dx_acc, o_low, wbuf, gbuf, sem_w, sem_g, sem_a = refs[at + 2 * steps + 2 :]
    s = pl.program_id(0)
    slot = lax.rem(s, 2)
    w_in = [pltpu.make_async_copy(ws[k], wbuf.at[k % 2], sem_w.at[k]) for k in range(steps)]
    g_out = [pltpu.make_async_copy(gbuf.at[k % 2], gs[k], sem_g.at[k]) for k in range(steps)]
    sums = [pltpu.make_async_copy(o_in, o_acc, sem_a.at[0])]
    if second:
        sums.append(pltpu.make_async_copy(refs[3], dx_acc, sem_a.at[1]))
    ends = [
        pltpu.make_async_copy(o_low if second else o_acc, o_ref, sem_a.at[2]),
        pltpu.make_async_copy(dx_acc, dx_ref, sem_a.at[3]),
    ]

    @pl.when(s == 0)
    def _():
        w_in[0].start()
        for c in sums:
            c.start()
        if not second:
            dx_acc[...] = jnp.zeros_like(dx_acc)

    for k in range(steps):

        @pl.when(s == k)
        def _():
            if k + 1 < steps:
                w_in[k + 1].start()
            w_in[k].wait()

    d = x_ref.shape[1]
    wu = wbuf[slot, :, 0].reshape(-1, d)
    wd = wbuf[slot, :, 1].reshape(-1, d)
    x, df = x_ref[...], df_ref[...]
    g, dg = gelu_both(dot(x, wu, 1, 1))
    act = g.astype(bf16)
    du = (dot(df, wd, 1, 1) * dg).astype(bf16)

    @pl.when(s == 0)
    def _():
        for c in sums:
            c.wait()

    o_acc[...] += dot(act, wd, 1, 0)
    dx_acc[...] += dot(du, wu, 1, 0)
    for k in range(2, steps):

        @pl.when(s == k)
        def _():
            g_out[k - 2].wait()

    part = gbuf.shape[1:2] + gbuf.shape[3:]
    gbuf[slot, :, 1] = dot(act, df, 0, 0).astype(bf16).reshape(part)
    gbuf[slot, :, 0] = dot(du, x, 0, 0).astype(bf16).reshape(part)
    for k in range(steps):

        @pl.when(s == k)
        def _():
            g_out[k].start()

    @pl.when(s == steps - 1)
    def _():
        if second:
            o_low[...] = o_acc[...].astype(bf16)
        for c in ends:
            c.start()
        for k in range(max(0, steps - 2), steps):
            g_out[k].wait()
        for c in ends:
            c.wait()


def ffn(x, df, o_in, pieces, dx_in=None):
    second = dx_in is not None
    r, d = x.shape
    steps = len(pieces)
    full = pl.BlockSpec((r, d), lambda s: (0, 0), pipeline_mode=pl.Buffered(1))
    far = pl.BlockSpec(memory_space=pl.ANY)
    args = [x, df, o_in] + ([dx_in] if second else []) + list(pieces)
    piece = shape(pieces[0].shape, bf16)
    units = piece.shape[0] * piece.shape[2]
    return pl.pallas_call(
        partial(ffn_kernel, steps=steps, second=second),
        grid=(steps,),
        in_specs=[full, full] + [far] * (len(args) - 2),
        out_specs=[far] * (steps + 2),
        out_shape=[shape((r, d), bf16 if second else f32), shape((r, d), f32)] + [piece] * steps,
        scratch_shapes=[
            pltpu.VMEM((r, d), f32),
            pltpu.VMEM((r, d), f32),
            pltpu.VMEM((r, d) if second else (16, LANES), bf16),
            pltpu.VMEM((2, *piece.shape), bf16),
            pltpu.VMEM((2, *piece.shape), bf16),
            pltpu.SemaphoreType.DMA((steps,)),
            pltpu.SemaphoreType.DMA((steps,)),
            pltpu.SemaphoreType.DMA((4,)),
        ],
        compiler_params=params(),
        cost_estimate=cost(12 * r * d * steps * units, 16 * r * d + 8 * steps * units * d, steps * units * r),
        name="ffn",
    )(*args)


def head_sel(h):
    lane = lax.broadcasted_iota(jnp.int32, (1, LANES), 1)
    return lane < HD if h == 0 else lane >= HD


def load_rolled(idx, hold, refs, part, rest):
    rows = refs[0].shape[-2]
    t = rows * len(refs)
    for r, ref in enumerate(refs):
        x = ref[part] if part is not None else ref[...]
        hold[pl.ds(pl.multiple_of((idx[0] ^ r) * rows, rows), rows), :] = x.astype(f32)
    hold[t : t + rest, :] = hold[0:rest, :]
    return hold[pl.ds(idx[1], t), :]


def store_unrolled(idx, hold, t, rest):
    row = lax.broadcasted_iota(jnp.int32, (rest, 1), 0)
    hold[0:rest, :] = jnp.where(row < idx[1], hold[t : t + rest, :], hold[0:rest, :])


def attn_fwd_kernel(idx, *refs, na, long):
    pieces = refs[:na]
    segr, segc = refs[na : na + 2]
    outs = refs[na + 2 : 2 * na + 2]
    lse_ref, hold, ql, kl, vt = refs[2 * na + 2 :]
    rows = outs[0].shape[0]
    t = rows * na
    rest = t - long
    ql[...] = load_rolled(idx, hold, pieces, 0, rest).astype(bf16)
    kl[...] = load_rolled(idx, hold, pieces, 1, rest).astype(bf16)
    vt[...] = jnp.transpose(load_rolled(idx, hold, pieces, 2, rest)).astype(bf16)

    def pair(r0, n, c0, cn, mask):
        q = ql[pl.ds(r0, n), :]
        k = kl[c0 : c0 + cn, :]
        got, lses = [], []
        for h in range(2):
            qh = jnp.where(head_sel(h), q, jnp.zeros_like(q))
            s = dot(k, qh, 1, 1)
            if mask is not None:
                s = jnp.where(mask, s, NEG)
            top = jnp.max(s, axis=0, keepdims=True)
            p = jnp.exp(s - top)
            total = jnp.sum(p, axis=0, keepdims=True)
            got.append(dot(vt[HD * h : HD * h + HD, c0 : c0 + cn], p.astype(bf16), 1, 0) / total)
            lses.append(top + jnp.log(total))
        lse_ref[0, :, pl.ds(r0, n)] = jnp.concatenate(lses, axis=0)
        hold[pl.ds(idx[1] + r0, n), :] = jnp.transpose(jnp.concatenate(got, axis=0))

    step = long // 2
    for i in range(2):
        pair(i * step, step, 0, long, None)
    pair(long, rest, long, rest, segc[:, :1] == segr[:1, :])
    store_unrolled(idx, hold, t, rest)
    for r in range(na):
        outs[r][...] = hold[pl.ds(pl.multiple_of((idx[0] ^ r) * rows, rows), rows), :].astype(bf16)


def attn_fwd(net, idx, pieces, segr, segc, long):
    na = net.na
    _, rows, hw = pieces[0].shape
    t = rows * na
    rest = t - long
    pairs = hw // LANES
    const = lambda a: pl.BlockSpec(a.shape, lambda j, s: (0, 0))
    work = pairs * 2 * (long * long + rest * rest)
    res = pl.pallas_call(
        partial(attn_fwd_kernel, na=na, long=long),
        grid_spec=pltpu.PrefetchScalarGridSpec(
            num_scalar_prefetch=1,
            grid=(pairs,),
            in_specs=[pl.BlockSpec((3, rows, LANES), lambda j, s: (0, 0, j))] * na + [const(segr), const(segc)],
            out_specs=[pl.BlockSpec((rows, LANES), lambda j, s: (0, j))] * na
            + [pl.BlockSpec((1, 2, t), lambda j, s: (j, 0, 0))],
            scratch_shapes=[
                pltpu.VMEM((t + rest, LANES), f32),
                pltpu.VMEM((t, LANES), bf16),
                pltpu.VMEM((t, LANES), bf16),
                pltpu.VMEM((LANES, t), bf16),
            ],
        ),
        out_shape=[shape((rows, hw), bf16)] * na + [shape((pairs, 2, t), f32)],
        compiler_params=params(),
        cost_estimate=cost(16 * HD * work, 8 * t * hw, work),
        name="attn_fwd",
    )(idx, *pieces, segr, segc)
    return res[:na], res[na]


def attn_bwd_kernel(idx, *refs, na, long):
    pieces, d_pieces = refs[:na], refs[na : 2 * na]
    lse_ref, segr, segc = refs[2 * na : 2 * na + 3]
    outs = refs[2 * na + 3 : 3 * na + 3]
    hold, ql, kl, vl, dl, kt, dqt, dka, dva = refs[3 * na + 3 :]
    rows = outs[0].shape[1]
    t = rows * na
    rest = t - long
    ql[...] = load_rolled(idx, hold, pieces, 0, rest).astype(bf16)
    kf = load_rolled(idx, hold, pieces, 1, rest)
    kl[...] = kf.astype(bf16)
    kt[...] = jnp.transpose(kf).astype(bf16)
    vl[...] = load_rolled(idx, hold, pieces, 2, rest).astype(bf16)
    dl[...] = load_rolled(idx, hold, d_pieces, None, rest).astype(bf16)
    dka[...] = jnp.zeros_like(dka)
    dva[...] = jnp.zeros_like(dva)

    def pair(r0, n, c0, cn, mask):
        q, do = ql[pl.ds(r0, n), :], dl[pl.ds(r0, n), :]
        k, v = kl[c0 : c0 + cn, :], vl[c0 : c0 + cn, :]
        dqs = []
        for h in range(2):
            qh = jnp.where(head_sel(h), q, jnp.zeros_like(q))
            dh = jnp.where(head_sel(h), do, jnp.zeros_like(do))
            s = dot(k, qh, 1, 1)
            if mask is not None:
                s = jnp.where(mask, s, NEG)
            p = jnp.exp(s - lse_ref[0, h : h + 1, pl.ds(r0, n)])
            dp = dot(v, dh, 1, 1)
            delta = jnp.sum(p * dp, axis=0, keepdims=True)
            ds = (p * (dp - delta)).astype(bf16)
            dqs.append(dot(kt[HD * h : HD * h + HD, c0 : c0 + cn], ds, 1, 0))
            dva[c0 : c0 + cn, :] += dot(p.astype(bf16), dh, 1, 0)
            dka[c0 : c0 + cn, :] += dot(ds, qh, 1, 0)
        dqt[pl.ds(r0, n), :] = jnp.transpose(jnp.concatenate(dqs, axis=0))

    step = long // 2

    def body(i, carry):
        pair(pl.multiple_of(i * step, step), step, 0, long, None)
        return carry

    lax.fori_loop(0, 2, body, 0)
    pair(long, rest, long, rest, segc[:, :1] == segr[:1, :])
    for part, src in enumerate((dqt, dka, dva)):
        x = src[...]
        if part == 0:
            x = x * (1.0 / math.sqrt(HD))
        hold[pl.ds(idx[1], t), :] = x
        store_unrolled(idx, hold, t, rest)
        for r in range(na):
            at = pl.multiple_of((idx[0] ^ r) * rows, rows)
            outs[r][part] = hold[pl.ds(at, rows), :].astype(bf16)


def attn_bwd(net, idx, pieces, d_pieces, lse, segr, segc, long, start, pairs):
    na = net.na
    rows = pieces[0].shape[1]
    t = rows * na
    rest = t - long
    hw = pairs * LANES
    const = lambda a: pl.BlockSpec(a.shape, lambda j, s: (0, 0))
    three = pl.BlockSpec((3, rows, LANES), lambda j, s: (0, 0, j + start))
    out = pl.BlockSpec((3, rows, LANES), lambda j, s: (0, 0, j))
    work = pairs * 2 * (long * long + rest * rest)
    return pl.pallas_call(
        partial(attn_bwd_kernel, na=na, long=long),
        grid_spec=pltpu.PrefetchScalarGridSpec(
            num_scalar_prefetch=1,
            grid=(pairs,),
            in_specs=[three] * na
            + [pl.BlockSpec((rows, LANES), lambda j, s: (0, j + start))] * na
            + [pl.BlockSpec((1, 2, t), lambda j, s: (j + start, 0, 0)), const(segr), const(segc)],
            out_specs=[out] * na,
            scratch_shapes=[pltpu.VMEM((t + rest, LANES), f32)]
            + [pltpu.VMEM((t, LANES), bf16)] * 4
            + [pltpu.VMEM((LANES, t), bf16)]
            + [pltpu.VMEM((t, LANES), f32)] * 3,
        ),
        out_shape=[shape((3, rows, hw), bf16)] * na,
        compiler_params=params(),
        cost_estimate=cost(40 * HD * work, 16 * t * hw, work),
        name="attn_bwd",
    )(idx, *pieces, *d_pieces, lse, segr, segc)


def prep_kernel(ints, me, w_mod, cos, sin, pick, segr, segc, smooth, part, idx, gs, *, nd, utt, long, regroup):
    nf = ints.shape[0]
    rows, rest = cos.shape[0], segr.shape[1]
    total = rows * (2 if regroup else nd)
    y, f, block = me[0], me[1], me[3]
    mine = ((f & ~1) | y) ^ f if regroup else 0
    starts, ends, at, first = [], [], 0, 0
    for u in range(utt):
        size = ints[mine, u]
        starts.append(at)
        first = jnp.where(size == long, at, first)
        at = at + size
        ends.append(at)
    idx[0], idx[1], idx[2] = block, first, me[2]
    kept = 0
    for g in range(nf):
        for u in range(utt):
            kept = kept + (1 - ints[g, utt + u])
    gs[0] = (nf * utt) / jnp.maximum(kept.astype(f32), 1.0)

    pos = block * rows + lax.broadcasted_iota(jnp.int32, (rows, LANES), 0)
    lane = lax.broadcasted_iota(jnp.int32, (rows, LANES), 1)
    offset = jnp.zeros((rows, LANES), jnp.int32)
    number = jnp.zeros((rows, LANES), jnp.int32)
    for u in range(1, utt):
        past = pos >= starts[u]
        offset = jnp.where(past, starts[u], offset)
        number = jnp.where(past, u, number)
    pick[...] = jnp.where((lane % utt == number) & (lane < 3 * utt), 1.0, 0.0).astype(bf16)
    half = HD // 2
    frequency = jnp.exp((lane[:1] % half).astype(f32) * (-math.log(10000.0) / half))
    angles = (pos - offset).astype(f32) * frequency
    cos[...] = jnp.cos(angles)
    sin[...] = jnp.where(lane[:1] % HD < half, -1.0, 1.0) * jnp.sin(angles)

    for ref, axis in ((segr, 1), (segc, 0)):
        p = first + long + lax.broadcasted_iota(jnp.int32, ref.shape, axis)
        p = jnp.where(p >= total, p - total, p)
        number = jnp.zeros(ref.shape, jnp.int32)
        for u in range(1, utt):
            number = jnp.where(p >= starts[u], u, number)
        ref[...] = number

    n, wide = smooth.shape
    d = wide * nd
    row = lax.broadcasted_iota(jnp.int32, (n, LANES), 0)
    when = jnp.zeros((n, LANES), jnp.int32)
    for j in range(n):
        k, u = divmod(j, utt)
        g = 2 * (k % (nf // 2)) + k // (nf // 2) if regroup else k
        when = jnp.where(row == j, ints[g ^ f, 2 * utt + u], when)
    flow = 1000.0 * (when[:, :1].astype(f32) / STEPS)
    col = y * wide + lax.broadcasted_iota(jnp.int32, (1, wide), 1)
    low = col < d // 2
    at = jnp.where(low, col, col - d // 2).astype(f32)
    angles = flow * jnp.exp(at * (-math.log(10000.0) / (d // 2)))
    e = jnp.where(low, jnp.sin(angles), jnp.cos(angles))
    e = (e / (1.0 + jnp.exp(-e))).astype(bf16)
    smooth[...] = e
    part[...] = dot(e, w_mod[...], 1, 0)


def prep(net, ints, me, w_mod, rows, long, rest):
    utt = ints.shape[1] // 3
    n = net.nf * utt
    smem = pl.BlockSpec(memory_space=pltpu.SMEM)
    vmem = pl.BlockSpec(memory_space=pltpu.VMEM)
    return pl.pallas_call(
        partial(prep_kernel, nd=net.nd, utt=utt, long=long, regroup=net.regroup),
        in_specs=[smem, smem, vmem],
        out_specs=[vmem] * 7 + [smem, smem],
        out_shape=[
            shape((rows, LANES), f32),
            shape((rows, LANES), f32),
            shape((rows, LANES), bf16),
            shape((8, rest), jnp.int32),
            shape((rest, LANES), jnp.int32),
            shape((n, w_mod.shape[0]), bf16),
            shape((n, w_mod.shape[1]), f32),
            shape((3,), jnp.int32),
            shape((1,), f32),
        ],
        compiler_params=params(32),
        cost_estimate=cost(2 * n * w_mod.size, 16 * rows * LANES, 4 * n * w_mod.shape[0]),
        name="prep",
    )(ints, me, w_mod)


def terms_kernel(*refs):
    out = refs[-1]
    x = refs[0][...]
    for ref in refs[1:-1]:
        x = x + ref[...]
    a = x.astype(bf16)
    b = (x - a.astype(f32)).astype(bf16)
    c = (x - a.astype(f32) - b.astype(f32)).astype(bf16)
    n = x.shape[0]
    out[...] = jnp.zeros_like(out)
    out[0 : 3 * n, :] = jnp.concatenate([a.astype(f32), b.astype(f32), c.astype(f32)], axis=0).astype(bf16)


def three_terms(*xs):
    return pl.pallas_call(
        terms_kernel,
        out_shape=shape((LANES, xs[0].shape[1]), bf16),
        compiler_params=params(16),
        cost_estimate=cost(0, 300 * xs[0].shape[1]),
        name="three_terms",
    )(*xs)


def scale_kernel(gs, x, out):
    out[...] = (x[...].astype(f32) * gs[0]).astype(bf16)


def scaled(x, gs):
    r, d = x.shape
    rb = min(512, r)
    row = pl.BlockSpec((rb, d), lambda i, s: (i, 0))
    return pl.pallas_call(
        scale_kernel,
        grid_spec=pltpu.PrefetchScalarGridSpec(num_scalar_prefetch=1, grid=(r // rb,), in_specs=[row], out_specs=row),
        out_shape=shape((r, d), bf16),
        compiler_params=params(16),
        cost_estimate=cost(r * d, 4 * r * d),
        name="scaled",
    )(gs, x)


def to_units(net, turned, w_down, y, f):
    nd, nf = net.nd, net.nf
    units = w_down.shape[0] // nf
    down = lax.all_to_all(w_down, "fsdp", split_axis=0, concat_axis=1, tiled=True)
    got = []
    for j in range(nd):
        perm = [(a * nf + b, nd * b + (a + j) % nd) for a in range(nd) for b in range(nf)]
        send = lax.dynamic_slice_in_dim(turned, (y + j) % nd * units, units, 0)
        got.append(move(net, send, perm, y, f))
    return got, down


def mix_kernel(idx, *refs, half, nd):
    ups, down, out = refs[:nd], refs[nd], refs[nd + 1]
    units, width = ups[0].shape
    own = lax.rem(idx[0], nd)
    for j, up in enumerate(ups):
        col = pl.multiple_of(lax.rem(own + nd - j, nd) * width, width)
        for at in range(0, units, half):
            out[2 * at : 2 * at + half, pl.ds(col, width)] = up[at : at + half, :]
    for at in range(0, units, half):
        out[2 * at + half : 2 * at + 2 * half, :] = down[at : at + half, :]


def own_units(net, ups, down, half, y, f):
    whole = pl.BlockSpec(memory_space=pltpu.VMEM)
    return pl.pallas_call(
        partial(mix_kernel, half=half, nd=net.nd),
        in_specs=[pl.BlockSpec(memory_space=pltpu.SMEM)] + [whole] * (net.nd + 1),
        out_specs=whole,
        out_shape=shape((2 * down.shape[0], down.shape[1]), bf16),
        compiler_params=params(16),
        cost_estimate=cost(0, 8 * down.size),
        name="own_units",
    )(jnp.stack([y * net.nf + f]).astype(jnp.int32), *ups, down)


def from_units(net, g_up, g_down, y, f):
    nd, nf = net.nd, net.nf
    grad_down = lax.all_to_all(g_down, "fsdp", split_axis=1, concat_axis=0, tiled=True)
    width = g_up.shape[1] // nd
    own = (y * nf + f) % nd
    got = []
    for j in range(nd):
        perm = [(nd * b + (a + j) % nd, a * nf + b) for a in range(nd) for b in range(nf)]
        send = lax.dynamic_slice_in_dim(g_up, (own - j) % nd * width, width, 1)
        got.append(move(net, send, perm, y, f))
    got = jnp.stack(got)
    rows = [lax.dynamic_index_in_dim(got, (h - y) % nd, 0, keepdims=False) for h in range(nd)]
    return jnp.concatenate(rows, axis=0).T.astype(f32), grad_down.astype(f32)


def move(net, x, perm, y, f):
    fixed = [a for a, b in perm if a == b]
    got = lax.ppermute(x, ("dp", "fsdp"), [(a, b) for a, b in perm if a != b])
    me = y * net.nf + f
    stays = False
    for a in fixed:
        stays = stays | (me == a)
    return jnp.where(stays, x, got) if fixed else got


def local(net, frames, skip_in, cond_in, lengths, drop_mask, time_index, w_skip, w_qkv, w_out, w_up, w_down, w_mod, d_out):
    frames, skip_in, cond_in, d_out = frames[0], skip_in[0], cond_in[0], d_out[0]
    rows, d = frames.shape
    nd, nf, na = net.nd, net.nf, net.na
    y, f = lax.axis_index("dp"), lax.axis_index("fsdp")
    utt = lengths.shape[1]
    group_len = rows * nd
    long = int(group_len * LONG_PART)
    rest = group_len - long
    core_bit = ("fsdp", 1)
    n_skip, n_qkv, n_out = w_skip.shape[1], w_qkv.shape[1], w_out.shape[1]
    part_of = lambda n, share: int(n * share) // 16 * 16
    block = net.attn_index()
    moved = ((f & 1) != y if net.regroup else y < 0).astype(jnp.int32)
    me = jnp.stack([y, f, moved, block]).astype(jnp.int32)
    cut = rows // 2
    cols = w_mod.shape[1]

    skip_turned, qkv_turned, out_turned, up_turned = flip(w_skip, w_qkv, w_out, w_up)
    g1 = Gather(net, skip_turned, part_of(n_skip, 0.5))
    g2 = Gather(net, jnp.concatenate([qkv_turned, out_turned], axis=0), part_of(n_qkv + n_out, 0.33))
    lens = jnp.concatenate([lengths, drop_mask], axis=0)
    ints = jnp.concatenate([lengths, drop_mask, time_index], axis=1)
    bits = list(range(net.fb))

    def more_ints():
        nonlocal ints
        if bits:
            ints = jnp.concatenate([ints, net.swap(ints, ("fsdp", 1 << bits.pop(0)))], axis=0)

    def step(g):
        if g.done < g.common:
            g.join()

    def start(g):
        if g.done < g.common:
            g.send()
        else:
            g.raw = []

    while g1.done < g1.common:
        g1.send()
        more_ints()
        g1.raw, (ints, lens), g2.x = tie(g1.raw, [ints, lens], g2.x)
        g1.join()
    g1.send()
    start(g2)
    while bits:
        more_ints()
    g1.raw, g2.raw, (ints, up_turned, w_down) = tie(g1.raw, g2.raw, [ints, up_turned, w_down])
    g1.join()
    step(g2)
    g1.send()
    start(g2)
    up_parts, down = to_units(net, up_turned, w_down, y, f)
    cos, sin, pick, segr, segc, smooth, part, idx, gs = prep(net, ints, me, w_mod, rows, long, rest)
    if net.regroup:
        part = part.reshape(2, nf // 2, utt, cols)
        mod_got = net.swap(lax.dynamic_index_in_dim(part, 1 - y, 0, keepdims=False), ("dp", 1))
        part = lax.dynamic_index_in_dim(part, y, 0, keepdims=False)
    else:
        for b in range(net.db):
            part = part + net.swap(part, ("dp", 1 << b))
        mod_got = part
    g1.raw, g2.raw, (ints, down, part, mod_got), up_parts = tie(
        g1.raw, g2.raw, [ints, down, part, mod_got], up_parts
    )
    g1.join()
    theirs = g1.core(g1.x + g1.far)
    step(g2)
    g2.finish_common()
    g2.send()
    if net.regroup:
        part = jnp.broadcast_to((part + mod_got)[:, None], (nf // 2, 2, utt, cols))
    part = part.reshape(nf, utt, cols)
    mod = lax.all_to_all(part, "fsdp", split_axis=0, concat_axis=2, tiled=True)
    skip_t, = place(net, me, g1, theirs, [n_skip])
    (skip_t, lens), = tie([skip_t, lens])
    hidden0, mixed = skip_fwd(me, lens, frames, skip_in, cond_in, skip_t)
    (hidden0, mixed, mod, down), g2.raw, up_parts = tie([hidden0, mixed, mod, down], g2.raw, up_parts)

    hidden_got = [net.trade(hidden0)]
    g2.join()
    g2.send()
    units = down.shape[0]
    half = units // 2 if units // 2 % 16 == 0 else units
    g3 = Gather(net, own_units(net, up_parts, down, half, y, f), units * 2 if half == units else units)
    start(g3)
    mods = three_terms(mod.reshape(utt, nf * cols))
    mod_a, mod_f = mods[:, : 2 * d], mods[:, 2 * d :]
    (hidden0, mod_a, mod_f, d_out), g2.raw, g3.raw = tie([hidden0, mod_a, mod_f, d_out], g2.raw, g3.raw)
    g2.join()
    theirs = g2.core(g2.x + g2.far)
    qkv_t, out_t = place(net, me, g2, theirs, [n_qkv, n_out])
    step(g3)
    (hidden0, qkv_t, out_t, d_out), hidden_got, g3.x = tie([hidden0, qkv_t, out_t, d_out], hidden_got, g3.x)

    start(g3)
    d_f0 = scaled(d_out, gs)
    d_f_got = [net.trade(d_f0[:cut])]
    hidden, normed_a, sent = qkv_fwd(net, idx, hidden0, hidden_got[0], pick, mod_a, qkv_t, cos, sin)
    sent, g3.raw, d_f_got, (d_f0,) = tie(list(sent), g3.raw, d_f_got, [d_f0])
    step(g3)
    g3.finish_common()
    pieces = [sent[0]] + [net.attn_swap(sent[r], r) for r in range(1, na)]
    pieces, (d_f0,), g3.x = tie(pieces, [d_f0], g3.x)
    g3.send()
    d_f_got.append(net.trade(d_f0[cut:]))
    attn_p, lse = attn_fwd(net, idx, pieces, segr, segc, long)
    (lse,), d_f_got, attn_p, g3.raw = tie([lse], d_f_got, list(attn_p), g3.raw)
    attn_p = [attn_p[0]] + [net.attn_swap(attn_p[r], r) for r in range(1, na)]
    g3.join()
    attn_p, near = tie(attn_p, g3.x)
    g3.send()
    near_core = g3.core(near)
    attn, hidden2, normed_f, d_f = out_fwd(net, idx, attn_p, hidden, pick, mod_f, out_t, d_f0, d_f_got)

    view = lambda x: x.reshape(x.shape[0], 2, x.shape[1] // 2, x.shape[2])
    acc, dx, *got1 = ffn(normed_f, d_f, hidden2, [view(x) for x in near_core + near])
    (acc, dx, mixed, skip_in), far, got1 = tie([acc, dx, mixed, skip_in], g3.raw, got1)
    mixed_got, skip_got = net.trade(mixed), net.trade(skip_in)
    far_core = g3.core(far)
    count = len(far)
    swapped1 = [net.swap(x, core_bit) for x in got1[:count]]
    out_b, dx, *got2 = ffn(normed_f, d_f, acc, [view(x) for x in far_core + far], dx)
    (out_b, dx, mixed_got), got2, swapped1 = tie([out_b, dx, mixed_got], got2, swapped1)
    swapped2 = [net.swap(x, core_bit) for x in got2[:count]]

    d_h2, d_att, sums_f, d_attn_p = out_bwd(net, idx, dx, hidden2, d_f, pick, mod_f[:, d:], out_t)
    (d_h2, d_att, skip_got), d_attn_p, swapped2 = tie([d_h2, d_att, skip_got], list(d_attn_p), swapped2)
    d_attn_p = [d_attn_p[0]] + [net.attn_swap(d_attn_p[r], r) for r in range(1, na)]
    sum_far = [plus(a, b) for a, b in zip(got2[count:], swapped2)]
    d_attn_p, sum_far, (d_att,) = tie(d_attn_p, sum_far, [d_att])
    came = [net.swap(x, o[-2]) for x, o in zip(sum_far, g3.orders)]
    into = outer(net, me, d_att, [attn], n_out, n_qkv + n_out, n_qkv)
    d_attn_p, into, (out_b,) = tie(d_attn_p, list(into), [out_b])

    def send_half(xs, bits):
        n = xs[0].shape[0] // 2
        return [x[:n] for x in xs], [net.swap(x[n:], b) for x, b in zip(xs, bits)]

    all_pairs = d // na // LANES
    pairs = max(1, all_pairs // 2)
    d_sent = attn_bwd(net, idx, pieces, d_attn_p, lse, segr, segc, long, 0, pairs)
    d_sent, came, d_attn_p = tie(list(d_sent), came, d_attn_p)
    d_pieces = [d_sent[0]] + [net.attn_swap(d_sent[r], r) for r in range(1, na)]
    ff = [plus(a, b, c) for a, b, c in zip(got1[count:], swapped1, came)]
    d_attn_p, ff, (out_b,) = tie(d_attn_p, ff, [out_b])
    kept, raw = send_half(ff, [o[-3] for o in g3.orders])
    output_got = net.trade(out_b)
    if all_pairs > pairs:
        d_sent = attn_bwd(net, idx, pieces, d_attn_p, lse, segr, segc, long, pairs, all_pairs - pairs)
        d_sent, (output_got,), raw, d_pieces = tie(list(d_sent), [output_got], raw, d_pieces)
        d_pieces += [d_sent[0]] + [net.attn_swap(d_sent[r], r) for r in range(1, na)]
    ff = jnp.stack([plus(a, b) for a, b in zip(kept, raw)], axis=1)
    common = list(reversed(g3.orders[0][:-3]))
    d_pieces, (ff,) = tie(d_pieces, [ff])
    raw = []
    if common:
        kept, raw = send_half([ff], [common[0]])
    d_qkv = turn_back(net, idx, d_pieces, cos, sin, d)
    d_h, sums_a = qkv_bwd(d_qkv, hidden, d_h2, pick, mod_a[:, d:], qkv_t)
    (d_h, sums_a, d_qkv, output_got), raw = tie([d_h, sums_a, d_qkv, output_got], raw)
    if common:
        ff = plus(kept[0], raw[0])
    raw = []
    if len(common) > 1:
        kept, raw = send_half([ff], [common[1]])
    keep1, send1 = outer(net, me, d_h, [mixed, mixed_got, skip_in, skip_got], n_skip, n_skip, 0, choose=True)
    (keep1, send1, d_qkv, d_h), = tie([keep1, send1, d_qkv, d_h])
    got1 = net.swap(send1, core_bit)
    keep2, send2 = outer(net, me, d_qkv, [normed_a], n_qkv, n_qkv + n_out, 0, into)
    (keep2, send2, keep1, got1), = tie([keep2, send2, keep1, got1])
    got2 = net.swap(send2, core_bit)
    s1 = Sum(net, plus(keep1, got1))
    s1.send()
    (keep2, got2), = tie([keep2, got2])
    s2 = Sum(net, plus(keep2, got2))
    (s2.parts[0][0], s2.parts[1][0], sums_a, d_h, out_b), s1.raw = tie([s2.parts[0][0], s2.parts[1][0], sums_a, d_h, out_b], s1.raw)
    s2.send()
    s1.join()
    s1.send()
    d_h_got = net.trade(d_h)
    output = net.traded(out_b, output_got)

    d_mod = jnp.concatenate([sums_a, sums_f], axis=1).reshape(utt, nf, cols).transpose(1, 0, 2)
    d_mod = lax.all_to_all(d_mod, "fsdp", split_axis=0, concat_axis=0, tiled=True)
    s2.raw, s1.raw, raw, (d_h, d_mod, output) = tie(s2.raw, s1.raw, raw, [d_h, d_mod, output])
    if len(common) > 1:
        ff = plus(kept[0], raw[0])
    for bit in common[2:]:
        kept, raw = send_half([ff], [bit])
        ff = plus(kept[0], raw[0])
    ff = ff.reshape(-1, 2, half, d)
    s2.join()
    s2.send()
    s1.join()
    s1.send()
    grad_up, grad_down = from_units(net, ff[:, 0].reshape(units, d), ff[:, 1].reshape(units, d), y, f)
    s1.raw, s2.raw, (d_h, d_h_got, grad_up, grad_down) = tie(s1.raw, s2.raw, [d_h, d_h_got, grad_up, grad_down])
    s2.join()
    s2.send()
    s1.join()
    if s1.left:
        s1.send()
    d_frames, d_skip = skip_bwd(me, d_h, d_h_got, skip_t)
    s1.raw, s2.raw, (d_frames, d_skip, d_mod) = tie(s1.raw, s2.raw, [d_frames, d_skip, d_mod])
    if net.regroup:
        pair_sum = d_mod.reshape(nf // 2, 2, utt, cols).sum(axis=1)
        here = (jnp.arange(2) == y).astype(f32)
        d_mod = pair_sum[None] * here[:, None, None, None]
    d_mod = d_mod.reshape(nf * utt, cols)
    for b in range(net.db):
        d_mod = d_mod + net.swap(d_mod, ("dp", 1 << b))
    while s2.left:
        s2.join()
        if s1.left:
            s1.join()
        if s2.left:
            s2.send()
        if s1.left:
            s1.send()
        if s1.left and s2.left:
            s1.raw, s2.raw = tie(s1.raw, s2.raw)
    g_two = s2.finish()
    grad_qkv = g_two[:n_qkv].T.astype(f32)
    grad_out = g_two[n_qkv:].T.astype(f32)
    grad_skip = s1.finish().T.astype(f32)
    grad_mod = jnp.dot(smooth.astype(f32).T, d_mod, precision=highest)

    return (output[None], d_frames[None], d_skip[None], grad_skip, grad_qkv, grad_out, grad_up, grad_down, grad_mod)


def solution(mesh):
    rows = P("fsdp", "dp", None)
    ints = P("fsdp", None)
    weight = P("dp", "fsdp")
    return jax.shard_map(
        partial(local, Net(mesh)),
        mesh=mesh,
        in_specs=(rows, rows, rows, ints, ints, ints, *([weight] * 6), rows),
        out_specs=(rows, rows, rows, *([weight] * 6)),
        check_vma=False,
    )
```

```python
from functools import partial
import math

import jax
import jax.numpy as jnp
from jax import lax
from jax.experimental import pallas as pl
from jax.experimental.pallas import tpu as pltpu
from jax.sharding import PartitionSpec as P

HD = 64
LANES = 128
STEPS = 1000
LONG_PART = 0.75
NEG = -1e30
GELU_C = math.sqrt(2.0 / math.pi)
VMEM_MIB = 60

bf16 = jnp.bfloat16
f32 = jnp.float32
highest = lax.Precision.HIGHEST
epsilon = 1e-06


def dot(a, b, ca, cb):
    return lax.dot_general(a, b, (((ca,), (cb,)), ((), ())), preferred_element_type=f32)


def params(mib=VMEM_MIB):
    return pltpu.CompilerParams(vmem_limit_bytes=mib * 2**20)


def cost(flops, nbytes, trans=0):
    return pl.CostEstimate(flops=int(flops), bytes_accessed=int(nbytes), transcendentals=int(trans))


def shape(dims, dtype):
    return jax.ShapeDtypeStruct(dims, dtype)


class Net:
    def __init__(self, mesh):
        self.nd = mesh.shape["dp"]
        self.nf = mesh.shape["fsdp"]
        self.fb = self.nf.bit_length() - 1
        self.db = self.nd.bit_length() - 1
        common = [("fsdp", 1 << b) for b in range(self.fb - 1, 1, -1)]
        common += [("dp", 1 << b) for b in range(self.db - 1, 0, -1)]
        x, y, core = ("fsdp", 2), ("dp", 1), ("fsdp", 1)
        self.orders = (common + [x, y, core], common + [y, x, core])
        self.regroup = self.nd == 2
        self.int_bits = [*range(2, self.fb), 0, 1]
        self.na = 2 if self.regroup else self.nd

    def swap(self, x, bit):
        axis, mask = bit
        size = self.nf if axis == "fsdp" else self.nd
        return lax.ppermute(x, axis, [(i, i ^ mask) for i in range(size)])

    def attn_swap(self, x, r):
        return self.swap(x, ("fsdp", r) if self.regroup else ("dp", r))

    def attn_index(self):
        return lax.axis_index("fsdp") & 1 if self.regroup else lax.axis_index("dp")

    def group_of(self, f, y):
        return (f & ~1) | y if self.regroup else f

    def trade(self, x):
        if not self.regroup:
            return x
        perm = []
        for y in range(self.nd):
            for f in range(self.nf):
                c = f & 1
                if c != y:
                    perm.append((y * self.nf + f, c * self.nf + (f & ~1 | y)))
        return lax.ppermute(x, ("dp", "fsdp"), perm)

    def traded(self, x, got):
        if not self.regroup:
            return x
        return jnp.where(lax.axis_index("fsdp") & 1 != lax.axis_index("dp"), got, x)

    def offsets(self, order):
        out = []
        for s in range(self.nd * self.nf):
            d = f = 0
            for j, (axis, mask) in enumerate(order):
                if s >> j & 1:
                    if axis == "dp":
                        d ^= mask
                    else:
                        f ^= mask
            out.append((d, f))
        return out

    def halves(self, x, bit, axes):
        axis, mask = bit
        b = jnp.where(lax.axis_index(axis) & mask != 0, 1, 0)
        if axis == "fsdp":
            at = axes.index(mask)
            keep = lax.dynamic_index_in_dim(x, b, at, keepdims=False)
            send = lax.dynamic_index_in_dim(x, 1 - b, at, keepdims=False)
            return keep, send, axes[:at] + axes[at + 1 :]
        half = x.shape[-1] // 2
        keep = lax.dynamic_slice_in_dim(x, b * half, half, x.ndim - 1)
        send = lax.dynamic_slice_in_dim(x, (1 - b) * half, half, x.ndim - 1)
        return keep, send, axes


def plus(*xs):
    total = xs[0].astype(f32)
    for x in xs[1:]:
        total = total + x.astype(f32)
    return total.astype(bf16)


def tie(*groups):
    flat = lax.optimization_barrier(tuple(x for g in groups for x in g))
    out, at = [], 0
    for g in groups:
        out.append(list(flat[at : at + len(g)]))
        at += len(g)
    return out


class Gather:
    def __init__(self, net, block, split):
        self.net = net
        rows = block.shape[0]
        cuts = [(0, split, net.orders[0]), (split, rows, net.orders[1])]
        cuts = [c for c in cuts if c[0] < c[1]]
        self.bounds = [c[:2] for c in cuts]
        self.orders = [c[2] for c in cuts]
        self.x = [block[None]]
        self.done = 0
        self.common = len(net.orders[0]) - 3

    def send(self):
        if self.done == self.common:
            self.x = [self.x[0][:, a:b] for a, b in self.bounds]
        self.raw = [self.net.swap(x, o[self.done]) for x, o in zip(self.x, self.orders)]

    def join(self):
        if self.done == self.common + 1:
            self.far = self.raw
        else:
            self.x = [jnp.concatenate([x, r], axis=0) for x, r in zip(self.x, self.raw)]
        self.done += 1

    def finish_common(self):
        while self.done < self.common:
            self.send()
            self.join()

    def core(self, which):
        return [self.net.swap(x, self.orders[0][-1]) for x in which]


class Sum:
    def __init__(self, net, x):
        self.net = net
        n = x.shape[1]
        x = x.reshape((2,) * (net.fb - 1) + x.shape[1:])
        axes = [1 << b for b in range(net.fb - 1, 0, -1)]
        dps = [("dp", 1 << b) for b in range(net.db - 1, -1, -1)]
        fs = [("fsdp", 1 << b) for b in range(1, net.fb)]
        half = n // 2
        self.parts = [
            [lax.slice_in_dim(x, p * half, p * half + half, axis=x.ndim - 2), axes, order]
            for p, order in enumerate((dps + fs[:1], fs[:1] + dps))
        ]
        self.tail = fs[1:]

    @property
    def left(self):
        return max(len(p[2]) for p in self.parts) + len(self.tail)

    def send(self):
        if not self.parts[0][2] and len(self.parts) > 1:
            self.parts = [[jnp.concatenate([p[0] for p in self.parts], axis=-2), self.parts[0][1], self.tail]]
            self.tail = []
        self.keeps, self.raw = [], []
        for p in self.parts:
            keep, send, p[1] = self.net.halves(p[0], p[2][0], p[1])
            self.keeps.append(keep)
            self.raw.append(self.net.swap(send, p[2][0]))

    def join(self):
        for p, keep, got in zip(self.parts, self.keeps, self.raw):
            p[0] = plus(keep, got)
            p[2] = p[2][1:]

    def finish(self):
        while self.left:
            self.send()
            self.join()
        return self.parts[0][0]


def place_kernel(idx, *refs, plans, count):
    srcs, outs, sems = refs[:count], refs[count:-1], refs[-1]
    copies = []
    for ref, plan in zip(srcs, plans):
        kd = ref.shape[2]
        for slot, ((d, f), moves) in enumerate(plan):
            for first, rows, which, n, start in moves:
                row = pl.multiple_of((idx[1] ^ f) * n + start, 16)
                col = pl.multiple_of((idx[0] ^ d) * kd, LANES)
                copies.append(
                    pltpu.make_async_copy(
                        ref.at[slot, pl.ds(first, rows), :],
                        outs[which].at[pl.ds(row, rows), pl.ds(col, kd)],
                        sems.at[len(copies)],
                    )
                )
    for c in copies:
        c.start()
    for c in copies:
        c.wait()


def place(net, idx, gather, theirs, sizes):
    pieces = gather.x + gather.far + theirs
    lanes = pieces[0].shape[-1]
    plans = []
    total = 0
    count = len(gather.bounds)
    for i in range(len(pieces)):
        quarter, part = divmod(i, count)
        offs = net.offsets(gather.orders[part])
        some = offs[quarter * len(offs) // 4 : (quarter + 1) * len(offs) // 4]
        lo, hi = gather.bounds[part]
        moves, at = [], 0
        for which, n in enumerate(sizes):
            a, b = max(lo, at), min(hi, at + n)
            if a < b:
                moves.append((a - lo, b - a, which, n, a - at))
            at += n
        plans.append([(o, moves) for o in some])
        total += len(some) * len(moves)
    shapes = [shape((n * net.nf, lanes * net.nd), bf16) for n in sizes]
    return pl.pallas_call(
        partial(place_kernel, plans=plans, count=len(pieces)),
        grid_spec=pltpu.PrefetchScalarGridSpec(
            num_scalar_prefetch=1,
            grid=(1,),
            in_specs=[pl.BlockSpec(memory_space=pl.ANY)] * len(pieces),
            out_specs=[pl.BlockSpec(memory_space=pl.ANY)] * len(sizes),
            scratch_shapes=[pltpu.SemaphoreType.DMA((total,))],
        ),
        out_shape=shapes,
        compiler_params=params(16),
        cost_estimate=cost(0, 4 * sum(sizes) * net.nf * lanes * net.nd),
        name="place",
    )(idx, *pieces)


def norm_stats(x):
    mean = jnp.mean(x, axis=-1, keepdims=True)
    centered = x - mean
    var = jnp.mean(centered * centered, axis=-1, keepdims=True)
    rstd = lax.rsqrt(var + epsilon)
    return centered * rstd, rstd


def seg_sums(pick, x):
    top = x.astype(bf16)
    low = (x - top.astype(f32)).astype(bf16)
    return (dot(pick, top, 0, 0) + dot(pick, low, 0, 0))[:8]


def flip_kernel(*refs):
    n = len(refs) // 2
    for src, dst in zip(refs[:n], refs[n:]):
        dst[...] = jnp.transpose(src[...].astype(f32)).astype(bf16)


def flip(*xs):
    return pl.pallas_call(
        flip_kernel,
        out_shape=[shape(x.shape[::-1], bf16) for x in xs],
        compiler_params=params(32),
        cost_estimate=cost(0, 4 * sum(x.size for x in xs)),
        name="flip",
    )(*xs)


def skip_fwd_kernel(idx, lens, frames, skip, cond, w, hidden, mixed):
    rb, d = frames.shape
    pos = idx[0] * (rb * pl.num_programs(0)) + pl.program_id(0) * rb + lax.broadcasted_iota(jnp.int32, (rb, 1), 0)
    keep = jnp.zeros((rb, 1), f32)
    end = 0
    for u in range(lens.shape[1]):
        start, end = end, end + lens[0, u]
        keep = jnp.where((pos >= start) & (pos < end), (1 - lens[1, u]).astype(f32), keep)
    m = (frames[...].astype(f32) + keep * cond[...].astype(f32)).astype(bf16)
    mixed[...] = m
    hidden[...] = (dot(m, w[:, :d], 1, 1) + dot(skip[...], w[:, d:], 1, 1)).astype(bf16)


def skip_fwd(idx, lens, frames, skip, cond, w):
    r, d = frames.shape
    rb = min(256, r)
    row = pl.BlockSpec((rb, d), lambda i, s, t: (i, 0))
    return pl.pallas_call(
        skip_fwd_kernel,
        grid_spec=pltpu.PrefetchScalarGridSpec(
            num_scalar_prefetch=2,
            grid=(r // rb,),
            in_specs=[row, row, row, pl.BlockSpec(w.shape, lambda i, s, t: (0, 0))],
            out_specs=[row, row],
        ),
        out_shape=[shape((r, d), bf16)] * 2,
        compiler_params=params(),
        cost_estimate=cost(4 * r * d * d, 10 * r * d + 4 * d * d),
        name="skip_fwd",
    )(idx, lens, frames, skip, cond, w)


def turn(x, cos, sin, sign):
    width = x.shape[1]
    reps = width // LANES
    if reps > 1:
        cos = jnp.concatenate([cos] * reps, axis=1)
        sin = jnp.concatenate([sin] * reps, axis=1)
    lane = lax.broadcasted_iota(jnp.int32, (1, width), 1)
    other = jnp.where(lane % HD < HD // 2, pltpu.roll(x, width - HD // 2, 1), pltpu.roll(x, HD // 2, 1))
    return x * cos + other * sin if sign > 0 else x * cos - other * sin


def chosen(idx, own, got, part):
    half = pl.program_id(0) * 2 < pl.num_programs(0)
    new = jnp.where(half, got[0][part, :], got[1][part, :]) if len(got) > 1 else got[0][part, :]
    return jnp.where(idx[2] > 0, new, own[part, :])


def parts_of(rows):
    return (slice(0, rows),)


def chosen_specs(rb, d, steps, halves=2):
    row = pl.BlockSpec((rb, d), lambda i, s: (i, 0))
    if halves == 1:
        return [row, row]
    return [
        row,
        pl.BlockSpec((rb, d), lambda i, s: (jnp.minimum(i, steps // 2 - 1), 0)),
        pl.BlockSpec((rb, d), lambda i, s: (jnp.maximum(i - steps // 2, 0), 0)),
    ]


def qkv_fwd_kernel(idx, hidden0, got, pick, mod, w, cos, sin, hidden, normed, *pieces):
    d = hidden.shape[1]
    na = len(pieces)
    hw = d // na
    ys = []
    for rows in parts_of(hidden.shape[0]):
        h = chosen(idx, hidden0, (got,), rows)
        hidden[rows, :] = h
        xh, _ = norm_stats(h.astype(f32))
        pk = pick[rows, :]
        y = (xh * (1.0 + dot(pk, mod[:, d:], 1, 0)) + dot(pk, mod[:, :d], 1, 0)).astype(bf16)
        normed[rows, :] = y
        ys.append((rows, y))
    for rows, y in ys:
        for part in range(3):
            for r in range(na):
                at = pl.multiple_of(part * d + (idx[0] ^ r) * hw, hw)
                z = dot(y, w[pl.ds(at, hw), :], 1, 1)
                if part < 2:
                    z = turn(z, cos[rows, :], sin[rows, :], 1)
                if part == 0:
                    z = z * (1.0 / math.sqrt(HD))
                pieces[r][part, rows, :] = z.astype(bf16)


def qkv_fwd(net, idx, hidden0, got, pick, mod, w, cos, sin):
    r, d = hidden0.shape
    rb = min(256, r // 2)
    hw = d // net.na
    row = pl.BlockSpec((rb, d), lambda i, s: (i, 0))
    narrow = pl.BlockSpec((rb, LANES), lambda i, s: (i, 0))
    out = pl.BlockSpec((3, rb, hw), lambda i, s: (0, i, 0))
    res = pl.pallas_call(
        qkv_fwd_kernel,
        grid_spec=pltpu.PrefetchScalarGridSpec(
            num_scalar_prefetch=1,
            grid=(r // rb,),
            in_specs=chosen_specs(rb, d, r // rb, 1)
            + [
                narrow,
                pl.BlockSpec(mod.shape, lambda i, s: (0, 0)),
                pl.BlockSpec(w.shape, lambda i, s: (0, 0)),
                narrow,
                narrow,
            ],
            out_specs=[row, row] + [out] * net.na,
        ),
        out_shape=[shape((r, d), bf16)] * 2 + [shape((3, r, hw), bf16)] * net.na,
        compiler_params=params(),
        cost_estimate=cost(6 * r * d * d, 14 * r * d + 6 * d * d),
        name="qkv_fwd",
    )(idx, hidden0, got, pick, mod, w, cos, sin)
    return res[0], res[1], res[2:]


def out_fwd_kernel(idx, *refs, na):
    pieces = refs[:na]
    hidden, pick, mod, w, d_f0, got0, got1, attn, hidden2, normed, d_f = refs[na:]
    d = hidden.shape[1]
    hw = d // na
    for rows in parts_of(hidden.shape[0]):
        d_f[rows, :] = chosen(idx, d_f0, (got0, got1), rows)
        for r in range(na):
            attn[rows, pl.ds(pl.multiple_of((idx[0] ^ r) * hw, hw), hw)] = pieces[r][rows, :]
        h2 = hidden[rows, :].astype(f32) + dot(attn[rows, :], w[...], 1, 1)
        hidden2[rows, :] = h2
        xh, _ = norm_stats(h2)
        pk = pick[rows, :]
        normed[rows, :] = (xh * (1.0 + dot(pk, mod[:, d:], 1, 0)) + dot(pk, mod[:, :d], 1, 0)).astype(bf16)


def out_fwd(net, idx, pieces, hidden, pick, mod, w, d_f0, d_f_got):
    r, d = hidden.shape
    rb = min(256, r // 2)
    hw = d // net.na
    row = pl.BlockSpec((rb, d), lambda i, s: (i, 0))
    narrow = pl.BlockSpec((rb, LANES), lambda i, s: (i, 0))
    return pl.pallas_call(
        partial(out_fwd_kernel, na=net.na),
        grid_spec=pltpu.PrefetchScalarGridSpec(
            num_scalar_prefetch=1,
            grid=(r // rb,),
            in_specs=[pl.BlockSpec((rb, hw), lambda i, s: (i, 0))] * net.na
            + [
                row,
                narrow,
                pl.BlockSpec(mod.shape, lambda i, s: (0, 0)),
                pl.BlockSpec(w.shape, lambda i, s: (0, 0)),
            ]
            + chosen_specs(rb, d, r // rb),
            out_specs=[row, row, row, row],
        ),
        out_shape=[shape((r, d), bf16), shape((r, d), f32)] + [shape((r, d), bf16)] * 2,
        compiler_params=params(),
        cost_estimate=cost(2 * r * d * d, 12 * r * d + 2 * d * d),
        name="out_fwd",
    )(idx, *pieces, hidden, pick, mod, w, d_f0, *d_f_got)


def norm_back(x, grad, pick, scale):
    xh, rstd = norm_stats(x)
    g = grad * (1.0 + dot(pick, scale, 1, 0))
    dx = rstd * (
        g
        - jnp.mean(g, axis=-1, keepdims=True)
        - xh * jnp.mean(g * xh, axis=-1, keepdims=True)
    )
    return dx, seg_sums(pick, grad * xh), seg_sums(pick, grad)


def out_bwd_kernel(idx, grad, hidden2, d_f, pick, scale, w, d_h2, d_att, sums, *outs):
    refs, hold = outs[:-1], outs[-1]
    i = pl.program_id(0)
    na = len(refs)
    d = grad.shape[1]
    hw = d // na
    both = jnp.zeros(sums.shape, f32)
    for rows in parts_of(grad.shape[0]):
        dx, d_scale, d_shift = norm_back(hidden2[rows, :], grad[rows, :], pick[rows, :], scale[...])
        dh = d_f[rows, :].astype(f32) + dx
        d_h2[rows, :] = dh
        low = dh.astype(bf16)
        d_att[rows, :] = low
        hold[rows, :] = dot(low, w[...], 1, 0).astype(bf16)
        for r in range(na):
            refs[r][rows, :] = hold[rows, pl.ds(pl.multiple_of((idx[0] ^ r) * hw, hw), hw)]
        both = both + jnp.concatenate([d_shift, d_scale], axis=1)

    @pl.when(i == 0)
    def _():
        sums[...] = both

    @pl.when(i > 0)
    def _():
        sums[...] += both


def out_bwd(net, idx, grad, hidden2, d_f, pick, scale, w):
    r, d = grad.shape
    rb = min(256, r)
    hw = d // net.na
    row = pl.BlockSpec((rb, d), lambda i, s: (i, 0))
    narrow = pl.BlockSpec((rb, LANES), lambda i, s: (i, 0))
    whole = lambda a: pl.BlockSpec(a.shape, lambda i, s: (0, 0))
    res = pl.pallas_call(
        out_bwd_kernel,
        grid_spec=pltpu.PrefetchScalarGridSpec(
            num_scalar_prefetch=1,
            grid=(r // rb,),
            in_specs=[row, row, row, narrow, whole(scale), whole(w)],
            out_specs=[row, row, pl.BlockSpec((8, 2 * d), lambda i, s: (0, 0))]
            + [pl.BlockSpec((rb, hw), lambda i, s: (i, 0))] * net.na,
            scratch_shapes=[pltpu.VMEM((rb, d), bf16)],
        ),
        out_shape=[shape((r, d), f32), shape((r, d), bf16), shape((8, 2 * d), f32)]
        + [shape((r, hw), bf16)] * net.na,
        compiler_params=params(),
        cost_estimate=cost(2 * r * d * d, 20 * r * d + 2 * d * d),
        name="out_bwd",
    )(idx, grad, hidden2, d_f, pick, scale, w)
    return res[0], res[1], res[2], res[3:]


def turn_back_kernel(idx, *refs, na):
    pieces = refs[:-3]
    cos, sin, d_qkv = refs[-3:]
    d = d_qkv.shape[1] // 3
    hw = d // na
    for part in range(3):
        first = 0
        for k, piece in enumerate(pieces):
            r = k % na
            wide = piece.shape[2]
            z = piece[part]
            if part < 2:
                z = turn(z.astype(f32), cos[...], sin[...], -1).astype(bf16)
            d_qkv[:, pl.ds(pl.multiple_of(part * d + (idx[0] ^ r) * hw + first, LANES), wide)] = z
            first += wide if r == na - 1 else 0


def turn_back(net, idx, pieces, cos, sin, d):
    r = cos.shape[0]
    rb = min(256, r)
    narrow = pl.BlockSpec((rb, LANES), lambda i, s: (i, 0))
    return pl.pallas_call(
        partial(turn_back_kernel, na=net.na),
        grid_spec=pltpu.PrefetchScalarGridSpec(
            num_scalar_prefetch=1,
            grid=(r // rb,),
            in_specs=[pl.BlockSpec((3, rb, p.shape[2]), lambda i, s: (0, i, 0)) for p in pieces] + [narrow, narrow],
            out_specs=pl.BlockSpec((rb, 3 * d), lambda i, s: (i, 0)),
        ),
        out_shape=shape((r, 3 * d), bf16),
        compiler_params=params(),
        cost_estimate=cost(12 * r * d, 12 * r * d),
        name="turn_back",
    )(idx, *pieces, cos, sin)


def qkv_bwd_kernel(d_qkv, hidden, d_h2, pick, scale, w, d_h, sums):
    i = pl.program_id(0)
    both = jnp.zeros(sums.shape, f32)
    for rows in parts_of(hidden.shape[0]):
        grad = dot(d_qkv[rows, :], w[...], 1, 0)
        dx, d_scale, d_shift = norm_back(hidden[rows, :].astype(f32), grad, pick[rows, :], scale[...])
        d_h[rows, :] = (d_h2[rows, :] + dx).astype(bf16)
        both = both + jnp.concatenate([d_shift, d_scale], axis=1)

    @pl.when(i == 0)
    def _():
        sums[...] = both

    @pl.when(i > 0)
    def _():
        sums[...] += both


def qkv_bwd(d_qkv, hidden, d_h2, pick, scale, w):
    r, d = hidden.shape
    rb = min(256, r)
    row = pl.BlockSpec((rb, d), lambda i: (i, 0))
    narrow = pl.BlockSpec((rb, LANES), lambda i: (i, 0))
    whole = lambda a: pl.BlockSpec(a.shape, lambda i: (0, 0))
    return pl.pallas_call(
        qkv_bwd_kernel,
        grid=(r // rb,),
        in_specs=[pl.BlockSpec((rb, 3 * d), lambda i: (i, 0)), row, row, narrow, whole(scale), whole(w)],
        out_specs=[row, pl.BlockSpec((8, 2 * d), lambda i: (0, 0))],
        out_shape=[shape((r, d), bf16), shape((8, 2 * d), f32)],
        compiler_params=params(),
        cost_estimate=cost(6 * r * d * d, 16 * r * d + 6 * d * d),
        name="qkv_bwd",
    )(d_qkv, hidden, d_h2, pick, scale, w)


def skip_bwd_kernel(idx, d_h, got0, got1, w, d_frames, d_skip):
    d = d_h.shape[1]
    g = chosen(idx, d_h, (got0, got1), slice(None))
    d_frames[...] = dot(g, w[:, :d], 1, 0)
    d_skip[...] = dot(g, w[:, d:], 1, 0)


def skip_bwd(idx, d_h, d_h_got, w):
    r, d = d_h.shape
    rb = min(256, r // 2)
    row = pl.BlockSpec((rb, d), lambda i, s: (i, 0))
    return pl.pallas_call(
        skip_bwd_kernel,
        grid_spec=pltpu.PrefetchScalarGridSpec(
            num_scalar_prefetch=1,
            grid=(r // rb,),
            in_specs=chosen_specs(rb, d, r // rb) + [pl.BlockSpec(w.shape, lambda i, s: (0, 0))],
            out_specs=[row, row],
        ),
        out_shape=[shape((r, d), f32)] * 2,
        compiler_params=params(),
        cost_estimate=cost(4 * r * d * d, 12 * r * d + 4 * d * d),
        name="skip_bwd",
    )(idx, d_h, *d_h_got, w)


def outer_kernel(idx, g, *refs, n, own, choose):
    xs = refs[:own]
    keep, send = refs[-2:]
    pairs = keep.shape[0]
    at = 0
    low = idx[1] & 1 == 0
    for k in range(0, own, 2 if choose else 1):
        x = jnp.where(idx[2] > 0, xs[k + 1][...], xs[k][...]) if choose else xs[k][...]
        width = x.shape[1]
        z = dot(g[...], x, 0, 0).astype(bf16).reshape(pairs, 2, n, width)
        keep[:, :, at : at + width] = jnp.where(low, z[:, 0], z[:, 1])
        send[:, :, at : at + width] = jnp.where(low, z[:, 1], z[:, 0])
        at += width


def outer(net, idx, g, xs, n, rows, first, into=None, choose=False):
    r, wide = g.shape
    per = max(1, 512 // (2 * n))
    while net.nf // 2 % per:
        per -= 1
    k = sum(x.shape[1] for x in xs) // (2 if choose else 1)
    out = pl.BlockSpec((per, n, k), lambda i, s: (i, first // n, 0))
    big = shape((net.nf // 2, rows, k), bf16)
    extra = list(into) if into is not None else []
    return pl.pallas_call(
        partial(outer_kernel, n=n, own=len(xs), choose=choose),
        grid_spec=pltpu.PrefetchScalarGridSpec(
            num_scalar_prefetch=1,
            grid=(wide // (2 * n * per),),
            in_specs=[pl.BlockSpec((r, 2 * n * per), lambda i, s: (0, i))]
            + [pl.BlockSpec(x.shape, lambda i, s: (0, 0)) for x in xs]
            + [pl.BlockSpec(memory_space=pl.ANY)] * len(extra),
            out_specs=[out, out],
        ),
        out_shape=[big, big],
        input_output_aliases={2 + len(xs) + i: i for i in range(len(extra))},
        compiler_params=params(),
        cost_estimate=cost(2 * r * wide * k, 2 * (r * wide + r * k + wide * k)),
        name="outer",
    )(idx, g, *xs, *extra)


def gelu_both(u):
    u2 = u * u
    t = jnp.tanh(GELU_C * u * (1.0 + 0.044715 * u2))
    half = 0.5 * (1.0 + t)
    return u * half, half + 0.5 * u * (1.0 - t * t) * (GELU_C * (1.0 + 3 * 0.044715 * u2))


def ffn_kernel(*refs, steps, second):
    x_ref, df_ref, o_in = refs[:3]
    at = 4 if second else 3
    ws = refs[at : at + steps]
    o_ref, dx_ref = refs[at + steps : at + steps + 2]
    gs = refs[at + steps + 2 : at + 2 * steps + 2]
    o_acc, dx_acc, o_low, wbuf, gbuf, sem_w, sem_g, sem_a = refs[at + 2 * steps + 2 :]
    s = pl.program_id(0)
    slot = lax.rem(s, 2)
    w_in = [pltpu.make_async_copy(ws[k], wbuf.at[k % 2], sem_w.at[k]) for k in range(steps)]
    g_out = [pltpu.make_async_copy(gbuf.at[k % 2], gs[k], sem_g.at[k]) for k in range(steps)]
    sums = [pltpu.make_async_copy(o_in, o_acc, sem_a.at[0])]
    if second:
        sums.append(pltpu.make_async_copy(refs[3], dx_acc, sem_a.at[1]))
    ends = [
        pltpu.make_async_copy(o_low if second else o_acc, o_ref, sem_a.at[2]),
        pltpu.make_async_copy(dx_acc, dx_ref, sem_a.at[3]),
    ]

    @pl.when(s == 0)
    def _():
        w_in[0].start()
        for c in sums:
            c.start()
        if not second:
            dx_acc[...] = jnp.zeros_like(dx_acc)

    for k in range(steps):

        @pl.when(s == k)
        def _():
            if k + 1 < steps:
                w_in[k + 1].start()
            w_in[k].wait()

    d = x_ref.shape[1]
    wu = wbuf[slot, :, 0].reshape(-1, d)
    wd = wbuf[slot, :, 1].reshape(-1, d)
    x, df = x_ref[...], df_ref[...]
    g, dg = gelu_both(dot(x, wu, 1, 1))
    act = g.astype(bf16)
    du = (dot(df, wd, 1, 1) * dg).astype(bf16)

    @pl.when(s == 0)
    def _():
        for c in sums:
            c.wait()

    o_acc[...] += dot(act, wd, 1, 0)
    dx_acc[...] += dot(du, wu, 1, 0)
    for k in range(2, steps):

        @pl.when(s == k)
        def _():
            g_out[k - 2].wait()

    part = gbuf.shape[1:2] + gbuf.shape[3:]
    gbuf[slot, :, 1] = dot(act, df, 0, 0).astype(bf16).reshape(part)
    gbuf[slot, :, 0] = dot(du, x, 0, 0).astype(bf16).reshape(part)
    for k in range(steps):

        @pl.when(s == k)
        def _():
            g_out[k].start()

    @pl.when(s == steps - 1)
    def _():
        if second:
            o_low[...] = o_acc[...].astype(bf16)
        for c in ends:
            c.start()
        for k in range(max(0, steps - 2), steps):
            g_out[k].wait()
        for c in ends:
            c.wait()


def ffn(x, df, o_in, pieces, dx_in=None):
    second = dx_in is not None
    r, d = x.shape
    steps = len(pieces)
    full = pl.BlockSpec((r, d), lambda s: (0, 0), pipeline_mode=pl.Buffered(1))
    far = pl.BlockSpec(memory_space=pl.ANY)
    args = [x, df, o_in] + ([dx_in] if second else []) + list(pieces)
    piece = shape(pieces[0].shape, bf16)
    units = piece.shape[0] * piece.shape[2]
    return pl.pallas_call(
        partial(ffn_kernel, steps=steps, second=second),
        grid=(steps,),
        in_specs=[full, full] + [far] * (len(args) - 2),
        out_specs=[far] * (steps + 2),
        out_shape=[shape((r, d), bf16 if second else f32), shape((r, d), f32)] + [piece] * steps,
        scratch_shapes=[
            pltpu.VMEM((r, d), f32),
            pltpu.VMEM((r, d), f32),
            pltpu.VMEM((r, d) if second else (16, LANES), bf16),
            pltpu.VMEM((2, *piece.shape), bf16),
            pltpu.VMEM((2, *piece.shape), bf16),
            pltpu.SemaphoreType.DMA((steps,)),
            pltpu.SemaphoreType.DMA((steps,)),
            pltpu.SemaphoreType.DMA((4,)),
        ],
        compiler_params=params(),
        cost_estimate=cost(12 * r * d * steps * units, 16 * r * d + 8 * steps * units * d, steps * units * r),
        name="ffn",
    )(*args)


def head_sel(h):
    lane = lax.broadcasted_iota(jnp.int32, (1, LANES), 1)
    return lane < HD if h == 0 else lane >= HD


def load_rolled(idx, hold, refs, part, rest):
    rows = refs[0].shape[-2]
    t = rows * len(refs)
    for r, ref in enumerate(refs):
        x = ref[part] if part is not None else ref[...]
        hold[pl.ds(pl.multiple_of((idx[0] ^ r) * rows, rows), rows), :] = x.astype(f32)
    hold[t : t + rest, :] = hold[0:rest, :]
    return hold[pl.ds(idx[1], t), :]


def store_unrolled(idx, hold, t, rest):
    row = lax.broadcasted_iota(jnp.int32, (rest, 1), 0)
    hold[0:rest, :] = jnp.where(row < idx[1], hold[t : t + rest, :], hold[0:rest, :])


def attn_fwd_kernel(idx, *refs, na, long):
    pieces = refs[:na]
    segr, segc = refs[na : na + 2]
    outs = refs[na + 2 : 2 * na + 2]
    lse_ref, hold, ql, kl, vt = refs[2 * na + 2 :]
    rows = outs[0].shape[0]
    t = rows * na
    rest = t - long
    ql[...] = load_rolled(idx, hold, pieces, 0, rest).astype(bf16)
    kl[...] = load_rolled(idx, hold, pieces, 1, rest).astype(bf16)
    vt[...] = jnp.transpose(load_rolled(idx, hold, pieces, 2, rest)).astype(bf16)

    def pair(r0, n, c0, cn, mask):
        q = ql[pl.ds(r0, n), :]
        k = kl[c0 : c0 + cn, :]
        got, lses = [], []
        for h in range(2):
            qh = jnp.where(head_sel(h), q, jnp.zeros_like(q))
            s = dot(k, qh, 1, 1)
            if mask is not None:
                s = jnp.where(mask, s, NEG)
            top = jnp.max(s, axis=0, keepdims=True)
            p = jnp.exp(s - top)
            total = jnp.sum(p, axis=0, keepdims=True)
            got.append(dot(vt[HD * h : HD * h + HD, c0 : c0 + cn], p.astype(bf16), 1, 0) / total)
            lses.append(top + jnp.log(total))
        lse_ref[0, :, pl.ds(r0, n)] = jnp.concatenate(lses, axis=0)
        hold[pl.ds(idx[1] + r0, n), :] = jnp.transpose(jnp.concatenate(got, axis=0))

    step = long // 2
    for i in range(2):
        pair(i * step, step, 0, long, None)
    pair(long, rest, long, rest, segc[:, :1] == segr[:1, :])
    store_unrolled(idx, hold, t, rest)
    for r in range(na):
        outs[r][...] = hold[pl.ds(pl.multiple_of((idx[0] ^ r) * rows, rows), rows), :].astype(bf16)


def attn_fwd(net, idx, pieces, segr, segc, long):
    na = net.na
    _, rows, hw = pieces[0].shape
    t = rows * na
    rest = t - long
    pairs = hw // LANES
    const = lambda a: pl.BlockSpec(a.shape, lambda j, s: (0, 0))
    work = pairs * 2 * (long * long + rest * rest)
    res = pl.pallas_call(
        partial(attn_fwd_kernel, na=na, long=long),
        grid_spec=pltpu.PrefetchScalarGridSpec(
            num_scalar_prefetch=1,
            grid=(pairs,),
            in_specs=[pl.BlockSpec((3, rows, LANES), lambda j, s: (0, 0, j))] * na + [const(segr), const(segc)],
            out_specs=[pl.BlockSpec((rows, LANES), lambda j, s: (0, j))] * na
            + [pl.BlockSpec((1, 2, t), lambda j, s: (j, 0, 0))],
            scratch_shapes=[
                pltpu.VMEM((t + rest, LANES), f32),
                pltpu.VMEM((t, LANES), bf16),
                pltpu.VMEM((t, LANES), bf16),
                pltpu.VMEM((LANES, t), bf16),
            ],
        ),
        out_shape=[shape((rows, hw), bf16)] * na + [shape((pairs, 2, t), f32)],
        compiler_params=params(),
        cost_estimate=cost(16 * HD * work, 8 * t * hw, work),
        name="attn_fwd",
    )(idx, *pieces, segr, segc)
    return res[:na], res[na]


def attn_bwd_kernel(idx, *refs, na, long):
    pieces, d_pieces = refs[:na], refs[na : 2 * na]
    lse_ref, segr, segc = refs[2 * na : 2 * na + 3]
    outs = refs[2 * na + 3 : 3 * na + 3]
    hold, ql, kl, vl, dl, kt, dqt, dka, dva = refs[3 * na + 3 :]
    rows = outs[0].shape[1]
    t = rows * na
    rest = t - long
    ql[...] = load_rolled(idx, hold, pieces, 0, rest).astype(bf16)
    kf = load_rolled(idx, hold, pieces, 1, rest)
    kl[...] = kf.astype(bf16)
    kt[...] = jnp.transpose(kf).astype(bf16)
    vl[...] = load_rolled(idx, hold, pieces, 2, rest).astype(bf16)
    dl[...] = load_rolled(idx, hold, d_pieces, None, rest).astype(bf16)
    dka[...] = jnp.zeros_like(dka)
    dva[...] = jnp.zeros_like(dva)

    def pair(r0, n, c0, cn, mask):
        q, do = ql[pl.ds(r0, n), :], dl[pl.ds(r0, n), :]
        k, v = kl[c0 : c0 + cn, :], vl[c0 : c0 + cn, :]
        dqs = []
        for h in range(2):
            qh = jnp.where(head_sel(h), q, jnp.zeros_like(q))
            dh = jnp.where(head_sel(h), do, jnp.zeros_like(do))
            s = dot(k, qh, 1, 1)
            if mask is not None:
                s = jnp.where(mask, s, NEG)
            p = jnp.exp(s - lse_ref[0, h : h + 1, pl.ds(r0, n)])
            dp = dot(v, dh, 1, 1)
            delta = jnp.sum(p * dp, axis=0, keepdims=True)
            ds = (p * (dp - delta)).astype(bf16)
            dqs.append(dot(kt[HD * h : HD * h + HD, c0 : c0 + cn], ds, 1, 0))
            dva[c0 : c0 + cn, :] += dot(p.astype(bf16), dh, 1, 0)
            dka[c0 : c0 + cn, :] += dot(ds, qh, 1, 0)
        dqt[pl.ds(r0, n), :] = jnp.transpose(jnp.concatenate(dqs, axis=0))

    step = long // 2

    def body(i, carry):
        pair(pl.multiple_of(i * step, step), step, 0, long, None)
        return carry

    lax.fori_loop(0, 2, body, 0)
    pair(long, rest, long, rest, segc[:, :1] == segr[:1, :])
    for part, src in enumerate((dqt, dka, dva)):
        x = src[...]
        if part == 0:
            x = x * (1.0 / math.sqrt(HD))
        hold[pl.ds(idx[1], t), :] = x
        store_unrolled(idx, hold, t, rest)
        for r in range(na):
            at = pl.multiple_of((idx[0] ^ r) * rows, rows)
            outs[r][part] = hold[pl.ds(at, rows), :].astype(bf16)


def attn_bwd(net, idx, pieces, d_pieces, lse, segr, segc, long, start, pairs):
    na = net.na
    rows = pieces[0].shape[1]
    t = rows * na
    rest = t - long
    hw = pairs * LANES
    const = lambda a: pl.BlockSpec(a.shape, lambda j, s: (0, 0))
    three = pl.BlockSpec((3, rows, LANES), lambda j, s: (0, 0, j + start))
    out = pl.BlockSpec((3, rows, LANES), lambda j, s: (0, 0, j))
    work = pairs * 2 * (long * long + rest * rest)
    return pl.pallas_call(
        partial(attn_bwd_kernel, na=na, long=long),
        grid_spec=pltpu.PrefetchScalarGridSpec(
            num_scalar_prefetch=1,
            grid=(pairs,),
            in_specs=[three] * na
            + [pl.BlockSpec((rows, LANES), lambda j, s: (0, j + start))] * na
            + [pl.BlockSpec((1, 2, t), lambda j, s: (j + start, 0, 0)), const(segr), const(segc)],
            out_specs=[out] * na,
            scratch_shapes=[pltpu.VMEM((t + rest, LANES), f32)]
            + [pltpu.VMEM((t, LANES), bf16)] * 4
            + [pltpu.VMEM((LANES, t), bf16)]
            + [pltpu.VMEM((t, LANES), f32)] * 3,
        ),
        out_shape=[shape((3, rows, hw), bf16)] * na,
        compiler_params=params(),
        cost_estimate=cost(40 * HD * work, 16 * t * hw, work),
        name="attn_bwd",
    )(idx, *pieces, *d_pieces, lse, segr, segc)


def prep_kernel(ints, me, w_mod, cos, sin, pick, segr, segc, smooth, part, idx, gs, *, nd, utt, long, regroup, bits):
    nf = ints.shape[0]
    rows, rest = cos.shape[0], segr.shape[1]
    total = rows * (2 if regroup else nd)
    y, f, block = me[0], me[1], me[3]

    def slot(g):
        r = g ^ f
        return sum(((r >> b) & 1) << j for j, b in enumerate(bits))

    mine = slot((f & ~1) | y if regroup else f)
    starts, ends, at, first = [], [], 0, 0
    for u in range(utt):
        size = ints[mine, u]
        starts.append(at)
        first = jnp.where(size == long, at, first)
        at = at + size
        ends.append(at)
    idx[0], idx[1], idx[2] = block, first, me[2]
    kept = 0
    for g in range(nf):
        for u in range(utt):
            kept = kept + (1 - ints[g, utt + u])
    gs[0] = (nf * utt) / jnp.maximum(kept.astype(f32), 1.0)

    pos = block * rows + lax.broadcasted_iota(jnp.int32, (rows, LANES), 0)
    lane = lax.broadcasted_iota(jnp.int32, (rows, LANES), 1)
    offset = jnp.zeros((rows, LANES), jnp.int32)
    number = jnp.zeros((rows, LANES), jnp.int32)
    for u in range(1, utt):
        past = pos >= starts[u]
        offset = jnp.where(past, starts[u], offset)
        number = jnp.where(past, u, number)
    pick[...] = jnp.where((lane % utt == number) & (lane < 3 * utt), 1.0, 0.0).astype(bf16)
    half = HD // 2
    frequency = jnp.exp((lane[:1] % half).astype(f32) * (-math.log(10000.0) / half))
    angles = (pos - offset).astype(f32) * frequency
    cos[...] = jnp.cos(angles)
    sin[...] = jnp.where(lane[:1] % HD < half, -1.0, 1.0) * jnp.sin(angles)

    for ref, axis in ((segr, 1), (segc, 0)):
        p = first + long + lax.broadcasted_iota(jnp.int32, ref.shape, axis)
        p = jnp.where(p >= total, p - total, p)
        number = jnp.zeros(ref.shape, jnp.int32)
        for u in range(1, utt):
            number = jnp.where(p >= starts[u], u, number)
        ref[...] = number

    n, wide = smooth.shape
    d = wide * nd
    row = lax.broadcasted_iota(jnp.int32, (n, LANES), 0)
    when = jnp.zeros((n, LANES), jnp.int32)
    slots = [slot(g) for g in range(nf)]
    for j in range(n):
        k, u = divmod(j, utt)
        g = 2 * (k % (nf // 2)) + k // (nf // 2) if regroup else k
        when = jnp.where(row == j, ints[slots[g], 2 * utt + u], when)
    flow = 1000.0 * (when[:, :1].astype(f32) / STEPS)
    col = y * wide + lax.broadcasted_iota(jnp.int32, (1, wide), 1)
    low = col < d // 2
    at = jnp.where(low, col, col - d // 2).astype(f32)
    angles = flow * jnp.exp(at * (-math.log(10000.0) / (d // 2)))
    e = jnp.where(low, jnp.sin(angles), jnp.cos(angles))
    e = (e / (1.0 + jnp.exp(-e))).astype(bf16)
    smooth[...] = e
    part[...] = dot(e, w_mod[...], 1, 0)


def prep(net, ints, me, w_mod, rows, long, rest):
    utt = ints.shape[1] // 3
    n = net.nf * utt
    smem = pl.BlockSpec(memory_space=pltpu.SMEM)
    vmem = pl.BlockSpec(memory_space=pltpu.VMEM)
    return pl.pallas_call(
        partial(prep_kernel, nd=net.nd, utt=utt, long=long, regroup=net.regroup, bits=tuple(net.int_bits)),
        in_specs=[smem, smem, vmem],
        out_specs=[vmem] * 7 + [smem, smem],
        out_shape=[
            shape((rows, LANES), f32),
            shape((rows, LANES), f32),
            shape((rows, LANES), bf16),
            shape((8, rest), jnp.int32),
            shape((rest, LANES), jnp.int32),
            shape((n, w_mod.shape[0]), bf16),
            shape((n, w_mod.shape[1]), f32),
            shape((3,), jnp.int32),
            shape((1,), f32),
        ],
        compiler_params=params(32),
        cost_estimate=cost(2 * n * w_mod.size, 16 * rows * LANES, 4 * n * w_mod.shape[0]),
        name="prep",
    )(ints, me, w_mod)


def terms_kernel(*refs):
    out = refs[-1]
    x = refs[0][...]
    for ref in refs[1:-1]:
        x = x + ref[...]
    a = x.astype(bf16)
    b = (x - a.astype(f32)).astype(bf16)
    c = (x - a.astype(f32) - b.astype(f32)).astype(bf16)
    n = x.shape[0]
    out[...] = jnp.zeros_like(out)
    out[0 : 3 * n, :] = jnp.concatenate([a.astype(f32), b.astype(f32), c.astype(f32)], axis=0).astype(bf16)


def three_terms(*xs):
    return pl.pallas_call(
        terms_kernel,
        out_shape=shape((LANES, xs[0].shape[1]), bf16),
        compiler_params=params(16),
        cost_estimate=cost(0, 300 * xs[0].shape[1]),
        name="three_terms",
    )(*xs)


def scale_kernel(gs, x, out):
    out[...] = (x[...].astype(f32) * gs[0]).astype(bf16)


def scaled(x, gs):
    r, d = x.shape
    rb = min(256, r)
    row = pl.BlockSpec((rb, d), lambda i, s: (i, 0))
    return pl.pallas_call(
        scale_kernel,
        grid_spec=pltpu.PrefetchScalarGridSpec(num_scalar_prefetch=1, grid=(r // rb,), in_specs=[row], out_specs=row),
        out_shape=shape((r, d), bf16),
        compiler_params=params(16),
        cost_estimate=cost(r * d, 4 * r * d),
        name="scaled",
    )(gs, x)


def to_units(net, turned, w_down, y, f):
    nd, nf = net.nd, net.nf
    units = w_down.shape[0] // nf
    down = lax.all_to_all(w_down, "fsdp", split_axis=0, concat_axis=1, tiled=True)
    got = []
    for j in range(nd):
        perm = [(a * nf + b, nd * b + (a + j) % nd) for a in range(nd) for b in range(nf)]
        send = lax.dynamic_slice_in_dim(turned, (y + j) % nd * units, units, 0)
        got.append(move(net, send, perm, y, f))
    return got, down


def mix_kernel(idx, *refs, half, nd):
    ups, down, out = refs[:nd], refs[nd], refs[nd + 1]
    units, width = ups[0].shape
    own = lax.rem(idx[0], nd)
    for j, up in enumerate(ups):
        col = pl.multiple_of(lax.rem(own + nd - j, nd) * width, width)
        for at in range(0, units, half):
            out[2 * at : 2 * at + half, pl.ds(col, width)] = up[at : at + half, :]
    for at in range(0, units, half):
        out[2 * at + half : 2 * at + 2 * half, :] = down[at : at + half, :]


def own_units(net, ups, down, half, y, f):
    whole = pl.BlockSpec(memory_space=pltpu.VMEM)
    return pl.pallas_call(
        partial(mix_kernel, half=half, nd=net.nd),
        in_specs=[pl.BlockSpec(memory_space=pltpu.SMEM)] + [whole] * (net.nd + 1),
        out_specs=whole,
        out_shape=shape((2 * down.shape[0], down.shape[1]), bf16),
        compiler_params=params(16),
        cost_estimate=cost(0, 8 * down.size),
        name="own_units",
    )(jnp.stack([y * net.nf + f]).astype(jnp.int32), *ups, down)


def from_units(net, g_up, g_down, y, f):
    nd, nf = net.nd, net.nf
    grad_down = lax.all_to_all(g_down, "fsdp", split_axis=1, concat_axis=0, tiled=True)
    width = g_up.shape[1] // nd
    own = (y * nf + f) % nd
    got = []
    for j in range(nd):
        perm = [(nd * b + (a + j) % nd, a * nf + b) for a in range(nd) for b in range(nf)]
        send = lax.dynamic_slice_in_dim(g_up, (own - j) % nd * width, width, 1)
        got.append(move(net, send, perm, y, f))
    got = jnp.stack(got)
    rows = [lax.dynamic_index_in_dim(got, (h - y) % nd, 0, keepdims=False) for h in range(nd)]
    return jnp.concatenate(rows, axis=0).T.astype(f32), grad_down.astype(f32)


def move(net, x, perm, y, f):
    fixed = [a for a, b in perm if a == b]
    got = lax.ppermute(x, ("dp", "fsdp"), [(a, b) for a, b in perm if a != b])
    me = y * net.nf + f
    stays = False
    for a in fixed:
        stays = stays | (me == a)
    return jnp.where(stays, x, got) if fixed else got


def local(net, frames, skip_in, cond_in, lengths, drop_mask, time_index, w_skip, w_qkv, w_out, w_up, w_down, w_mod, d_out):
    frames, skip_in, cond_in, d_out = frames[0], skip_in[0], cond_in[0], d_out[0]
    rows, d = frames.shape
    nd, nf, na = net.nd, net.nf, net.na
    y, f = lax.axis_index("dp"), lax.axis_index("fsdp")
    utt = lengths.shape[1]
    group_len = rows * nd
    long = int(group_len * LONG_PART)
    rest = group_len - long
    core_bit = ("fsdp", 1)
    n_skip, n_qkv, n_out = w_skip.shape[1], w_qkv.shape[1], w_out.shape[1]
    part_of = lambda n, share: int(n * share) // 16 * 16
    block = net.attn_index()
    moved = ((f & 1) != y if net.regroup else y < 0).astype(jnp.int32)
    me = jnp.stack([y, f, moved, block]).astype(jnp.int32)
    cut = rows // 2
    cols = w_mod.shape[1]

    skip_turned, qkv_turned, out_turned, up_turned = flip(w_skip, w_qkv, w_out, w_up)
    g2 = Gather(net, jnp.concatenate([qkv_turned, out_turned], axis=0), part_of(n_qkv + n_out, 0.33))
    lens = jnp.concatenate([lengths, drop_mask], axis=0)
    ints = jnp.concatenate([lengths, drop_mask, time_index], axis=1)
    bits = net.int_bits[:]

    def more_ints():
        nonlocal ints
        if bits:
            ints = jnp.concatenate([ints, net.swap(ints, ("fsdp", 1 << bits.pop(0)))], axis=0)

    def step(g):
        if g.done < g.common:
            g.join()

    def start(g):
        if g.done < g.common:
            g.send()
        else:
            g.raw = []

    g1 = Gather(net, skip_turned, part_of(n_skip, 0.5))
    while g1.done < g1.common:
        g1.send()
        more_ints()
        g1.raw, (ints, lens, up_turned, w_down), g2.x = tie(g1.raw, [ints, lens, up_turned, w_down], g2.x)
        g1.join()
    g1.send()
    start(g2)
    while bits:
        more_ints()
    g1.raw, g2.raw, (ints, up_turned, w_down) = tie(g1.raw, g2.raw, [ints, up_turned, w_down])
    g1.join()
    step(g2)
    g1.send()
    start(g2)
    up_parts, down = to_units(net, up_turned, w_down, y, f)
    cos, sin, pick, segr, segc, smooth, part, idx, gs = prep(net, ints, me, w_mod, rows, long, rest)
    if net.regroup:
        part = part.reshape(2, nf // 2, utt, cols)
        mod_got = net.swap(lax.dynamic_index_in_dim(part, 1 - y, 0, keepdims=False), ("dp", 1))
        part = lax.dynamic_index_in_dim(part, y, 0, keepdims=False)
    else:
        for b in range(net.db):
            part = part + net.swap(part, ("dp", 1 << b))
        mod_got = part
    g1.raw, g2.raw, (ints, part, mod_got, down) = tie(g1.raw, g2.raw, [ints, part, mod_got, down])
    g1.join()
    theirs = g1.core(g1.x + g1.far)
    step(g2)
    g2.finish_common()
    g2.send()
    skip_t, = place(net, me, g1, theirs, [n_skip])
    (skip_t, lens, part, mod_got, down), up_parts = tie([skip_t, lens, part, mod_got, down], up_parts)
    units = down.shape[0]
    half = units // 2 if units // 2 % 16 == 0 else units
    g3 = Gather(net, own_units(net, up_parts, down, half, y, f), units * 2 if half == units else units)
    start(g3)
    hidden0, mixed = skip_fwd(me, lens, frames, skip_in, cond_in, skip_t)
    (hidden0, mixed, part, mod_got), g2.raw = tie([hidden0, mixed, part, mod_got], g2.raw)

    hidden_got = [net.trade(hidden0)]
    g2.join()
    g2.send()
    if net.regroup:
        part = jnp.broadcast_to((part + mod_got)[:, None], (nf // 2, 2, utt, cols))
    part = part.reshape(nf, utt, cols)
    mod = lax.all_to_all(part, "fsdp", split_axis=0, concat_axis=2, tiled=True)
    (hidden0, mod, d_out), g2.raw, g3.raw = tie([hidden0, mod, d_out], g2.raw, g3.raw)
    mods = three_terms(mod.reshape(utt, nf * cols))
    mod_a, mod_f = mods[:, : 2 * d], mods[:, 2 * d :]
    g2.join()
    theirs = g2.core(g2.x + g2.far)
    qkv_t, out_t = place(net, me, g2, theirs, [n_qkv, n_out])
    step(g3)
    (hidden0, qkv_t, out_t, d_out, mod_a, mod_f), hidden_got, g3.x = tie([hidden0, qkv_t, out_t, d_out, mod_a, mod_f], hidden_got, g3.x)

    start(g3)
    d_f0 = scaled(d_out, gs)
    d_f_got = [net.trade(d_f0[:cut])]
    hidden, normed_a, sent = qkv_fwd(net, idx, hidden0, hidden_got[0], pick, mod_a, qkv_t, cos, sin)
    sent, g3.raw, d_f_got, (d_f0,) = tie(list(sent), g3.raw, d_f_got, [d_f0])
    step(g3)
    g3.finish_common()
    pieces = [sent[0]] + [net.attn_swap(sent[r], r) for r in range(1, na)]
    pieces, (d_f0,), g3.x = tie(pieces, [d_f0], g3.x)
    g3.send()
    d_f_got.append(net.trade(d_f0[cut:]))
    attn_p, lse = attn_fwd(net, idx, pieces, segr, segc, long)
    (lse,), d_f_got, attn_p, g3.raw = tie([lse], d_f_got, list(attn_p), g3.raw)
    attn_p = [attn_p[0]] + [net.attn_swap(attn_p[r], r) for r in range(1, na)]
    g3.join()
    attn_p, near = tie(attn_p, g3.x)
    g3.send()
    near_core = g3.core(near)
    attn, hidden2, normed_f, d_f = out_fwd(net, idx, attn_p, hidden, pick, mod_f, out_t, d_f0, d_f_got)

    view = lambda x: x.reshape(x.shape[0], 2, x.shape[1] // 2, x.shape[2])
    acc, dx, *got1 = ffn(normed_f, d_f, hidden2, [view(x) for x in near_core + near])
    (acc, dx, mixed, skip_in), far, got1 = tie([acc, dx, mixed, skip_in], g3.raw, got1)
    far_core = g3.core(far)
    count = len(far)
    far_core, got1, (mixed, skip_in) = tie(far_core, got1, [mixed, skip_in])
    mixed_got, skip_got = net.trade(mixed), net.trade(skip_in)
    swapped1 = [net.swap(x, core_bit) for x in got1[:count]]
    out_b, dx, *got2 = ffn(normed_f, d_f, acc, [view(x) for x in far_core + far], dx)
    (out_b, dx, mixed_got), got2, swapped1 = tie([out_b, dx, mixed_got], got2, swapped1)
    swapped2 = [net.swap(x, core_bit) for x in got2[:count]]

    d_h2, d_att, sums_f, d_attn_p = out_bwd(net, idx, dx, hidden2, d_f, pick, mod_f[:, d:], out_t)
    (d_h2, d_att, skip_got), d_attn_p, swapped2 = tie([d_h2, d_att, skip_got], list(d_attn_p), swapped2)
    d_attn_p = [d_attn_p[0]] + [net.attn_swap(d_attn_p[r], r) for r in range(1, na)]
    sum_far = [plus(a, b) for a, b in zip(got2[count:], swapped2)]
    d_attn_p, sum_far, (d_att,) = tie(d_attn_p, sum_far, [d_att])
    came = [net.swap(x, o[-2]) for x, o in zip(sum_far, g3.orders)]
    into = outer(net, me, d_att, [attn], n_out, n_qkv + n_out, n_qkv)
    d_attn_p, into, (out_b,) = tie(d_attn_p, list(into), [out_b])

    def send_half(xs, bits):
        n = xs[0].shape[0] // 2
        return [x[:n] for x in xs], [net.swap(x[n:], b) for x, b in zip(xs, bits)]

    all_pairs = d // na // LANES
    pairs = max(1, all_pairs // 2)
    d_sent = attn_bwd(net, idx, pieces, d_attn_p, lse, segr, segc, long, 0, pairs)
    d_sent, came, d_attn_p = tie(list(d_sent), came, d_attn_p)
    d_pieces = [d_sent[0]] + [net.attn_swap(d_sent[r], r) for r in range(1, na)]
    ff = [plus(a, b, c) for a, b, c in zip(got1[count:], swapped1, came)]
    d_attn_p, ff, (out_b,) = tie(d_attn_p, ff, [out_b])
    kept, raw = send_half(ff, [o[-3] for o in g3.orders])
    output_got = net.trade(out_b)
    if all_pairs > pairs:
        d_sent = attn_bwd(net, idx, pieces, d_attn_p, lse, segr, segc, long, pairs, all_pairs - pairs)
        d_sent, (output_got,), raw, d_pieces = tie(list(d_sent), [output_got], raw, d_pieces)
        d_pieces += [d_sent[0]] + [net.attn_swap(d_sent[r], r) for r in range(1, na)]
    ff = jnp.stack([plus(a, b) for a, b in zip(kept, raw)], axis=1)
    common = list(reversed(g3.orders[0][:-3]))
    d_pieces, (ff,) = tie(d_pieces, [ff])
    raw = []
    if common:
        kept, raw = send_half([ff], [common[0]])
    d_qkv = turn_back(net, idx, d_pieces, cos, sin, d)
    d_h, sums_a = qkv_bwd(d_qkv, hidden, d_h2, pick, mod_a[:, d:], qkv_t)
    (d_h, sums_a, d_qkv, output_got), raw = tie([d_h, sums_a, d_qkv, output_got], raw)
    if common:
        ff = plus(kept[0], raw[0])
    raw = []
    if len(common) > 1:
        kept, raw = send_half([ff], [common[1]])
    keep1, send1 = outer(net, me, d_h, [mixed, mixed_got, skip_in, skip_got], n_skip, n_skip, 0, choose=True)
    (keep1, send1, d_qkv, d_h), = tie([keep1, send1, d_qkv, d_h])
    got1 = net.swap(send1, core_bit)
    keep2, send2 = outer(net, me, d_qkv, [normed_a], n_qkv, n_qkv + n_out, 0, into)
    (keep2, send2, keep1, got1), = tie([keep2, send2, keep1, got1])
    got2 = net.swap(send2, core_bit)
    s1 = Sum(net, plus(keep1, got1))
    s1.send()
    (keep2, got2), = tie([keep2, got2])
    s2 = Sum(net, plus(keep2, got2))
    (s2.parts[0][0], s2.parts[1][0], sums_a, d_h, out_b), s1.raw = tie(
        [s2.parts[0][0], s2.parts[1][0], sums_a, d_h, out_b], s1.raw
    )
    s2.send()
    s1.join()
    s1.send()
    s1.raw, raw, (out_b, d_h) = tie(s1.raw, raw, [out_b, d_h])
    if len(common) > 1:
        ff = plus(kept[0], raw[0])
    for bit in common[2:]:
        kept, raw = send_half([ff], [bit])
        ff = plus(kept[0], raw[0])
    ff = ff.reshape(-1, 2, half, d)
    s1.join()
    s1.send()
    output = net.traded(out_b, output_got)
    grad_up, grad_down = from_units(net, ff[:, 0].reshape(units, d), ff[:, 1].reshape(units, d), y, f)
    s1.raw, s2.raw, (sums_a, output, grad_up, grad_down, d_h) = tie(s1.raw, s2.raw, [sums_a, output, grad_up, grad_down, d_h])
    d_h_got = [net.trade(d_h[:cut])]
    s2.join()
    s2.send()
    s1.join()
    if s1.left:
        s1.send()

    d_mod = jnp.concatenate([sums_a, sums_f], axis=1).reshape(utt, nf, cols).transpose(1, 0, 2)
    d_mod = lax.all_to_all(d_mod, "fsdp", split_axis=0, concat_axis=0, tiled=True)
    s1.raw, s2.raw, (d_mod, d_h), d_h_got = tie(s1.raw, s2.raw, [d_mod, d_h], d_h_got)
    d_h_got.append(net.trade(d_h[cut:]))
    if net.regroup:
        pair_sum = d_mod.reshape(nf // 2, 2, utt, cols).sum(axis=1)
        here = (jnp.arange(2) == y).astype(f32)
        d_mod = pair_sum[None] * here[:, None, None, None]
    d_mod = d_mod.reshape(nf * utt, cols)
    for b in range(net.db):
        d_mod = d_mod + net.swap(d_mod, ("dp", 1 << b))
    while s2.left:
        s2.join()
        if s1.left:
            s1.join()
        if s2.left:
            s2.send()
        if s1.left:
            s1.send()
        if s1.left and s2.left:
            s1.raw, s2.raw, d_h_got = tie(s1.raw, s2.raw, d_h_got)
        elif s2.left == 2:
            s2.raw, d_h_got = tie(s2.raw, d_h_got)
    d_frames, d_skip = skip_bwd(me, d_h, d_h_got, skip_t)
    g_two = s2.finish()
    grad_qkv = g_two[:n_qkv].T.astype(f32)
    grad_out = g_two[n_qkv:].T.astype(f32)
    grad_skip = s1.finish().T.astype(f32)
    grad_mod = jnp.dot(smooth.astype(f32).T, d_mod, precision=highest)

    return (output[None], d_frames[None], d_skip[None], grad_skip, grad_qkv, grad_out, grad_up, grad_down, grad_mod)


def solution(mesh):
    rows = P("fsdp", "dp", None)
    ints = P("fsdp", None)
    weight = P("dp", "fsdp")
    return jax.shard_map(
        partial(local, Net(mesh)),
        mesh=mesh,
        in_specs=(rows, rows, rows, ints, ints, ints, *([weight] * 6), rows),
        out_specs=(rows, rows, rows, *([weight] * 6)),
        check_vma=False,
    )
```

```python
from functools import partial
import math

import jax
import jax.numpy as jnp
from jax import lax
from jax.experimental import pallas as pl
from jax.experimental.pallas import tpu as pltpu
from jax.sharding import PartitionSpec as P

HD = 64
LANES = 128
STEPS = 1000
LONG_PART = 0.75
NEG = -1e30
GELU_C = math.sqrt(2.0 / math.pi)
VMEM_MIB = 60

bf16 = jnp.bfloat16
f32 = jnp.float32
highest = lax.Precision.HIGHEST
epsilon = 1e-06


def dot(a, b, ca, cb):
    return lax.dot_general(a, b, (((ca,), (cb,)), ((), ())), preferred_element_type=f32)


def params(mib=VMEM_MIB):
    return pltpu.CompilerParams(vmem_limit_bytes=mib * 2**20)


def cost(flops, nbytes, trans=0):
    return pl.CostEstimate(flops=int(flops), bytes_accessed=int(nbytes), transcendentals=int(trans))


def shape(dims, dtype):
    return jax.ShapeDtypeStruct(dims, dtype)


class Net:
    def __init__(self, mesh):
        self.nd = mesh.shape["dp"]
        self.nf = mesh.shape["fsdp"]
        self.fb = self.nf.bit_length() - 1
        self.db = self.nd.bit_length() - 1
        common = [("fsdp", 1 << b) for b in range(self.fb - 1, 1, -1)]
        common += [("dp", 1 << b) for b in range(self.db - 1, 0, -1)]
        x, y, core = ("fsdp", 2), ("dp", 1), ("fsdp", 1)
        self.orders = (common + [x, y, core], common + [y, x, core])
        self.regroup = self.nd == 2
        self.int_bits = [*range(2, self.fb), 0, 1]
        self.na = 2 if self.regroup else self.nd

    def swap(self, x, bit):
        axis, mask = bit
        size = self.nf if axis == "fsdp" else self.nd
        return lax.ppermute(x, axis, [(i, i ^ mask) for i in range(size)])

    def attn_swap(self, x, r):
        return self.swap(x, ("fsdp", r) if self.regroup else ("dp", r))

    def attn_index(self):
        return lax.axis_index("fsdp") & 1 if self.regroup else lax.axis_index("dp")

    def group_of(self, f, y):
        return (f & ~1) | y if self.regroup else f

    def trade(self, x):
        if not self.regroup:
            return x
        perm = []
        for y in range(self.nd):
            for f in range(self.nf):
                c = f & 1
                if c != y:
                    perm.append((y * self.nf + f, c * self.nf + (f & ~1 | y)))
        return lax.ppermute(x, ("dp", "fsdp"), perm)

    def traded(self, x, got):
        if not self.regroup:
            return x
        return jnp.where(lax.axis_index("fsdp") & 1 != lax.axis_index("dp"), got, x)

    def offsets(self, order):
        out = []
        for s in range(self.nd * self.nf):
            d = f = 0
            for j, (axis, mask) in enumerate(order):
                if s >> j & 1:
                    if axis == "dp":
                        d ^= mask
                    else:
                        f ^= mask
            out.append((d, f))
        return out

    def halves(self, x, bit, axes):
        axis, mask = bit
        b = jnp.where(lax.axis_index(axis) & mask != 0, 1, 0)
        if axis == "fsdp":
            at = axes.index(mask)
            keep = lax.dynamic_index_in_dim(x, b, at, keepdims=False)
            send = lax.dynamic_index_in_dim(x, 1 - b, at, keepdims=False)
            return keep, send, axes[:at] + axes[at + 1 :]
        half = x.shape[-1] // 2
        keep = lax.dynamic_slice_in_dim(x, b * half, half, x.ndim - 1)
        send = lax.dynamic_slice_in_dim(x, (1 - b) * half, half, x.ndim - 1)
        return keep, send, axes


def plus(*xs):
    total = xs[0].astype(f32)
    for x in xs[1:]:
        total = total + x.astype(f32)
    return total.astype(bf16)


def tie(*groups):
    flat = lax.optimization_barrier(tuple(x for g in groups for x in g))
    out, at = [], 0
    for g in groups:
        out.append(list(flat[at : at + len(g)]))
        at += len(g)
    return out


class Gather:
    def __init__(self, net, block, split):
        self.net = net
        rows = block.shape[0]
        cuts = [(0, split, net.orders[0]), (split, rows, net.orders[1])]
        cuts = [c for c in cuts if c[0] < c[1]]
        self.bounds = [c[:2] for c in cuts]
        self.orders = [c[2] for c in cuts]
        self.x = [block[None]]
        self.done = 0
        self.common = len(net.orders[0]) - 3

    def send(self):
        if self.done == self.common:
            self.x = [self.x[0][:, a:b] for a, b in self.bounds]
        self.raw = [self.net.swap(x, o[self.done]) for x, o in zip(self.x, self.orders)]

    def join(self):
        if self.done == self.common + 1:
            self.far = self.raw
        else:
            self.x = [jnp.concatenate([x, r], axis=0) for x, r in zip(self.x, self.raw)]
        self.done += 1

    def finish_common(self):
        while self.done < self.common:
            self.send()
            self.join()

    def core(self, which):
        return [self.net.swap(x, self.orders[0][-1]) for x in which]


class Sum:
    def __init__(self, net, x):
        self.net = net
        n = x.shape[1]
        x = x.reshape((2,) * (net.fb - 1) + x.shape[1:])
        axes = [1 << b for b in range(net.fb - 1, 0, -1)]
        dps = [("dp", 1 << b) for b in range(net.db - 1, -1, -1)]
        fs = [("fsdp", 1 << b) for b in range(1, net.fb)]
        half = n // 2
        self.parts = [
            [lax.slice_in_dim(x, p * half, p * half + half, axis=x.ndim - 2), axes, order]
            for p, order in enumerate((dps + fs[:1], fs[:1] + dps))
        ]
        self.tail = fs[1:]

    @property
    def left(self):
        return max(len(p[2]) for p in self.parts) + len(self.tail)

    def send(self):
        if not self.parts[0][2] and len(self.parts) > 1:
            self.parts = [[jnp.concatenate([p[0] for p in self.parts], axis=-2), self.parts[0][1], self.tail]]
            self.tail = []
        self.keeps, self.raw = [], []
        for p in self.parts:
            keep, send, p[1] = self.net.halves(p[0], p[2][0], p[1])
            self.keeps.append(keep)
            self.raw.append(self.net.swap(send, p[2][0]))

    def join(self):
        for p, keep, got in zip(self.parts, self.keeps, self.raw):
            p[0] = plus(keep, got)
            p[2] = p[2][1:]

    def finish(self):
        while self.left:
            self.send()
            self.join()
        return self.parts[0][0]


def place_kernel(idx, *refs, plans, count):
    srcs, outs, sems = refs[:count], refs[count:-1], refs[-1]
    copies = []
    for ref, plan in zip(srcs, plans):
        kd = ref.shape[2]
        for slot, ((d, f), moves) in enumerate(plan):
            for first, rows, which, n, start in moves:
                row = pl.multiple_of((idx[1] ^ f) * n + start, 16)
                col = pl.multiple_of((idx[0] ^ d) * kd, LANES)
                copies.append(
                    pltpu.make_async_copy(
                        ref.at[slot, pl.ds(first, rows), :],
                        outs[which].at[pl.ds(row, rows), pl.ds(col, kd)],
                        sems.at[len(copies)],
                    )
                )
    for c in copies:
        c.start()
    for c in copies:
        c.wait()


def place(net, idx, gather, theirs, sizes):
    pieces = gather.x + gather.far + theirs
    lanes = pieces[0].shape[-1]
    plans = []
    total = 0
    count = len(gather.bounds)
    for i in range(len(pieces)):
        quarter, part = divmod(i, count)
        offs = net.offsets(gather.orders[part])
        some = offs[quarter * len(offs) // 4 : (quarter + 1) * len(offs) // 4]
        lo, hi = gather.bounds[part]
        moves, at = [], 0
        for which, n in enumerate(sizes):
            a, b = max(lo, at), min(hi, at + n)
            if a < b:
                moves.append((a - lo, b - a, which, n, a - at))
            at += n
        plans.append([(o, moves) for o in some])
        total += len(some) * len(moves)
    shapes = [shape((n * net.nf, lanes * net.nd), bf16) for n in sizes]
    return pl.pallas_call(
        partial(place_kernel, plans=plans, count=len(pieces)),
        grid_spec=pltpu.PrefetchScalarGridSpec(
            num_scalar_prefetch=1,
            grid=(1,),
            in_specs=[pl.BlockSpec(memory_space=pl.ANY)] * len(pieces),
            out_specs=[pl.BlockSpec(memory_space=pl.ANY)] * len(sizes),
            scratch_shapes=[pltpu.SemaphoreType.DMA((total,))],
        ),
        out_shape=shapes,
        compiler_params=params(16),
        cost_estimate=cost(0, 4 * sum(sizes) * net.nf * lanes * net.nd),
        name="place",
    )(idx, *pieces)


def norm_stats(x):
    mean = jnp.mean(x, axis=-1, keepdims=True)
    centered = x - mean
    var = jnp.mean(centered * centered, axis=-1, keepdims=True)
    rstd = lax.rsqrt(var + epsilon)
    return centered * rstd, rstd


def seg_sums(pick, x):
    top = x.astype(bf16)
    low = (x - top.astype(f32)).astype(bf16)
    return (dot(pick, top, 0, 0) + dot(pick, low, 0, 0))[:8]


def flip_kernel(*refs):
    n = len(refs) // 2
    for src, dst in zip(refs[:n], refs[n:]):
        dst[...] = jnp.transpose(src[...].astype(f32)).astype(bf16)


def flip(*xs):
    return pl.pallas_call(
        flip_kernel,
        out_shape=[shape(x.shape[::-1], bf16) for x in xs],
        compiler_params=params(32),
        cost_estimate=cost(0, 4 * sum(x.size for x in xs)),
        name="flip",
    )(*xs)


def skip_fwd_kernel(idx, lens, frames, skip, cond, w, hidden, mixed):
    rb, d = frames.shape
    pos = idx[0] * (rb * pl.num_programs(0)) + pl.program_id(0) * rb + lax.broadcasted_iota(jnp.int32, (rb, 1), 0)
    keep = jnp.zeros((rb, 1), f32)
    end = 0
    for u in range(lens.shape[1]):
        start, end = end, end + lens[0, u]
        keep = jnp.where((pos >= start) & (pos < end), (1 - lens[1, u]).astype(f32), keep)
    m = (frames[...].astype(f32) + keep * cond[...].astype(f32)).astype(bf16)
    mixed[...] = m
    hidden[...] = (dot(m, w[:, :d], 1, 1) + dot(skip[...], w[:, d:], 1, 1)).astype(bf16)


def skip_fwd(idx, lens, frames, skip, cond, w):
    r, d = frames.shape
    rb = min(256, r)
    row = pl.BlockSpec((rb, d), lambda i, s, t: (i, 0))
    return pl.pallas_call(
        skip_fwd_kernel,
        grid_spec=pltpu.PrefetchScalarGridSpec(
            num_scalar_prefetch=2,
            grid=(r // rb,),
            in_specs=[row, row, row, pl.BlockSpec(w.shape, lambda i, s, t: (0, 0))],
            out_specs=[row, row],
        ),
        out_shape=[shape((r, d), bf16)] * 2,
        compiler_params=params(),
        cost_estimate=cost(4 * r * d * d, 10 * r * d + 4 * d * d),
        name="skip_fwd",
    )(idx, lens, frames, skip, cond, w)


def turn(x, cos, sin, sign):
    width = x.shape[1]
    reps = width // LANES
    if reps > 1:
        cos = jnp.concatenate([cos] * reps, axis=1)
        sin = jnp.concatenate([sin] * reps, axis=1)
    lane = lax.broadcasted_iota(jnp.int32, (1, width), 1)
    other = jnp.where(lane % HD < HD // 2, pltpu.roll(x, width - HD // 2, 1), pltpu.roll(x, HD // 2, 1))
    return x * cos + other * sin if sign > 0 else x * cos - other * sin


def chosen(idx, own, got, part):
    half = pl.program_id(0) * 2 < pl.num_programs(0)
    new = jnp.where(half, got[0][part, :], got[1][part, :]) if len(got) > 1 else got[0][part, :]
    return jnp.where(idx[2] > 0, new, own[part, :])


def parts_of(rows):
    return (slice(0, rows),)


def chosen_specs(rb, d, steps, halves=2):
    row = pl.BlockSpec((rb, d), lambda i, s: (i, 0))
    if halves == 1:
        return [row, row]
    return [
        row,
        pl.BlockSpec((rb, d), lambda i, s: (jnp.minimum(i, steps // 2 - 1), 0)),
        pl.BlockSpec((rb, d), lambda i, s: (jnp.maximum(i - steps // 2, 0), 0)),
    ]


def qkv_fwd_kernel(idx, hidden0, got, pick, mod, w, cos, sin, hidden, normed, *pieces):
    d = hidden.shape[1]
    na = len(pieces)
    hw = d // na
    ys = []
    for rows in parts_of(hidden.shape[0]):
        h = chosen(idx, hidden0, (got,), rows)
        hidden[rows, :] = h
        xh, _ = norm_stats(h.astype(f32))
        pk = pick[rows, :]
        y = (xh * (1.0 + dot(pk, mod[:, d:], 1, 0)) + dot(pk, mod[:, :d], 1, 0)).astype(bf16)
        normed[rows, :] = y
        ys.append((rows, y))
    for rows, y in ys:
        for part in range(3):
            for r in range(na):
                at = pl.multiple_of(part * d + (idx[0] ^ r) * hw, hw)
                z = dot(y, w[pl.ds(at, hw), :], 1, 1)
                if part < 2:
                    z = turn(z, cos[rows, :], sin[rows, :], 1)
                if part == 0:
                    z = z * (1.0 / math.sqrt(HD))
                pieces[r][part, rows, :] = z.astype(bf16)


def qkv_fwd(net, idx, hidden0, got, pick, mod, w, cos, sin):
    r, d = hidden0.shape
    rb = min(256, r // 2)
    hw = d // net.na
    row = pl.BlockSpec((rb, d), lambda i, s: (i, 0))
    narrow = pl.BlockSpec((rb, LANES), lambda i, s: (i, 0))
    out = pl.BlockSpec((3, rb, hw), lambda i, s: (0, i, 0))
    res = pl.pallas_call(
        qkv_fwd_kernel,
        grid_spec=pltpu.PrefetchScalarGridSpec(
            num_scalar_prefetch=1,
            grid=(r // rb,),
            in_specs=chosen_specs(rb, d, r // rb, 1)
            + [
                narrow,
                pl.BlockSpec(mod.shape, lambda i, s: (0, 0)),
                pl.BlockSpec(w.shape, lambda i, s: (0, 0)),
                narrow,
                narrow,
            ],
            out_specs=[row, row] + [out] * net.na,
        ),
        out_shape=[shape((r, d), bf16)] * 2 + [shape((3, r, hw), bf16)] * net.na,
        compiler_params=params(),
        cost_estimate=cost(6 * r * d * d, 14 * r * d + 6 * d * d),
        name="qkv_fwd",
    )(idx, hidden0, got, pick, mod, w, cos, sin)
    return res[0], res[1], res[2:]


def out_fwd_kernel(idx, *refs, na):
    pieces = refs[:na]
    hidden, pick, mod, w, d_f0, got0, got1, attn, hidden2, normed, d_f = refs[na:]
    d = hidden.shape[1]
    hw = d // na
    for rows in parts_of(hidden.shape[0]):
        d_f[rows, :] = chosen(idx, d_f0, (got0, got1), rows)
        for r in range(na):
            attn[rows, pl.ds(pl.multiple_of((idx[0] ^ r) * hw, hw), hw)] = pieces[r][rows, :]
        h2 = hidden[rows, :].astype(f32) + dot(attn[rows, :], w[...], 1, 1)
        hidden2[rows, :] = h2
        xh, _ = norm_stats(h2)
        pk = pick[rows, :]
        normed[rows, :] = (xh * (1.0 + dot(pk, mod[:, d:], 1, 0)) + dot(pk, mod[:, :d], 1, 0)).astype(bf16)


def out_fwd(net, idx, pieces, hidden, pick, mod, w, d_f0, d_f_got):
    r, d = hidden.shape
    rb = min(256, r // 2)
    hw = d // net.na
    row = pl.BlockSpec((rb, d), lambda i, s: (i, 0))
    narrow = pl.BlockSpec((rb, LANES), lambda i, s: (i, 0))
    return pl.pallas_call(
        partial(out_fwd_kernel, na=net.na),
        grid_spec=pltpu.PrefetchScalarGridSpec(
            num_scalar_prefetch=1,
            grid=(r // rb,),
            in_specs=[pl.BlockSpec((rb, hw), lambda i, s: (i, 0))] * net.na
            + [
                row,
                narrow,
                pl.BlockSpec(mod.shape, lambda i, s: (0, 0)),
                pl.BlockSpec(w.shape, lambda i, s: (0, 0)),
            ]
            + chosen_specs(rb, d, r // rb),
            out_specs=[row, row, row, row],
        ),
        out_shape=[shape((r, d), bf16), shape((r, d), f32)] + [shape((r, d), bf16)] * 2,
        compiler_params=params(),
        cost_estimate=cost(2 * r * d * d, 12 * r * d + 2 * d * d),
        name="out_fwd",
    )(idx, *pieces, hidden, pick, mod, w, d_f0, *d_f_got)


def norm_back(x, grad, pick, scale):
    xh, rstd = norm_stats(x)
    g = grad * (1.0 + dot(pick, scale, 1, 0))
    dx = rstd * (
        g
        - jnp.mean(g, axis=-1, keepdims=True)
        - xh * jnp.mean(g * xh, axis=-1, keepdims=True)
    )
    return dx, seg_sums(pick, grad * xh), seg_sums(pick, grad)


def out_bwd_kernel(idx, grad, hidden2, d_f, pick, scale, w, d_h2, d_att, sums, *outs):
    refs, hold = outs[:-1], outs[-1]
    i = pl.program_id(0)
    na = len(refs)
    d = grad.shape[1]
    hw = d // na
    both = jnp.zeros(sums.shape, f32)
    for rows in parts_of(grad.shape[0]):
        dx, d_scale, d_shift = norm_back(hidden2[rows, :], grad[rows, :], pick[rows, :], scale[...])
        dh = d_f[rows, :].astype(f32) + dx
        d_h2[rows, :] = dh
        low = dh.astype(bf16)
        d_att[rows, :] = low
        hold[rows, :] = dot(low, w[...], 1, 0).astype(bf16)
        for r in range(na):
            refs[r][rows, :] = hold[rows, pl.ds(pl.multiple_of((idx[0] ^ r) * hw, hw), hw)]
        both = both + jnp.concatenate([d_shift, d_scale], axis=1)

    @pl.when(i == 0)
    def _():
        sums[...] = both

    @pl.when(i > 0)
    def _():
        sums[...] += both


def out_bwd(net, idx, grad, hidden2, d_f, pick, scale, w):
    r, d = grad.shape
    rb = min(256, r)
    hw = d // net.na
    row = pl.BlockSpec((rb, d), lambda i, s: (i, 0))
    narrow = pl.BlockSpec((rb, LANES), lambda i, s: (i, 0))
    whole = lambda a: pl.BlockSpec(a.shape, lambda i, s: (0, 0))
    res = pl.pallas_call(
        out_bwd_kernel,
        grid_spec=pltpu.PrefetchScalarGridSpec(
            num_scalar_prefetch=1,
            grid=(r // rb,),
            in_specs=[row, row, row, narrow, whole(scale), whole(w)],
            out_specs=[row, row, pl.BlockSpec((8, 2 * d), lambda i, s: (0, 0))]
            + [pl.BlockSpec((rb, hw), lambda i, s: (i, 0))] * net.na,
            scratch_shapes=[pltpu.VMEM((rb, d), bf16)],
        ),
        out_shape=[shape((r, d), f32), shape((r, d), bf16), shape((8, 2 * d), f32)]
        + [shape((r, hw), bf16)] * net.na,
        compiler_params=params(),
        cost_estimate=cost(2 * r * d * d, 20 * r * d + 2 * d * d),
        name="out_bwd",
    )(idx, grad, hidden2, d_f, pick, scale, w)
    return res[0], res[1], res[2], res[3:]


def turn_back_kernel(idx, *refs, na):
    pieces = refs[:-3]
    cos, sin, d_qkv = refs[-3:]
    d = d_qkv.shape[1] // 3
    hw = d // na
    for part in range(3):
        first = 0
        for k, piece in enumerate(pieces):
            r = k % na
            wide = piece.shape[2]
            z = piece[part]
            if part < 2:
                z = turn(z.astype(f32), cos[...], sin[...], -1).astype(bf16)
            d_qkv[:, pl.ds(pl.multiple_of(part * d + (idx[0] ^ r) * hw + first, LANES), wide)] = z
            first += wide if r == na - 1 else 0


def turn_back(net, idx, pieces, cos, sin, d):
    r = cos.shape[0]
    rb = min(256, r)
    narrow = pl.BlockSpec((rb, LANES), lambda i, s: (i, 0))
    return pl.pallas_call(
        partial(turn_back_kernel, na=net.na),
        grid_spec=pltpu.PrefetchScalarGridSpec(
            num_scalar_prefetch=1,
            grid=(r // rb,),
            in_specs=[pl.BlockSpec((3, rb, p.shape[2]), lambda i, s: (0, i, 0)) for p in pieces] + [narrow, narrow],
            out_specs=pl.BlockSpec((rb, 3 * d), lambda i, s: (i, 0)),
        ),
        out_shape=shape((r, 3 * d), bf16),
        compiler_params=params(),
        cost_estimate=cost(12 * r * d, 12 * r * d),
        name="turn_back",
    )(idx, *pieces, cos, sin)


def qkv_bwd_kernel(d_qkv, hidden, d_h2, pick, scale, w, d_h, sums):
    i = pl.program_id(0)
    both = jnp.zeros(sums.shape, f32)
    for rows in parts_of(hidden.shape[0]):
        grad = dot(d_qkv[rows, :], w[...], 1, 0)
        dx, d_scale, d_shift = norm_back(hidden[rows, :].astype(f32), grad, pick[rows, :], scale[...])
        d_h[rows, :] = (d_h2[rows, :] + dx).astype(bf16)
        both = both + jnp.concatenate([d_shift, d_scale], axis=1)

    @pl.when(i == 0)
    def _():
        sums[...] = both

    @pl.when(i > 0)
    def _():
        sums[...] += both


def qkv_bwd(d_qkv, hidden, d_h2, pick, scale, w):
    r, d = hidden.shape
    rb = min(256, r)
    row = pl.BlockSpec((rb, d), lambda i: (i, 0))
    narrow = pl.BlockSpec((rb, LANES), lambda i: (i, 0))
    whole = lambda a: pl.BlockSpec(a.shape, lambda i: (0, 0))
    return pl.pallas_call(
        qkv_bwd_kernel,
        grid=(r // rb,),
        in_specs=[pl.BlockSpec((rb, 3 * d), lambda i: (i, 0)), row, row, narrow, whole(scale), whole(w)],
        out_specs=[row, pl.BlockSpec((8, 2 * d), lambda i: (0, 0))],
        out_shape=[shape((r, d), bf16), shape((8, 2 * d), f32)],
        compiler_params=params(),
        cost_estimate=cost(6 * r * d * d, 16 * r * d + 6 * d * d),
        name="qkv_bwd",
    )(d_qkv, hidden, d_h2, pick, scale, w)


def skip_bwd_kernel(idx, d_h, got0, got1, w, d_frames, d_skip):
    d = d_h.shape[1]
    g = chosen(idx, d_h, (got0, got1), slice(None))
    d_frames[...] = dot(g, w[:, :d], 1, 0)
    d_skip[...] = dot(g, w[:, d:], 1, 0)


def skip_bwd(idx, d_h, d_h_got, w):
    r, d = d_h.shape
    rb = min(256, r // 2)
    row = pl.BlockSpec((rb, d), lambda i, s: (i, 0))
    return pl.pallas_call(
        skip_bwd_kernel,
        grid_spec=pltpu.PrefetchScalarGridSpec(
            num_scalar_prefetch=1,
            grid=(r // rb,),
            in_specs=chosen_specs(rb, d, r // rb) + [pl.BlockSpec(w.shape, lambda i, s: (0, 0))],
            out_specs=[row, row],
        ),
        out_shape=[shape((r, d), f32)] * 2,
        compiler_params=params(),
        cost_estimate=cost(4 * r * d * d, 12 * r * d + 4 * d * d),
        name="skip_bwd",
    )(idx, d_h, *d_h_got, w)


def outer_kernel(idx, g, *refs, n, own, choose):
    xs = refs[:own]
    keep, send = refs[-2:]
    pairs = keep.shape[0]
    at = 0
    low = idx[1] & 1 == 0
    for k in range(0, own, 2 if choose else 1):
        x = jnp.where(idx[2] > 0, xs[k + 1][...], xs[k][...]) if choose else xs[k][...]
        width = x.shape[1]
        z = dot(g[...], x, 0, 0).astype(bf16).reshape(pairs, 2, n, width)
        keep[:, :, at : at + width] = jnp.where(low, z[:, 0], z[:, 1])
        send[:, :, at : at + width] = jnp.where(low, z[:, 1], z[:, 0])
        at += width


def outer(net, idx, g, xs, n, rows, first, into=None, choose=False):
    r, wide = g.shape
    per = max(1, 512 // (2 * n))
    while net.nf // 2 % per:
        per -= 1
    k = sum(x.shape[1] for x in xs) // (2 if choose else 1)
    out = pl.BlockSpec((per, n, k), lambda i, s: (i, first // n, 0))
    big = shape((net.nf // 2, rows, k), bf16)
    extra = list(into) if into is not None else []
    return pl.pallas_call(
        partial(outer_kernel, n=n, own=len(xs), choose=choose),
        grid_spec=pltpu.PrefetchScalarGridSpec(
            num_scalar_prefetch=1,
            grid=(wide // (2 * n * per),),
            in_specs=[pl.BlockSpec((r, 2 * n * per), lambda i, s: (0, i))]
            + [pl.BlockSpec(x.shape, lambda i, s: (0, 0)) for x in xs]
            + [pl.BlockSpec(memory_space=pl.ANY)] * len(extra),
            out_specs=[out, out],
        ),
        out_shape=[big, big],
        input_output_aliases={2 + len(xs) + i: i for i in range(len(extra))},
        compiler_params=params(),
        cost_estimate=cost(2 * r * wide * k, 2 * (r * wide + r * k + wide * k)),
        name="outer",
    )(idx, g, *xs, *extra)


def gelu_both(u):
    u2 = u * u
    t = jnp.tanh(GELU_C * u * (1.0 + 0.044715 * u2))
    half = 0.5 * (1.0 + t)
    return u * half, half + 0.5 * u * (1.0 - t * t) * (GELU_C * (1.0 + 3 * 0.044715 * u2))


def ffn_kernel(*refs, steps, second):
    x_ref, df_ref, o_in = refs[:3]
    at = 4 if second else 3
    ws = refs[at : at + steps]
    o_ref, dx_ref = refs[at + steps : at + steps + 2]
    gs = refs[at + steps + 2 : at + 2 * steps + 2]
    o_acc, dx_acc, o_low, wbuf, gbuf, sem_w, sem_g, sem_a = refs[at + 2 * steps + 2 :]
    s = pl.program_id(0)
    slot = lax.rem(s, 2)
    w_in = [pltpu.make_async_copy(ws[k], wbuf.at[k % 2], sem_w.at[k]) for k in range(steps)]
    g_out = [pltpu.make_async_copy(gbuf.at[k % 2], gs[k], sem_g.at[k]) for k in range(steps)]
    sums = [pltpu.make_async_copy(o_in, o_acc, sem_a.at[0])]
    if second:
        sums.append(pltpu.make_async_copy(refs[3], dx_acc, sem_a.at[1]))
    ends = [
        pltpu.make_async_copy(o_low if second else o_acc, o_ref, sem_a.at[2]),
        pltpu.make_async_copy(dx_acc, dx_ref, sem_a.at[3]),
    ]

    @pl.when(s == 0)
    def _():
        w_in[0].start()
        for c in sums:
            c.start()
        if not second:
            dx_acc[...] = jnp.zeros_like(dx_acc)

    for k in range(steps):

        @pl.when(s == k)
        def _():
            if k + 1 < steps:
                w_in[k + 1].start()
            w_in[k].wait()

    d = x_ref.shape[1]
    wu = wbuf[slot, :, 0].reshape(-1, d)
    wd = wbuf[slot, :, 1].reshape(-1, d)
    x, df = x_ref[...], df_ref[...]
    g, dg = gelu_both(dot(x, wu, 1, 1))
    act = g.astype(bf16)
    du = (dot(df, wd, 1, 1) * dg).astype(bf16)

    @pl.when(s == 0)
    def _():
        for c in sums:
            c.wait()

    o_acc[...] += dot(act, wd, 1, 0)
    dx_acc[...] += dot(du, wu, 1, 0)
    for k in range(2, steps):

        @pl.when(s == k)
        def _():
            g_out[k - 2].wait()

    part = gbuf.shape[1:2] + gbuf.shape[3:]
    gbuf[slot, :, 1] = dot(act, df, 0, 0).astype(bf16).reshape(part)
    gbuf[slot, :, 0] = dot(du, x, 0, 0).astype(bf16).reshape(part)
    for k in range(steps):

        @pl.when(s == k)
        def _():
            g_out[k].start()

    @pl.when(s == steps - 1)
    def _():
        if second:
            o_low[...] = o_acc[...].astype(bf16)
        for c in ends:
            c.start()
        for k in range(max(0, steps - 2), steps):
            g_out[k].wait()
        for c in ends:
            c.wait()


def ffn(x, df, o_in, pieces, dx_in=None):
    second = dx_in is not None
    r, d = x.shape
    steps = len(pieces)
    full = pl.BlockSpec((r, d), lambda s: (0, 0), pipeline_mode=pl.Buffered(1))
    far = pl.BlockSpec(memory_space=pl.ANY)
    args = [x, df, o_in] + ([dx_in] if second else []) + list(pieces)
    piece = shape(pieces[0].shape, bf16)
    units = piece.shape[0] * piece.shape[2]
    return pl.pallas_call(
        partial(ffn_kernel, steps=steps, second=second),
        grid=(steps,),
        in_specs=[full, full] + [far] * (len(args) - 2),
        out_specs=[far] * (steps + 2),
        out_shape=[shape((r, d), bf16 if second else f32), shape((r, d), f32)] + [piece] * steps,
        scratch_shapes=[
            pltpu.VMEM((r, d), f32),
            pltpu.VMEM((r, d), f32),
            pltpu.VMEM((r, d) if second else (16, LANES), bf16),
            pltpu.VMEM((2, *piece.shape), bf16),
            pltpu.VMEM((2, *piece.shape), bf16),
            pltpu.SemaphoreType.DMA((steps,)),
            pltpu.SemaphoreType.DMA((steps,)),
            pltpu.SemaphoreType.DMA((4,)),
        ],
        compiler_params=params(),
        cost_estimate=cost(12 * r * d * steps * units, 16 * r * d + 8 * steps * units * d, steps * units * r),
        name="ffn",
    )(*args)


def head_sel(h):
    lane = lax.broadcasted_iota(jnp.int32, (1, LANES), 1)
    return lane < HD if h == 0 else lane >= HD


def load_rolled(idx, hold, refs, part, rest):
    rows = refs[0].shape[-2]
    t = rows * len(refs)
    for r, ref in enumerate(refs):
        x = ref[part] if part is not None else ref[...]
        hold[pl.ds(pl.multiple_of((idx[0] ^ r) * rows, rows), rows), :] = x.astype(f32)
    hold[t : t + rest, :] = hold[0:rest, :]
    return hold[pl.ds(idx[1], t), :]


def store_unrolled(idx, hold, t, rest):
    row = lax.broadcasted_iota(jnp.int32, (rest, 1), 0)
    hold[0:rest, :] = jnp.where(row < idx[1], hold[t : t + rest, :], hold[0:rest, :])


def attn_fwd_kernel(idx, *refs, na, long):
    pieces = refs[:na]
    segr, segc = refs[na : na + 2]
    outs = refs[na + 2 : 2 * na + 2]
    lse_ref, hold, ql, kl, vt = refs[2 * na + 2 :]
    rows = outs[0].shape[0]
    t = rows * na
    rest = t - long
    ql[...] = load_rolled(idx, hold, pieces, 0, rest).astype(bf16)
    kl[...] = load_rolled(idx, hold, pieces, 1, rest).astype(bf16)
    vt[...] = jnp.transpose(load_rolled(idx, hold, pieces, 2, rest)).astype(bf16)

    def pair(r0, n, c0, cn, mask):
        q = ql[pl.ds(r0, n), :]
        k = kl[c0 : c0 + cn, :]
        got, lses = [], []
        for h in range(2):
            qh = jnp.where(head_sel(h), q, jnp.zeros_like(q))
            s = dot(k, qh, 1, 1)
            if mask is not None:
                s = jnp.where(mask, s, NEG)
            top = jnp.max(s, axis=0, keepdims=True)
            p = jnp.exp(s - top)
            total = jnp.sum(p, axis=0, keepdims=True)
            got.append(dot(vt[HD * h : HD * h + HD, c0 : c0 + cn], p.astype(bf16), 1, 0) / total)
            lses.append(top + jnp.log(total))
        lse_ref[0, :, pl.ds(r0, n)] = jnp.concatenate(lses, axis=0)
        hold[pl.ds(idx[1] + r0, n), :] = jnp.transpose(jnp.concatenate(got, axis=0))

    step = long // 2
    for i in range(2):
        pair(i * step, step, 0, long, None)
    pair(long, rest, long, rest, segc[:, :1] == segr[:1, :])
    store_unrolled(idx, hold, t, rest)
    for r in range(na):
        outs[r][...] = hold[pl.ds(pl.multiple_of((idx[0] ^ r) * rows, rows), rows), :].astype(bf16)


def attn_fwd(net, idx, pieces, segr, segc, long):
    na = net.na
    _, rows, hw = pieces[0].shape
    t = rows * na
    rest = t - long
    pairs = hw // LANES
    const = lambda a: pl.BlockSpec(a.shape, lambda j, s: (0, 0))
    work = pairs * 2 * (long * long + rest * rest)
    res = pl.pallas_call(
        partial(attn_fwd_kernel, na=na, long=long),
        grid_spec=pltpu.PrefetchScalarGridSpec(
            num_scalar_prefetch=1,
            grid=(pairs,),
            in_specs=[pl.BlockSpec((3, rows, LANES), lambda j, s: (0, 0, j))] * na + [const(segr), const(segc)],
            out_specs=[pl.BlockSpec((rows, LANES), lambda j, s: (0, j))] * na
            + [pl.BlockSpec((1, 2, t), lambda j, s: (j, 0, 0))],
            scratch_shapes=[
                pltpu.VMEM((t + rest, LANES), f32),
                pltpu.VMEM((t, LANES), bf16),
                pltpu.VMEM((t, LANES), bf16),
                pltpu.VMEM((LANES, t), bf16),
            ],
        ),
        out_shape=[shape((rows, hw), bf16)] * na + [shape((pairs, 2, t), f32)],
        compiler_params=params(),
        cost_estimate=cost(16 * HD * work, 8 * t * hw, work),
        name="attn_fwd",
    )(idx, *pieces, segr, segc)
    return res[:na], res[na]


def attn_bwd_kernel(idx, *refs, na, long):
    pieces, d_pieces = refs[:na], refs[na : 2 * na]
    lse_ref, segr, segc = refs[2 * na : 2 * na + 3]
    outs = refs[2 * na + 3 : 3 * na + 3]
    hold, ql, kl, vl, dl, kt, dqt, dka, dva = refs[3 * na + 3 :]
    rows = outs[0].shape[1]
    t = rows * na
    rest = t - long
    ql[...] = load_rolled(idx, hold, pieces, 0, rest).astype(bf16)
    kf = load_rolled(idx, hold, pieces, 1, rest)
    kl[...] = kf.astype(bf16)
    kt[...] = jnp.transpose(kf).astype(bf16)
    vl[...] = load_rolled(idx, hold, pieces, 2, rest).astype(bf16)
    dl[...] = load_rolled(idx, hold, d_pieces, None, rest).astype(bf16)
    dka[...] = jnp.zeros_like(dka)
    dva[...] = jnp.zeros_like(dva)

    def pair(r0, n, c0, cn, mask):
        q, do = ql[pl.ds(r0, n), :], dl[pl.ds(r0, n), :]
        k, v = kl[c0 : c0 + cn, :], vl[c0 : c0 + cn, :]
        dqs = []
        for h in range(2):
            qh = jnp.where(head_sel(h), q, jnp.zeros_like(q))
            dh = jnp.where(head_sel(h), do, jnp.zeros_like(do))
            s = dot(k, qh, 1, 1)
            if mask is not None:
                s = jnp.where(mask, s, NEG)
            p = jnp.exp(s - lse_ref[0, h : h + 1, pl.ds(r0, n)])
            dp = dot(v, dh, 1, 1)
            delta = jnp.sum(p * dp, axis=0, keepdims=True)
            ds = (p * (dp - delta)).astype(bf16)
            dqs.append(dot(kt[HD * h : HD * h + HD, c0 : c0 + cn], ds, 1, 0))
            dva[c0 : c0 + cn, :] += dot(p.astype(bf16), dh, 1, 0)
            dka[c0 : c0 + cn, :] += dot(ds, qh, 1, 0)
        dqt[pl.ds(r0, n), :] = jnp.transpose(jnp.concatenate(dqs, axis=0))

    step = long // 2

    def body(i, carry):
        pair(pl.multiple_of(i * step, step), step, 0, long, None)
        return carry

    lax.fori_loop(0, 2, body, 0)
    pair(long, rest, long, rest, segc[:, :1] == segr[:1, :])
    for part, src in enumerate((dqt, dka, dva)):
        x = src[...]
        if part == 0:
            x = x * (1.0 / math.sqrt(HD))
        hold[pl.ds(idx[1], t), :] = x
        store_unrolled(idx, hold, t, rest)
        for r in range(na):
            at = pl.multiple_of((idx[0] ^ r) * rows, rows)
            outs[r][part] = hold[pl.ds(at, rows), :].astype(bf16)


def attn_bwd(net, idx, pieces, d_pieces, lse, segr, segc, long, start, pairs):
    na = net.na
    rows = pieces[0].shape[1]
    t = rows * na
    rest = t - long
    hw = pairs * LANES
    const = lambda a: pl.BlockSpec(a.shape, lambda j, s: (0, 0))
    three = pl.BlockSpec((3, rows, LANES), lambda j, s: (0, 0, j + start))
    out = pl.BlockSpec((3, rows, LANES), lambda j, s: (0, 0, j))
    work = pairs * 2 * (long * long + rest * rest)
    return pl.pallas_call(
        partial(attn_bwd_kernel, na=na, long=long),
        grid_spec=pltpu.PrefetchScalarGridSpec(
            num_scalar_prefetch=1,
            grid=(pairs,),
            in_specs=[three] * na
            + [pl.BlockSpec((rows, LANES), lambda j, s: (0, j + start))] * na
            + [pl.BlockSpec((1, 2, t), lambda j, s: (j + start, 0, 0)), const(segr), const(segc)],
            out_specs=[out] * na,
            scratch_shapes=[pltpu.VMEM((t + rest, LANES), f32)]
            + [pltpu.VMEM((t, LANES), bf16)] * 4
            + [pltpu.VMEM((LANES, t), bf16)]
            + [pltpu.VMEM((t, LANES), f32)] * 3,
        ),
        out_shape=[shape((3, rows, hw), bf16)] * na,
        compiler_params=params(),
        cost_estimate=cost(40 * HD * work, 16 * t * hw, work),
        name="attn_bwd",
    )(idx, *pieces, *d_pieces, lse, segr, segc)


def prep_kernel(ints, me, w_mod, cos, sin, pick, segr, segc, smooth, part, idx, gs, *, nd, utt, long, regroup, bits):
    nf = ints.shape[0]
    rows, rest = cos.shape[0], segr.shape[1]
    total = rows * (2 if regroup else nd)
    y, f, block = me[0], me[1], me[3]

    def slot(g):
        r = g ^ f
        return sum(((r >> b) & 1) << j for j, b in enumerate(bits))

    mine = slot((f & ~1) | y if regroup else f)
    starts, ends, at, first = [], [], 0, 0
    for u in range(utt):
        size = ints[mine, u]
        starts.append(at)
        first = jnp.where(size == long, at, first)
        at = at + size
        ends.append(at)
    idx[0], idx[1], idx[2] = block, first, me[2]
    kept = 0
    for g in range(nf):
        for u in range(utt):
            kept = kept + (1 - ints[g, utt + u])
    gs[0] = (nf * utt) / jnp.maximum(kept.astype(f32), 1.0)

    pos = block * rows + lax.broadcasted_iota(jnp.int32, (rows, LANES), 0)
    lane = lax.broadcasted_iota(jnp.int32, (rows, LANES), 1)
    offset = jnp.zeros((rows, LANES), jnp.int32)
    number = jnp.zeros((rows, LANES), jnp.int32)
    for u in range(1, utt):
        past = pos >= starts[u]
        offset = jnp.where(past, starts[u], offset)
        number = jnp.where(past, u, number)
    pick[...] = jnp.where((lane % utt == number) & (lane < 3 * utt), 1.0, 0.0).astype(bf16)
    half = HD // 2
    frequency = jnp.exp((lane[:1] % half).astype(f32) * (-math.log(10000.0) / half))
    angles = (pos - offset).astype(f32) * frequency
    cos[...] = jnp.cos(angles)
    sin[...] = jnp.where(lane[:1] % HD < half, -1.0, 1.0) * jnp.sin(angles)

    for ref, axis in ((segr, 1), (segc, 0)):
        p = first + long + lax.broadcasted_iota(jnp.int32, ref.shape, axis)
        p = jnp.where(p >= total, p - total, p)
        number = jnp.zeros(ref.shape, jnp.int32)
        for u in range(1, utt):
            number = jnp.where(p >= starts[u], u, number)
        ref[...] = number

    n, wide = smooth.shape
    d = wide * nd
    row = lax.broadcasted_iota(jnp.int32, (n, LANES), 0)
    when = jnp.zeros((n, LANES), jnp.int32)
    slots = [slot(g) for g in range(nf)]
    for j in range(n):
        k, u = divmod(j, utt)
        g = 2 * (k % (nf // 2)) + k // (nf // 2) if regroup else k
        when = jnp.where(row == j, ints[slots[g], 2 * utt + u], when)
    flow = 1000.0 * (when[:, :1].astype(f32) / STEPS)
    col = y * wide + lax.broadcasted_iota(jnp.int32, (1, wide), 1)
    low = col < d // 2
    at = jnp.where(low, col, col - d // 2).astype(f32)
    angles = flow * jnp.exp(at * (-math.log(10000.0) / (d // 2)))
    e = jnp.where(low, jnp.sin(angles), jnp.cos(angles))
    e = (e / (1.0 + jnp.exp(-e))).astype(bf16)
    smooth[...] = e
    part[...] = dot(e, w_mod[...], 1, 0)


def prep(net, ints, me, w_mod, rows, long, rest):
    utt = ints.shape[1] // 3
    n = net.nf * utt
    smem = pl.BlockSpec(memory_space=pltpu.SMEM)
    vmem = pl.BlockSpec(memory_space=pltpu.VMEM)
    return pl.pallas_call(
        partial(prep_kernel, nd=net.nd, utt=utt, long=long, regroup=net.regroup, bits=tuple(net.int_bits)),
        in_specs=[smem, smem, vmem],
        out_specs=[vmem] * 7 + [smem, smem],
        out_shape=[
            shape((rows, LANES), f32),
            shape((rows, LANES), f32),
            shape((rows, LANES), bf16),
            shape((8, rest), jnp.int32),
            shape((rest, LANES), jnp.int32),
            shape((n, w_mod.shape[0]), bf16),
            shape((n, w_mod.shape[1]), f32),
            shape((3,), jnp.int32),
            shape((1,), f32),
        ],
        compiler_params=params(32),
        cost_estimate=cost(2 * n * w_mod.size, 16 * rows * LANES, 4 * n * w_mod.shape[0]),
        name="prep",
    )(ints, me, w_mod)


def terms_kernel(*refs):
    out = refs[-1]
    x = refs[0][...]
    for ref in refs[1:-1]:
        x = x + ref[...]
    a = x.astype(bf16)
    b = (x - a.astype(f32)).astype(bf16)
    c = (x - a.astype(f32) - b.astype(f32)).astype(bf16)
    n = x.shape[0]
    out[...] = jnp.zeros_like(out)
    out[0 : 3 * n, :] = jnp.concatenate([a.astype(f32), b.astype(f32), c.astype(f32)], axis=0).astype(bf16)


def three_terms(*xs):
    return pl.pallas_call(
        terms_kernel,
        out_shape=shape((LANES, xs[0].shape[1]), bf16),
        compiler_params=params(16),
        cost_estimate=cost(0, 300 * xs[0].shape[1]),
        name="three_terms",
    )(*xs)


def scale_kernel(gs, x, out):
    out[...] = (x[...].astype(f32) * gs[0]).astype(bf16)


def scaled(x, gs):
    r, d = x.shape
    rb = min(256, r)
    row = pl.BlockSpec((rb, d), lambda i, s: (i, 0))
    return pl.pallas_call(
        scale_kernel,
        grid_spec=pltpu.PrefetchScalarGridSpec(num_scalar_prefetch=1, grid=(r // rb,), in_specs=[row], out_specs=row),
        out_shape=shape((r, d), bf16),
        compiler_params=params(16),
        cost_estimate=cost(r * d, 4 * r * d),
        name="scaled",
    )(gs, x)


def to_units(net, turned, w_down, y, f):
    nd, nf = net.nd, net.nf
    units = w_down.shape[0] // nf
    down = lax.all_to_all(w_down, "fsdp", split_axis=0, concat_axis=1, tiled=True)
    got = []
    for j in range(nd):
        perm = [(a * nf + b, nd * b + (a + j) % nd) for a in range(nd) for b in range(nf)]
        send = lax.dynamic_slice_in_dim(turned, (y + j) % nd * units, units, 0)
        got.append(move(net, send, perm, y, f))
    return got, down


def mix_kernel(idx, *refs, half, nd):
    ups, down, out = refs[:nd], refs[nd], refs[nd + 1]
    units, width = ups[0].shape
    own = lax.rem(idx[0], nd)
    for j, up in enumerate(ups):
        col = pl.multiple_of(lax.rem(own + nd - j, nd) * width, width)
        for at in range(0, units, half):
            out[2 * at : 2 * at + half, pl.ds(col, width)] = up[at : at + half, :]
    for at in range(0, units, half):
        out[2 * at + half : 2 * at + 2 * half, :] = down[at : at + half, :]


def own_units(net, ups, down, half, y, f):
    whole = pl.BlockSpec(memory_space=pltpu.VMEM)
    return pl.pallas_call(
        partial(mix_kernel, half=half, nd=net.nd),
        in_specs=[pl.BlockSpec(memory_space=pltpu.SMEM)] + [whole] * (net.nd + 1),
        out_specs=whole,
        out_shape=shape((2 * down.shape[0], down.shape[1]), bf16),
        compiler_params=params(16),
        cost_estimate=cost(0, 8 * down.size),
        name="own_units",
    )(jnp.stack([y * net.nf + f]).astype(jnp.int32), *ups, down)


def from_units(net, g_up, g_down, y, f):
    nd, nf = net.nd, net.nf
    grad_down = lax.all_to_all(g_down, "fsdp", split_axis=1, concat_axis=0, tiled=True)
    width = g_up.shape[1] // nd
    own = (y * nf + f) % nd
    got = []
    for j in range(nd):
        perm = [(nd * b + (a + j) % nd, a * nf + b) for a in range(nd) for b in range(nf)]
        send = lax.dynamic_slice_in_dim(g_up, (own - j) % nd * width, width, 1)
        got.append(move(net, send, perm, y, f))
    got = jnp.stack(got)
    rows = [lax.dynamic_index_in_dim(got, (h - y) % nd, 0, keepdims=False) for h in range(nd)]
    return jnp.concatenate(rows, axis=0).T.astype(f32), grad_down.astype(f32)


def move(net, x, perm, y, f):
    fixed = [a for a, b in perm if a == b]
    got = lax.ppermute(x, ("dp", "fsdp"), [(a, b) for a, b in perm if a != b])
    me = y * net.nf + f
    stays = False
    for a in fixed:
        stays = stays | (me == a)
    return jnp.where(stays, x, got) if fixed else got


def local(net, frames, skip_in, cond_in, lengths, drop_mask, time_index, w_skip, w_qkv, w_out, w_up, w_down, w_mod, d_out):
    frames, skip_in, cond_in, d_out = frames[0], skip_in[0], cond_in[0], d_out[0]
    rows, d = frames.shape
    nd, nf, na = net.nd, net.nf, net.na
    y, f = lax.axis_index("dp"), lax.axis_index("fsdp")
    utt = lengths.shape[1]
    group_len = rows * nd
    long = int(group_len * LONG_PART)
    rest = group_len - long
    core_bit = ("fsdp", 1)
    n_skip, n_qkv, n_out = w_skip.shape[1], w_qkv.shape[1], w_out.shape[1]
    part_of = lambda n, share: int(n * share) // 16 * 16
    block = net.attn_index()
    moved = ((f & 1) != y if net.regroup else y < 0).astype(jnp.int32)
    me = jnp.stack([y, f, moved, block]).astype(jnp.int32)
    cut = rows // 2
    cols = w_mod.shape[1]

    (skip_turned,) = flip(w_skip)
    qkv_turned, out_turned, up_turned = flip(w_qkv, w_out, w_up)
    g2 = Gather(net, jnp.concatenate([qkv_turned, out_turned], axis=0), part_of(n_qkv + n_out, 0.33))
    lens = jnp.concatenate([lengths, drop_mask], axis=0)
    ints = jnp.concatenate([lengths, drop_mask, time_index], axis=1)
    bits = net.int_bits[:]

    def more_ints():
        nonlocal ints
        if bits:
            ints = jnp.concatenate([ints, net.swap(ints, ("fsdp", 1 << bits.pop(0)))], axis=0)

    def step(g):
        if g.done < g.common:
            g.join()

    def start(g):
        if g.done < g.common:
            g.send()
        else:
            g.raw = []

    g1 = Gather(net, skip_turned, part_of(n_skip, 0.5))
    while g1.done < g1.common:
        g1.send()
        more_ints()
        g1.raw, (ints, lens, up_turned, w_down), g2.x = tie(g1.raw, [ints, lens, up_turned, w_down], g2.x)
        g1.join()
    g1.send()
    start(g2)
    while bits:
        more_ints()
    g1.raw, g2.raw, (ints, up_turned, w_down) = tie(g1.raw, g2.raw, [ints, up_turned, w_down])
    g1.join()
    step(g2)
    g1.send()
    start(g2)
    up_parts, down = to_units(net, up_turned, w_down, y, f)
    cos, sin, pick, segr, segc, smooth, part, idx, gs = prep(net, ints, me, w_mod, rows, long, rest)
    if net.regroup:
        part = part.reshape(2, nf // 2, utt, cols)
        mod_got = net.swap(lax.dynamic_index_in_dim(part, 1 - y, 0, keepdims=False), ("dp", 1))
        part = lax.dynamic_index_in_dim(part, y, 0, keepdims=False)
    else:
        for b in range(net.db):
            part = part + net.swap(part, ("dp", 1 << b))
        mod_got = part
    g1.raw, g2.raw, (ints, part, mod_got, down) = tie(g1.raw, g2.raw, [ints, part, mod_got, down])
    g1.join()
    theirs = g1.core(g1.x + g1.far)
    step(g2)
    g2.finish_common()
    g2.send()
    skip_t, = place(net, me, g1, theirs, [n_skip])
    (skip_t, lens, part, mod_got, down), up_parts = tie([skip_t, lens, part, mod_got, down], up_parts)
    units = down.shape[0]
    half = units // 2 if units // 2 % 16 == 0 else units
    g3 = Gather(net, own_units(net, up_parts, down, half, y, f), units * 2 if half == units else units)
    start(g3)
    hidden0, mixed = skip_fwd(me, lens, frames, skip_in, cond_in, skip_t)
    (hidden0, mixed, part, mod_got), g2.raw = tie([hidden0, mixed, part, mod_got], g2.raw)

    hidden_got = [net.trade(hidden0)]
    g2.join()
    g2.send()
    if net.regroup:
        part = jnp.broadcast_to((part + mod_got)[:, None], (nf // 2, 2, utt, cols))
    part = part.reshape(nf, utt, cols)
    mod = lax.all_to_all(part, "fsdp", split_axis=0, concat_axis=2, tiled=True)
    (hidden0, mod, d_out), g2.raw, g3.raw = tie([hidden0, mod, d_out], g2.raw, g3.raw)
    mods = three_terms(mod.reshape(utt, nf * cols))
    mod_a, mod_f = mods[:, : 2 * d], mods[:, 2 * d :]
    g2.join()
    theirs = g2.core(g2.x + g2.far)
    qkv_t, out_t = place(net, me, g2, theirs, [n_qkv, n_out])
    step(g3)
    (hidden0, qkv_t, out_t, d_out, mod_a, mod_f), hidden_got, g3.x = tie([hidden0, qkv_t, out_t, d_out, mod_a, mod_f], hidden_got, g3.x)

    start(g3)
    d_f0 = scaled(d_out, gs)
    d_f_got = [net.trade(d_f0[:cut])]
    hidden, normed_a, sent = qkv_fwd(net, idx, hidden0, hidden_got[0], pick, mod_a, qkv_t, cos, sin)
    sent, g3.raw, d_f_got, (d_f0,) = tie(list(sent), g3.raw, d_f_got, [d_f0])
    step(g3)
    g3.finish_common()
    pieces = [sent[0]] + [net.attn_swap(sent[r], r) for r in range(1, na)]
    pieces, (d_f0,), g3.x = tie(pieces, [d_f0], g3.x)
    g3.send()
    d_f_got.append(net.trade(d_f0[cut:]))
    attn_p, lse = attn_fwd(net, idx, pieces, segr, segc, long)
    (lse,), d_f_got, attn_p, g3.raw = tie([lse], d_f_got, list(attn_p), g3.raw)
    attn_p = [attn_p[0]] + [net.attn_swap(attn_p[r], r) for r in range(1, na)]
    g3.join()
    attn_p, near = tie(attn_p, g3.x)
    g3.send()
    near_core = g3.core(near)
    attn, hidden2, normed_f, d_f = out_fwd(net, idx, attn_p, hidden, pick, mod_f, out_t, d_f0, d_f_got)

    view = lambda x: x.reshape(x.shape[0], 2, x.shape[1] // 2, x.shape[2])
    acc, dx, *got1 = ffn(normed_f, d_f, hidden2, [view(x) for x in near_core + near])
    (acc, dx, mixed, skip_in), far, got1 = tie([acc, dx, mixed, skip_in], g3.raw, got1)
    far_core = g3.core(far)
    count = len(far)
    far_core, got1, (mixed, skip_in) = tie(far_core, got1, [mixed, skip_in])
    mixed_got, skip_got = net.trade(mixed), net.trade(skip_in)
    swapped1 = [net.swap(x, core_bit) for x in got1[:count]]
    out_b, dx, *got2 = ffn(normed_f, d_f, acc, [view(x) for x in far_core + far], dx)
    (out_b, dx, mixed_got), got2, swapped1 = tie([out_b, dx, mixed_got], got2, swapped1)
    swapped2 = [net.swap(x, core_bit) for x in got2[:count]]

    d_h2, d_att, sums_f, d_attn_p = out_bwd(net, idx, dx, hidden2, d_f, pick, mod_f[:, d:], out_t)
    (d_h2, d_att, skip_got), d_attn_p, swapped2 = tie([d_h2, d_att, skip_got], list(d_attn_p), swapped2)
    d_attn_p = [d_attn_p[0]] + [net.attn_swap(d_attn_p[r], r) for r in range(1, na)]
    sum_far = [plus(a, b) for a, b in zip(got2[count:], swapped2)]
    d_attn_p, sum_far, (d_att,) = tie(d_attn_p, sum_far, [d_att])
    came = [net.swap(x, o[-2]) for x, o in zip(sum_far, g3.orders)]
    into = outer(net, me, d_att, [attn], n_out, n_qkv + n_out, n_qkv)
    d_attn_p, into, (out_b,) = tie(d_attn_p, list(into), [out_b])

    def send_half(xs, bits):
        n = xs[0].shape[0] // 2
        return [x[:n] for x in xs], [net.swap(x[n:], b) for x, b in zip(xs, bits)]

    all_pairs = d // na // LANES
    pairs = max(1, all_pairs // 2)
    d_sent = attn_bwd(net, idx, pieces, d_attn_p, lse, segr, segc, long, 0, pairs)
    d_sent, came, d_attn_p = tie(list(d_sent), came, d_attn_p)
    d_pieces = [d_sent[0]] + [net.attn_swap(d_sent[r], r) for r in range(1, na)]
    ff = [plus(a, b, c) for a, b, c in zip(got1[count:], swapped1, came)]
    d_attn_p, ff, (out_b,) = tie(d_attn_p, ff, [out_b])
    kept, raw = send_half(ff, [o[-3] for o in g3.orders])
    output_got = net.trade(out_b)
    if all_pairs > pairs:
        d_sent = attn_bwd(net, idx, pieces, d_attn_p, lse, segr, segc, long, pairs, all_pairs - pairs)
        d_sent, raw, d_pieces = tie(list(d_sent), raw, d_pieces)
        d_pieces += [d_sent[0]] + [net.attn_swap(d_sent[r], r) for r in range(1, na)]
    ff = jnp.stack([plus(a, b) for a, b in zip(kept, raw)], axis=1)
    common = list(reversed(g3.orders[0][:-3]))
    d_pieces, (ff,) = tie(d_pieces, [ff])
    raw = []
    if common:
        kept, raw = send_half([ff], [common[0]])
    d_qkv = turn_back(net, idx, d_pieces, cos, sin, d)
    d_h, sums_a = qkv_bwd(d_qkv, hidden, d_h2, pick, mod_a[:, d:], qkv_t)
    (d_h, sums_a, d_qkv, output_got), raw = tie([d_h, sums_a, d_qkv, output_got], raw)
    if common:
        ff = plus(kept[0], raw[0])
    raw = []
    if len(common) > 1:
        kept, raw = send_half([ff], [common[1]])
    keep1, send1 = outer(net, me, d_h, [mixed, mixed_got, skip_in, skip_got], n_skip, n_skip, 0, choose=True)
    (keep1, send1, d_qkv, d_h), = tie([keep1, send1, d_qkv, d_h])
    got1 = net.swap(send1, core_bit)
    keep2, send2 = outer(net, me, d_qkv, [normed_a], n_qkv, n_qkv + n_out, 0, into)
    (keep2, send2, keep1, got1), = tie([keep2, send2, keep1, got1])
    got2 = net.swap(send2, core_bit)
    s1 = Sum(net, plus(keep1, got1))
    s1.send()
    (keep2, got2), = tie([keep2, got2])
    s2 = Sum(net, plus(keep2, got2))
    (s2.parts[0][0], s2.parts[1][0], sums_a, d_h, out_b), s1.raw = tie(
        [s2.parts[0][0], s2.parts[1][0], sums_a, d_h, out_b], s1.raw
    )
    s2.send()
    s1.join()
    s1.send()
    s1.raw, raw, (out_b, d_h) = tie(s1.raw, raw, [out_b, d_h])
    if len(common) > 1:
        ff = plus(kept[0], raw[0])
    for bit in common[2:]:
        kept, raw = send_half([ff], [bit])
        ff = plus(kept[0], raw[0])
    ff = ff.reshape(-1, 2, half, d)
    s1.join()
    s1.send()
    output = net.traded(out_b, output_got)
    grad_up, grad_down = from_units(net, ff[:, 0].reshape(units, d), ff[:, 1].reshape(units, d), y, f)
    s1.raw, s2.raw, (sums_a, output, grad_up, grad_down, d_h) = tie(s1.raw, s2.raw, [sums_a, output, grad_up, grad_down, d_h])
    d_h_got = [net.trade(d_h[:cut])]
    s2.join()
    s2.send()
    s1.join()
    if s1.left:
        s1.send()

    d_mod = jnp.concatenate([sums_a, sums_f], axis=1).reshape(utt, nf, cols).transpose(1, 0, 2)
    d_mod = lax.all_to_all(d_mod, "fsdp", split_axis=0, concat_axis=0, tiled=True)
    s1.raw, s2.raw, (d_mod, d_h), d_h_got = tie(s1.raw, s2.raw, [d_mod, d_h], d_h_got)
    d_h_got.append(net.trade(d_h[cut:]))
    if net.regroup:
        pair_sum = d_mod.reshape(nf // 2, 2, utt, cols).sum(axis=1)
        here = (jnp.arange(2) == y).astype(f32)
        d_mod = pair_sum[None] * here[:, None, None, None]
    d_mod = d_mod.reshape(nf * utt, cols)
    for b in range(net.db):
        d_mod = d_mod + net.swap(d_mod, ("dp", 1 << b))
    while s2.left:
        s2.join()
        if s1.left:
            s1.join()
        if s2.left:
            s2.send()
        if s1.left:
            s1.send()
        if s1.left and s2.left:
            s1.raw, s2.raw, d_h_got = tie(s1.raw, s2.raw, d_h_got)
        elif s2.left == 2:
            s2.raw, d_h_got = tie(s2.raw, d_h_got)
    d_frames, d_skip = skip_bwd(me, d_h, d_h_got, skip_t)
    g_two = s2.finish()
    grad_qkv = g_two[:n_qkv].T.astype(f32)
    grad_out = g_two[n_qkv:].T.astype(f32)
    grad_skip = s1.finish().T.astype(f32)
    grad_mod = jnp.dot(smooth.astype(f32).T, d_mod, precision=highest)

    return (output[None], d_frames[None], d_skip[None], grad_skip, grad_qkv, grad_out, grad_up, grad_down, grad_mod)


def solution(mesh):
    rows = P("fsdp", "dp", None)
    ints = P("fsdp", None)
    weight = P("dp", "fsdp")
    return jax.shard_map(
        partial(local, Net(mesh)),
        mesh=mesh,
        in_specs=(rows, rows, rows, ints, ints, ints, *([weight] * 6), rows),
        out_specs=(rows, rows, rows, *([weight] * 6)),
        check_vma=False,
    )
```

```python
from functools import partial
import math

import jax
import jax.numpy as jnp
from jax import lax
from jax.experimental import pallas as pl
from jax.experimental.pallas import tpu as pltpu
from jax.sharding import PartitionSpec as P

HD = 64
LANES = 128
STEPS = 1000
LONG_PART = 0.75
NEG = -1e30
GELU_C = math.sqrt(2.0 / math.pi)
VMEM_MIB = 60

bf16 = jnp.bfloat16
f32 = jnp.float32
highest = lax.Precision.HIGHEST
epsilon = 1e-06


def dot(a, b, ca, cb):
    return lax.dot_general(a, b, (((ca,), (cb,)), ((), ())), preferred_element_type=f32)


def params(mib=VMEM_MIB):
    return pltpu.CompilerParams(vmem_limit_bytes=mib * 2**20)


def cost(flops, nbytes, trans=0):
    return pl.CostEstimate(flops=int(flops), bytes_accessed=int(nbytes), transcendentals=int(trans))


def shape(dims, dtype):
    return jax.ShapeDtypeStruct(dims, dtype)


class Net:
    def __init__(self, mesh):
        self.nd = mesh.shape["dp"]
        self.nf = mesh.shape["fsdp"]
        self.fb = self.nf.bit_length() - 1
        self.db = self.nd.bit_length() - 1
        common = [("fsdp", 1 << b) for b in range(self.fb - 1, 1, -1)]
        common += [("dp", 1 << b) for b in range(self.db - 1, 0, -1)]
        x, y, core = ("fsdp", 2), ("dp", 1), ("fsdp", 1)
        self.orders = (common + [x, y, core], common + [y, x, core])
        self.regroup = self.nd == 2
        self.int_bits = [*range(2, self.fb), 0, 1]
        self.na = 2 if self.regroup else self.nd

    def swap(self, x, bit):
        axis, mask = bit
        size = self.nf if axis == "fsdp" else self.nd
        return lax.ppermute(x, axis, [(i, i ^ mask) for i in range(size)])

    def attn_swap(self, x, r):
        return self.swap(x, ("fsdp", r) if self.regroup else ("dp", r))

    def attn_index(self):
        return lax.axis_index("fsdp") & 1 if self.regroup else lax.axis_index("dp")

    def group_of(self, f, y):
        return (f & ~1) | y if self.regroup else f

    def trade(self, x):
        if not self.regroup:
            return x
        perm = []
        for y in range(self.nd):
            for f in range(self.nf):
                c = f & 1
                if c != y:
                    perm.append((y * self.nf + f, c * self.nf + (f & ~1 | y)))
        return lax.ppermute(x, ("dp", "fsdp"), perm)

    def traded(self, x, got):
        if not self.regroup:
            return x
        return jnp.where(lax.axis_index("fsdp") & 1 != lax.axis_index("dp"), got, x)

    def offsets(self, order):
        out = []
        for s in range(self.nd * self.nf):
            d = f = 0
            for j, (axis, mask) in enumerate(order):
                if s >> j & 1:
                    if axis == "dp":
                        d ^= mask
                    else:
                        f ^= mask
            out.append((d, f))
        return out

    def halves(self, x, bit, axes):
        axis, mask = bit
        b = jnp.where(lax.axis_index(axis) & mask != 0, 1, 0)
        if axis == "fsdp":
            at = axes.index(mask)
            keep = lax.dynamic_index_in_dim(x, b, at, keepdims=False)
            send = lax.dynamic_index_in_dim(x, 1 - b, at, keepdims=False)
            return keep, send, axes[:at] + axes[at + 1 :]
        half = x.shape[-1] // 2
        keep = lax.dynamic_slice_in_dim(x, b * half, half, x.ndim - 1)
        send = lax.dynamic_slice_in_dim(x, (1 - b) * half, half, x.ndim - 1)
        return keep, send, axes


def plus(*xs):
    total = xs[0].astype(f32)
    for x in xs[1:]:
        total = total + x.astype(f32)
    return total.astype(bf16)


def tie(*groups):
    flat = lax.optimization_barrier(tuple(x for g in groups for x in g))
    out, at = [], 0
    for g in groups:
        out.append(list(flat[at : at + len(g)]))
        at += len(g)
    return out


class Gather:
    def __init__(self, net, block, split):
        self.net = net
        rows = block.shape[0]
        cuts = [(0, split, net.orders[0]), (split, rows, net.orders[1])]
        cuts = [c for c in cuts if c[0] < c[1]]
        self.bounds = [c[:2] for c in cuts]
        self.orders = [c[2] for c in cuts]
        self.x = [block[None]]
        self.done = 0
        self.common = len(net.orders[0]) - 3

    def send(self):
        if self.done == self.common:
            self.x = [self.x[0][:, a:b] for a, b in self.bounds]
        self.raw = [self.net.swap(x, o[self.done]) for x, o in zip(self.x, self.orders)]

    def join(self):
        if self.done == self.common + 1:
            self.far = self.raw
        else:
            self.x = [jnp.concatenate([x, r], axis=0) for x, r in zip(self.x, self.raw)]
        self.done += 1

    def finish_common(self):
        while self.done < self.common:
            self.send()
            self.join()

    def core(self, which):
        return [self.net.swap(x, self.orders[0][-1]) for x in which]


class Sum:
    def __init__(self, net, x):
        self.net = net
        n = x.shape[1]
        x = x.reshape((2,) * (net.fb - 1) + x.shape[1:])
        axes = [1 << b for b in range(net.fb - 1, 0, -1)]
        dps = [("dp", 1 << b) for b in range(net.db - 1, -1, -1)]
        fs = [("fsdp", 1 << b) for b in range(1, net.fb)]
        half = n // 2
        self.parts = [
            [lax.slice_in_dim(x, p * half, p * half + half, axis=x.ndim - 2), axes, order]
            for p, order in enumerate((dps + fs[:1], fs[:1] + dps))
        ]
        self.tail = fs[1:]

    @property
    def left(self):
        return max(len(p[2]) for p in self.parts) + len(self.tail)

    def send(self):
        if not self.parts[0][2] and len(self.parts) > 1:
            self.parts = [[jnp.concatenate([p[0] for p in self.parts], axis=-2), self.parts[0][1], self.tail]]
            self.tail = []
        self.keeps, self.raw = [], []
        for p in self.parts:
            keep, send, p[1] = self.net.halves(p[0], p[2][0], p[1])
            self.keeps.append(keep)
            self.raw.append(self.net.swap(send, p[2][0]))

    def join(self):
        for p, keep, got in zip(self.parts, self.keeps, self.raw):
            p[0] = plus(keep, got)
            p[2] = p[2][1:]

    def finish(self):
        while self.left:
            self.send()
            self.join()
        return self.parts[0][0]


def place_kernel(idx, *refs, plans, count):
    srcs, outs, sems = refs[:count], refs[count:-1], refs[-1]
    copies = []
    for ref, plan in zip(srcs, plans):
        kd = ref.shape[2]
        for slot, ((d, f), moves) in enumerate(plan):
            for first, rows, which, n, start in moves:
                row = pl.multiple_of((idx[1] ^ f) * n + start, 16)
                col = pl.multiple_of((idx[0] ^ d) * kd, LANES)
                copies.append(
                    pltpu.make_async_copy(
                        ref.at[slot, pl.ds(first, rows), :],
                        outs[which].at[pl.ds(row, rows), pl.ds(col, kd)],
                        sems.at[len(copies)],
                    )
                )
    for c in copies:
        c.start()
    for c in copies:
        c.wait()


def place(net, idx, gather, theirs, sizes):
    pieces = gather.x + gather.far + theirs
    lanes = pieces[0].shape[-1]
    plans = []
    total = 0
    count = len(gather.bounds)
    for i in range(len(pieces)):
        quarter, part = divmod(i, count)
        offs = net.offsets(gather.orders[part])
        some = offs[quarter * len(offs) // 4 : (quarter + 1) * len(offs) // 4]
        lo, hi = gather.bounds[part]
        moves, at = [], 0
        for which, n in enumerate(sizes):
            a, b = max(lo, at), min(hi, at + n)
            if a < b:
                moves.append((a - lo, b - a, which, n, a - at))
            at += n
        plans.append([(o, moves) for o in some])
        total += len(some) * len(moves)
    shapes = [shape((n * net.nf, lanes * net.nd), bf16) for n in sizes]
    return pl.pallas_call(
        partial(place_kernel, plans=plans, count=len(pieces)),
        grid_spec=pltpu.PrefetchScalarGridSpec(
            num_scalar_prefetch=1,
            grid=(1,),
            in_specs=[pl.BlockSpec(memory_space=pl.ANY)] * len(pieces),
            out_specs=[pl.BlockSpec(memory_space=pl.ANY)] * len(sizes),
            scratch_shapes=[pltpu.SemaphoreType.DMA((total,))],
        ),
        out_shape=shapes,
        compiler_params=params(16),
        cost_estimate=cost(0, 4 * sum(sizes) * net.nf * lanes * net.nd),
        name="place",
    )(idx, *pieces)


def norm_stats(x):
    mean = jnp.mean(x, axis=-1, keepdims=True)
    centered = x - mean
    var = jnp.mean(centered * centered, axis=-1, keepdims=True)
    rstd = lax.rsqrt(var + epsilon)
    return centered * rstd, rstd


def seg_sums(pick, x):
    top = x.astype(bf16)
    low = (x - top.astype(f32)).astype(bf16)
    return (dot(pick, top, 0, 0) + dot(pick, low, 0, 0))[:8]


def flip_kernel(*refs):
    n = len(refs) // 2
    for src, dst in zip(refs[:n], refs[n:]):
        dst[...] = jnp.transpose(src[...].astype(f32)).astype(bf16)


def flip(*xs):
    return pl.pallas_call(
        flip_kernel,
        out_shape=[shape(x.shape[::-1], bf16) for x in xs],
        compiler_params=params(32),
        cost_estimate=cost(0, 4 * sum(x.size for x in xs)),
        name="flip",
    )(*xs)


def skip_fwd_kernel(idx, lens, frames, skip, cond, w, hidden, mixed):
    rb, d = frames.shape
    pos = idx[0] * (rb * pl.num_programs(0)) + pl.program_id(0) * rb + lax.broadcasted_iota(jnp.int32, (rb, 1), 0)
    keep = jnp.zeros((rb, 1), f32)
    end = 0
    for u in range(lens.shape[1]):
        start, end = end, end + lens[0, u]
        keep = jnp.where((pos >= start) & (pos < end), (1 - lens[1, u]).astype(f32), keep)
    m = (frames[...].astype(f32) + keep * cond[...].astype(f32)).astype(bf16)
    mixed[...] = m
    hidden[...] = (dot(m, w[:, :d], 1, 1) + dot(skip[...], w[:, d:], 1, 1)).astype(bf16)


def skip_fwd(idx, lens, frames, skip, cond, w):
    r, d = frames.shape
    rb = min(256, r)
    row = pl.BlockSpec((rb, d), lambda i, s, t: (i, 0))
    return pl.pallas_call(
        skip_fwd_kernel,
        grid_spec=pltpu.PrefetchScalarGridSpec(
            num_scalar_prefetch=2,
            grid=(r // rb,),
            in_specs=[row, row, row, pl.BlockSpec(w.shape, lambda i, s, t: (0, 0))],
            out_specs=[row, row],
        ),
        out_shape=[shape((r, d), bf16)] * 2,
        compiler_params=params(),
        cost_estimate=cost(4 * r * d * d, 10 * r * d + 4 * d * d),
        name="skip_fwd",
    )(idx, lens, frames, skip, cond, w)


def turn(x, cos, sin, sign):
    width = x.shape[1]
    reps = width // LANES
    if reps > 1:
        cos = jnp.concatenate([cos] * reps, axis=1)
        sin = jnp.concatenate([sin] * reps, axis=1)
    lane = lax.broadcasted_iota(jnp.int32, (1, width), 1)
    other = jnp.where(lane % HD < HD // 2, pltpu.roll(x, width - HD // 2, 1), pltpu.roll(x, HD // 2, 1))
    return x * cos + other * sin if sign > 0 else x * cos - other * sin


def chosen(idx, own, got, part):
    half = pl.program_id(0) * 2 < pl.num_programs(0)
    new = jnp.where(half, got[0][part, :], got[1][part, :]) if len(got) > 1 else got[0][part, :]
    return jnp.where(idx[2] > 0, new, own[part, :])


def parts_of(rows):
    return (slice(0, rows),)


def chosen_specs(rb, d, steps, halves=2):
    row = pl.BlockSpec((rb, d), lambda i, s: (i, 0))
    if halves == 1:
        return [row, row]
    return [
        row,
        pl.BlockSpec((rb, d), lambda i, s: (jnp.minimum(i, steps // 2 - 1), 0)),
        pl.BlockSpec((rb, d), lambda i, s: (jnp.maximum(i - steps // 2, 0), 0)),
    ]


def qkv_fwd_kernel(idx, hidden0, got, pick, mod, w, cos, sin, hidden, normed, *pieces):
    d = hidden.shape[1]
    na = len(pieces)
    hw = d // na
    ys = []
    for rows in parts_of(hidden.shape[0]):
        h = chosen(idx, hidden0, (got,), rows)
        hidden[rows, :] = h
        xh, _ = norm_stats(h.astype(f32))
        pk = pick[rows, :]
        y = (xh * (1.0 + dot(pk, mod[:, d:], 1, 0)) + dot(pk, mod[:, :d], 1, 0)).astype(bf16)
        normed[rows, :] = y
        ys.append((rows, y))
    for rows, y in ys:
        for part in range(3):
            for r in range(na):
                at = pl.multiple_of(part * d + (idx[0] ^ r) * hw, hw)
                z = dot(y, w[pl.ds(at, hw), :], 1, 1)
                if part < 2:
                    z = turn(z, cos[rows, :], sin[rows, :], 1)
                if part == 0:
                    z = z * (1.0 / math.sqrt(HD))
                pieces[r][part, rows, :] = z.astype(bf16)


def qkv_fwd(net, idx, hidden0, got, pick, mod, w, cos, sin):
    r, d = hidden0.shape
    rb = min(256, r // 2)
    hw = d // net.na
    row = pl.BlockSpec((rb, d), lambda i, s: (i, 0))
    narrow = pl.BlockSpec((rb, LANES), lambda i, s: (i, 0))
    out = pl.BlockSpec((3, rb, hw), lambda i, s: (0, i, 0))
    res = pl.pallas_call(
        qkv_fwd_kernel,
        grid_spec=pltpu.PrefetchScalarGridSpec(
            num_scalar_prefetch=1,
            grid=(r // rb,),
            in_specs=chosen_specs(rb, d, r // rb, 1)
            + [
                narrow,
                pl.BlockSpec(mod.shape, lambda i, s: (0, 0)),
                pl.BlockSpec(w.shape, lambda i, s: (0, 0)),
                narrow,
                narrow,
            ],
            out_specs=[row, row] + [out] * net.na,
        ),
        out_shape=[shape((r, d), bf16)] * 2 + [shape((3, r, hw), bf16)] * net.na,
        compiler_params=params(),
        cost_estimate=cost(6 * r * d * d, 14 * r * d + 6 * d * d),
        name="qkv_fwd",
    )(idx, hidden0, got, pick, mod, w, cos, sin)
    return res[0], res[1], res[2:]


def out_fwd_kernel(idx, *refs, na):
    pieces = refs[:na]
    hidden, pick, mod, w, d_f0, got0, got1, attn, hidden2, normed, d_f = refs[na:]
    d = hidden.shape[1]
    hw = d // na
    for rows in parts_of(hidden.shape[0]):
        d_f[rows, :] = chosen(idx, d_f0, (got0, got1), rows)
        for r in range(na):
            attn[rows, pl.ds(pl.multiple_of((idx[0] ^ r) * hw, hw), hw)] = pieces[r][rows, :]
        h2 = hidden[rows, :].astype(f32) + dot(attn[rows, :], w[...], 1, 1)
        hidden2[rows, :] = h2
        xh, _ = norm_stats(h2)
        pk = pick[rows, :]
        normed[rows, :] = (xh * (1.0 + dot(pk, mod[:, d:], 1, 0)) + dot(pk, mod[:, :d], 1, 0)).astype(bf16)


def out_fwd(net, idx, pieces, hidden, pick, mod, w, d_f0, d_f_got):
    r, d = hidden.shape
    rb = min(256, r // 2)
    hw = d // net.na
    row = pl.BlockSpec((rb, d), lambda i, s: (i, 0))
    narrow = pl.BlockSpec((rb, LANES), lambda i, s: (i, 0))
    return pl.pallas_call(
        partial(out_fwd_kernel, na=net.na),
        grid_spec=pltpu.PrefetchScalarGridSpec(
            num_scalar_prefetch=1,
            grid=(r // rb,),
            in_specs=[pl.BlockSpec((rb, hw), lambda i, s: (i, 0))] * net.na
            + [
                row,
                narrow,
                pl.BlockSpec(mod.shape, lambda i, s: (0, 0)),
                pl.BlockSpec(w.shape, lambda i, s: (0, 0)),
            ]
            + chosen_specs(rb, d, r // rb),
            out_specs=[row, row, row, row],
        ),
        out_shape=[shape((r, d), bf16), shape((r, d), f32)] + [shape((r, d), bf16)] * 2,
        compiler_params=params(),
        cost_estimate=cost(2 * r * d * d, 12 * r * d + 2 * d * d),
        name="out_fwd",
    )(idx, *pieces, hidden, pick, mod, w, d_f0, *d_f_got)


def norm_back(x, grad, pick, scale):
    xh, rstd = norm_stats(x)
    g = grad * (1.0 + dot(pick, scale, 1, 0))
    dx = rstd * (
        g
        - jnp.mean(g, axis=-1, keepdims=True)
        - xh * jnp.mean(g * xh, axis=-1, keepdims=True)
    )
    return dx, seg_sums(pick, grad * xh), seg_sums(pick, grad)


def out_bwd_kernel(idx, grad, hidden2, d_f, pick, scale, w, d_h2, d_att, sums, *outs):
    refs, hold = outs[:-1], outs[-1]
    i = pl.program_id(0)
    na = len(refs)
    d = grad.shape[1]
    hw = d // na
    both = jnp.zeros(sums.shape, f32)
    for rows in parts_of(grad.shape[0]):
        dx, d_scale, d_shift = norm_back(hidden2[rows, :], grad[rows, :], pick[rows, :], scale[...])
        dh = d_f[rows, :].astype(f32) + dx
        d_h2[rows, :] = dh
        low = dh.astype(bf16)
        d_att[rows, :] = low
        hold[rows, :] = dot(low, w[...], 1, 0).astype(bf16)
        for r in range(na):
            refs[r][rows, :] = hold[rows, pl.ds(pl.multiple_of((idx[0] ^ r) * hw, hw), hw)]
        both = both + jnp.concatenate([d_shift, d_scale], axis=1)

    @pl.when(i == 0)
    def _():
        sums[...] = both

    @pl.when(i > 0)
    def _():
        sums[...] += both


def out_bwd(net, idx, grad, hidden2, d_f, pick, scale, w):
    r, d = grad.shape
    rb = min(256, r)
    hw = d // net.na
    row = pl.BlockSpec((rb, d), lambda i, s: (i, 0))
    narrow = pl.BlockSpec((rb, LANES), lambda i, s: (i, 0))
    whole = lambda a: pl.BlockSpec(a.shape, lambda i, s: (0, 0))
    res = pl.pallas_call(
        out_bwd_kernel,
        grid_spec=pltpu.PrefetchScalarGridSpec(
            num_scalar_prefetch=1,
            grid=(r // rb,),
            in_specs=[row, row, row, narrow, whole(scale), whole(w)],
            out_specs=[row, row, pl.BlockSpec((8, 2 * d), lambda i, s: (0, 0))]
            + [pl.BlockSpec((rb, hw), lambda i, s: (i, 0))] * net.na,
            scratch_shapes=[pltpu.VMEM((rb, d), bf16)],
        ),
        out_shape=[shape((r, d), f32), shape((r, d), bf16), shape((8, 2 * d), f32)]
        + [shape((r, hw), bf16)] * net.na,
        compiler_params=params(),
        cost_estimate=cost(2 * r * d * d, 20 * r * d + 2 * d * d),
        name="out_bwd",
    )(idx, grad, hidden2, d_f, pick, scale, w)
    return res[0], res[1], res[2], res[3:]


def turn_back_kernel(idx, *refs, na):
    pieces = refs[:-3]
    cos, sin, d_qkv = refs[-3:]
    d = d_qkv.shape[1] // 3
    hw = d // na
    for part in range(3):
        first = 0
        for k, piece in enumerate(pieces):
            r = k % na
            wide = piece.shape[2]
            z = piece[part]
            if part < 2:
                z = turn(z.astype(f32), cos[...], sin[...], -1).astype(bf16)
            d_qkv[:, pl.ds(pl.multiple_of(part * d + (idx[0] ^ r) * hw + first, LANES), wide)] = z
            first += wide if r == na - 1 else 0


def turn_back(net, idx, pieces, cos, sin, d):
    r = cos.shape[0]
    rb = min(256, r)
    narrow = pl.BlockSpec((rb, LANES), lambda i, s: (i, 0))
    return pl.pallas_call(
        partial(turn_back_kernel, na=net.na),
        grid_spec=pltpu.PrefetchScalarGridSpec(
            num_scalar_prefetch=1,
            grid=(r // rb,),
            in_specs=[pl.BlockSpec((3, rb, p.shape[2]), lambda i, s: (0, i, 0)) for p in pieces] + [narrow, narrow],
            out_specs=pl.BlockSpec((rb, 3 * d), lambda i, s: (i, 0)),
        ),
        out_shape=shape((r, 3 * d), bf16),
        compiler_params=params(),
        cost_estimate=cost(12 * r * d, 12 * r * d),
        name="turn_back",
    )(idx, *pieces, cos, sin)


def qkv_bwd_kernel(d_qkv, hidden, d_h2, pick, scale, w, d_h, sums):
    i = pl.program_id(0)
    both = jnp.zeros(sums.shape, f32)
    for rows in parts_of(hidden.shape[0]):
        grad = dot(d_qkv[rows, :], w[...], 1, 0)
        dx, d_scale, d_shift = norm_back(hidden[rows, :].astype(f32), grad, pick[rows, :], scale[...])
        d_h[rows, :] = (d_h2[rows, :] + dx).astype(bf16)
        both = both + jnp.concatenate([d_shift, d_scale], axis=1)

    @pl.when(i == 0)
    def _():
        sums[...] = both

    @pl.when(i > 0)
    def _():
        sums[...] += both


def qkv_bwd(d_qkv, hidden, d_h2, pick, scale, w):
    r, d = hidden.shape
    rb = min(256, r)
    row = pl.BlockSpec((rb, d), lambda i: (i, 0))
    narrow = pl.BlockSpec((rb, LANES), lambda i: (i, 0))
    whole = lambda a: pl.BlockSpec(a.shape, lambda i: (0, 0))
    return pl.pallas_call(
        qkv_bwd_kernel,
        grid=(r // rb,),
        in_specs=[pl.BlockSpec((rb, 3 * d), lambda i: (i, 0)), row, row, narrow, whole(scale), whole(w)],
        out_specs=[row, pl.BlockSpec((8, 2 * d), lambda i: (0, 0))],
        out_shape=[shape((r, d), bf16), shape((8, 2 * d), f32)],
        compiler_params=params(),
        cost_estimate=cost(6 * r * d * d, 16 * r * d + 6 * d * d),
        name="qkv_bwd",
    )(d_qkv, hidden, d_h2, pick, scale, w)


def skip_bwd_kernel(idx, d_h, got0, got1, w, d_frames, d_skip):
    d = d_h.shape[1]
    g = chosen(idx, d_h, (got0, got1), slice(None))
    d_frames[...] = dot(g, w[:, :d], 1, 0)
    d_skip[...] = dot(g, w[:, d:], 1, 0)


def skip_bwd(idx, d_h, d_h_got, w):
    r, d = d_h.shape
    rb = min(256, r // 2)
    row = pl.BlockSpec((rb, d), lambda i, s: (i, 0))
    return pl.pallas_call(
        skip_bwd_kernel,
        grid_spec=pltpu.PrefetchScalarGridSpec(
            num_scalar_prefetch=1,
            grid=(r // rb,),
            in_specs=chosen_specs(rb, d, r // rb) + [pl.BlockSpec(w.shape, lambda i, s: (0, 0))],
            out_specs=[row, row],
        ),
        out_shape=[shape((r, d), f32)] * 2,
        compiler_params=params(),
        cost_estimate=cost(4 * r * d * d, 12 * r * d + 4 * d * d),
        name="skip_bwd",
    )(idx, d_h, *d_h_got, w)


def outer_kernel(idx, g, *refs, n, own, choose):
    xs = refs[:own]
    keep, send = refs[-2:]
    pairs = keep.shape[0]
    at = 0
    low = idx[1] & 1 == 0
    for k in range(0, own, 2 if choose else 1):
        x = jnp.where(idx[2] > 0, xs[k + 1][...], xs[k][...]) if choose else xs[k][...]
        width = x.shape[1]
        z = dot(g[...], x, 0, 0).astype(bf16).reshape(pairs, 2, n, width)
        keep[:, :, at : at + width] = jnp.where(low, z[:, 0], z[:, 1])
        send[:, :, at : at + width] = jnp.where(low, z[:, 1], z[:, 0])
        at += width


def outer(net, idx, g, xs, n, rows, first, into=None, choose=False):
    r, wide = g.shape
    per = max(1, 768 // (2 * n))
    while net.nf // 2 % per:
        per -= 1
    k = sum(x.shape[1] for x in xs) // (2 if choose else 1)
    out = pl.BlockSpec((per, n, k), lambda i, s: (i, first // n, 0))
    big = shape((net.nf // 2, rows, k), bf16)
    extra = list(into) if into is not None else []
    return pl.pallas_call(
        partial(outer_kernel, n=n, own=len(xs), choose=choose),
        grid_spec=pltpu.PrefetchScalarGridSpec(
            num_scalar_prefetch=1,
            grid=(wide // (2 * n * per),),
            in_specs=[pl.BlockSpec((r, 2 * n * per), lambda i, s: (0, i))]
            + [pl.BlockSpec(x.shape, lambda i, s: (0, 0)) for x in xs]
            + [pl.BlockSpec(memory_space=pl.ANY)] * len(extra),
            out_specs=[out, out],
        ),
        out_shape=[big, big],
        input_output_aliases={2 + len(xs) + i: i for i in range(len(extra))},
        compiler_params=params(),
        cost_estimate=cost(2 * r * wide * k, 2 * (r * wide + r * k + wide * k)),
        name="outer",
    )(idx, g, *xs, *extra)


def gelu_both(u):
    u2 = u * u
    t = jnp.tanh(GELU_C * u * (1.0 + 0.044715 * u2))
    half = 0.5 * (1.0 + t)
    return u * half, half + 0.5 * u * (1.0 - t * t) * (GELU_C * (1.0 + 3 * 0.044715 * u2))


def ffn_kernel(*refs, steps, second):
    x_ref, df_ref, o_in = refs[:3]
    at = 4 if second else 3
    ws = refs[at : at + steps]
    o_ref, dx_ref = refs[at + steps : at + steps + 2]
    gs = refs[at + steps + 2 : at + 2 * steps + 2]
    o_acc, dx_acc, o_low, wbuf, gbuf, sem_w, sem_g, sem_a = refs[at + 2 * steps + 2 :]
    s = pl.program_id(0)
    slot = lax.rem(s, 2)
    w_in = [pltpu.make_async_copy(ws[k], wbuf.at[k % 2], sem_w.at[k]) for k in range(steps)]
    g_out = [pltpu.make_async_copy(gbuf.at[k % 2], gs[k], sem_g.at[k]) for k in range(steps)]
    sums = [pltpu.make_async_copy(o_in, o_acc, sem_a.at[0])]
    if second:
        sums.append(pltpu.make_async_copy(refs[3], dx_acc, sem_a.at[1]))
    ends = [
        pltpu.make_async_copy(o_low if second else o_acc, o_ref, sem_a.at[2]),
        pltpu.make_async_copy(dx_acc, dx_ref, sem_a.at[3]),
    ]

    @pl.when(s == 0)
    def _():
        w_in[0].start()
        for c in sums:
            c.start()
        if not second:
            dx_acc[...] = jnp.zeros_like(dx_acc)

    for k in range(steps):

        @pl.when(s == k)
        def _():
            if k + 1 < steps:
                w_in[k + 1].start()
            w_in[k].wait()

    d = x_ref.shape[1]
    wu = wbuf[slot, :, 0].reshape(-1, d)
    wd = wbuf[slot, :, 1].reshape(-1, d)
    x, df = x_ref[...], df_ref[...]
    g, dg = gelu_both(dot(x, wu, 1, 1))
    act = g.astype(bf16)
    du = (dot(df, wd, 1, 1) * dg).astype(bf16)

    @pl.when(s == 0)
    def _():
        for c in sums:
            c.wait()

    o_acc[...] += dot(act, wd, 1, 0)
    dx_acc[...] += dot(du, wu, 1, 0)
    for k in range(2, steps):

        @pl.when(s == k)
        def _():
            g_out[k - 2].wait()

    part = gbuf.shape[1:2] + gbuf.shape[3:]
    gbuf[slot, :, 1] = dot(act, df, 0, 0).astype(bf16).reshape(part)
    gbuf[slot, :, 0] = dot(du, x, 0, 0).astype(bf16).reshape(part)
    for k in range(steps):

        @pl.when(s == k)
        def _():
            g_out[k].start()

    @pl.when(s == steps - 1)
    def _():
        if second:
            o_low[...] = o_acc[...].astype(bf16)
        for c in ends:
            c.start()
        for k in range(max(0, steps - 2), steps):
            g_out[k].wait()
        for c in ends:
            c.wait()


def ffn(x, df, o_in, pieces, dx_in=None):
    second = dx_in is not None
    r, d = x.shape
    steps = len(pieces)
    full = pl.BlockSpec((r, d), lambda s: (0, 0), pipeline_mode=pl.Buffered(1))
    far = pl.BlockSpec(memory_space=pl.ANY)
    args = [x, df, o_in] + ([dx_in] if second else []) + list(pieces)
    piece = shape(pieces[0].shape, bf16)
    units = piece.shape[0] * piece.shape[2]
    return pl.pallas_call(
        partial(ffn_kernel, steps=steps, second=second),
        grid=(steps,),
        in_specs=[full, full] + [far] * (len(args) - 2),
        out_specs=[far] * (steps + 2),
        out_shape=[shape((r, d), bf16 if second else f32), shape((r, d), f32)] + [piece] * steps,
        scratch_shapes=[
            pltpu.VMEM((r, d), f32),
            pltpu.VMEM((r, d), f32),
            pltpu.VMEM((r, d) if second else (16, LANES), bf16),
            pltpu.VMEM((2, *piece.shape), bf16),
            pltpu.VMEM((2, *piece.shape), bf16),
            pltpu.SemaphoreType.DMA((steps,)),
            pltpu.SemaphoreType.DMA((steps,)),
            pltpu.SemaphoreType.DMA((4,)),
        ],
        compiler_params=params(),
        cost_estimate=cost(12 * r * d * steps * units, 16 * r * d + 8 * steps * units * d, steps * units * r),
        name="ffn",
    )(*args)


def head_sel(h):
    lane = lax.broadcasted_iota(jnp.int32, (1, LANES), 1)
    return lane < HD if h == 0 else lane >= HD


def load_rolled(idx, hold, refs, part, rest):
    rows = refs[0].shape[-2]
    t = rows * len(refs)
    for r, ref in enumerate(refs):
        x = ref[part] if part is not None else ref[...]
        hold[pl.ds(pl.multiple_of((idx[0] ^ r) * rows, rows), rows), :] = x.astype(f32)
    hold[t : t + rest, :] = hold[0:rest, :]
    return hold[pl.ds(idx[1], t), :]


def store_unrolled(idx, hold, t, rest):
    row = lax.broadcasted_iota(jnp.int32, (rest, 1), 0)
    hold[0:rest, :] = jnp.where(row < idx[1], hold[t : t + rest, :], hold[0:rest, :])


def attn_fwd_kernel(idx, *refs, na, long):
    pieces = refs[:na]
    segr, segc = refs[na : na + 2]
    outs = refs[na + 2 : 2 * na + 2]
    lse_ref, hold, ql, kl, vt = refs[2 * na + 2 :]
    rows = outs[0].shape[0]
    t = rows * na
    rest = t - long
    ql[...] = load_rolled(idx, hold, pieces, 0, rest).astype(bf16)
    kl[...] = load_rolled(idx, hold, pieces, 1, rest).astype(bf16)
    vt[...] = jnp.transpose(load_rolled(idx, hold, pieces, 2, rest)).astype(bf16)

    def pair(r0, n, c0, cn, mask):
        q = ql[pl.ds(r0, n), :]
        k = kl[c0 : c0 + cn, :]
        got, lses = [], []
        for h in range(2):
            qh = jnp.where(head_sel(h), q, jnp.zeros_like(q))
            s = dot(k, qh, 1, 1)
            if mask is not None:
                s = jnp.where(mask, s, NEG)
            top = jnp.max(s, axis=0, keepdims=True)
            p = jnp.exp(s - top)
            total = jnp.sum(p, axis=0, keepdims=True)
            got.append(dot(vt[HD * h : HD * h + HD, c0 : c0 + cn], p.astype(bf16), 1, 0) / total)
            lses.append(top + jnp.log(total))
        lse_ref[0, :, pl.ds(r0, n)] = jnp.concatenate(lses, axis=0)
        hold[pl.ds(idx[1] + r0, n), :] = jnp.transpose(jnp.concatenate(got, axis=0))

    step = long // 2
    for i in range(2):
        pair(i * step, step, 0, long, None)
    pair(long, rest, long, rest, segc[:, :1] == segr[:1, :])
    store_unrolled(idx, hold, t, rest)
    for r in range(na):
        outs[r][...] = hold[pl.ds(pl.multiple_of((idx[0] ^ r) * rows, rows), rows), :].astype(bf16)


def attn_fwd(net, idx, pieces, segr, segc, long):
    na = net.na
    _, rows, hw = pieces[0].shape
    t = rows * na
    rest = t - long
    pairs = hw // LANES
    const = lambda a: pl.BlockSpec(a.shape, lambda j, s: (0, 0))
    work = pairs * 2 * (long * long + rest * rest)
    res = pl.pallas_call(
        partial(attn_fwd_kernel, na=na, long=long),
        grid_spec=pltpu.PrefetchScalarGridSpec(
            num_scalar_prefetch=1,
            grid=(pairs,),
            in_specs=[pl.BlockSpec((3, rows, LANES), lambda j, s: (0, 0, j))] * na + [const(segr), const(segc)],
            out_specs=[pl.BlockSpec((rows, LANES), lambda j, s: (0, j))] * na
            + [pl.BlockSpec((1, 2, t), lambda j, s: (j, 0, 0))],
            scratch_shapes=[
                pltpu.VMEM((t + rest, LANES), f32),
                pltpu.VMEM((t, LANES), bf16),
                pltpu.VMEM((t, LANES), bf16),
                pltpu.VMEM((LANES, t), bf16),
            ],
        ),
        out_shape=[shape((rows, hw), bf16)] * na + [shape((pairs, 2, t), f32)],
        compiler_params=params(),
        cost_estimate=cost(16 * HD * work, 8 * t * hw, work),
        name="attn_fwd",
    )(idx, *pieces, segr, segc)
    return res[:na], res[na]


def attn_bwd_kernel(idx, *refs, na, long):
    pieces, d_pieces = refs[:na], refs[na : 2 * na]
    lse_ref, segr, segc = refs[2 * na : 2 * na + 3]
    outs = refs[2 * na + 3 : 3 * na + 3]
    hold, ql, kl, vl, dl, kt, dqt, dka, dva = refs[3 * na + 3 :]
    rows = outs[0].shape[1]
    t = rows * na
    rest = t - long
    ql[...] = load_rolled(idx, hold, pieces, 0, rest).astype(bf16)
    kf = load_rolled(idx, hold, pieces, 1, rest)
    kl[...] = kf.astype(bf16)
    kt[...] = jnp.transpose(kf).astype(bf16)
    vl[...] = load_rolled(idx, hold, pieces, 2, rest).astype(bf16)
    dl[...] = load_rolled(idx, hold, d_pieces, None, rest).astype(bf16)
    dka[...] = jnp.zeros_like(dka)
    dva[...] = jnp.zeros_like(dva)

    def pair(r0, n, c0, cn, mask):
        q, do = ql[pl.ds(r0, n), :], dl[pl.ds(r0, n), :]
        k, v = kl[c0 : c0 + cn, :], vl[c0 : c0 + cn, :]
        dqs = []
        for h in range(2):
            qh = jnp.where(head_sel(h), q, jnp.zeros_like(q))
            dh = jnp.where(head_sel(h), do, jnp.zeros_like(do))
            s = dot(k, qh, 1, 1)
            if mask is not None:
                s = jnp.where(mask, s, NEG)
            p = jnp.exp(s - lse_ref[0, h : h + 1, pl.ds(r0, n)])
            dp = dot(v, dh, 1, 1)
            delta = jnp.sum(p * dp, axis=0, keepdims=True)
            ds = (p * (dp - delta)).astype(bf16)
            dqs.append(dot(kt[HD * h : HD * h + HD, c0 : c0 + cn], ds, 1, 0))
            dva[c0 : c0 + cn, :] += dot(p.astype(bf16), dh, 1, 0)
            dka[c0 : c0 + cn, :] += dot(ds, qh, 1, 0)
        dqt[pl.ds(r0, n), :] = jnp.transpose(jnp.concatenate(dqs, axis=0))

    step = long // 2

    def body(i, carry):
        pair(pl.multiple_of(i * step, step), step, 0, long, None)
        return carry

    lax.fori_loop(0, 2, body, 0)
    pair(long, rest, long, rest, segc[:, :1] == segr[:1, :])
    for part, src in enumerate((dqt, dka, dva)):
        x = src[...]
        if part == 0:
            x = x * (1.0 / math.sqrt(HD))
        hold[pl.ds(idx[1], t), :] = x
        store_unrolled(idx, hold, t, rest)
        for r in range(na):
            at = pl.multiple_of((idx[0] ^ r) * rows, rows)
            outs[r][part] = hold[pl.ds(at, rows), :].astype(bf16)


def attn_bwd(net, idx, pieces, d_pieces, lse, segr, segc, long, start, pairs):
    na = net.na
    rows = pieces[0].shape[1]
    t = rows * na
    rest = t - long
    hw = pairs * LANES
    const = lambda a: pl.BlockSpec(a.shape, lambda j, s: (0, 0))
    three = pl.BlockSpec((3, rows, LANES), lambda j, s: (0, 0, j + start))
    out = pl.BlockSpec((3, rows, LANES), lambda j, s: (0, 0, j))
    work = pairs * 2 * (long * long + rest * rest)
    return pl.pallas_call(
        partial(attn_bwd_kernel, na=na, long=long),
        grid_spec=pltpu.PrefetchScalarGridSpec(
            num_scalar_prefetch=1,
            grid=(pairs,),
            in_specs=[three] * na
            + [pl.BlockSpec((rows, LANES), lambda j, s: (0, j + start))] * na
            + [pl.BlockSpec((1, 2, t), lambda j, s: (j + start, 0, 0)), const(segr), const(segc)],
            out_specs=[out] * na,
            scratch_shapes=[pltpu.VMEM((t + rest, LANES), f32)]
            + [pltpu.VMEM((t, LANES), bf16)] * 4
            + [pltpu.VMEM((LANES, t), bf16)]
            + [pltpu.VMEM((t, LANES), f32)] * 3,
        ),
        out_shape=[shape((3, rows, hw), bf16)] * na,
        compiler_params=params(),
        cost_estimate=cost(40 * HD * work, 16 * t * hw, work),
        name="attn_bwd",
    )(idx, *pieces, *d_pieces, lse, segr, segc)


def prep_kernel(ints, me, w_mod, cos, sin, pick, segr, segc, smooth, part, idx, gs, *, nd, utt, long, regroup, bits):
    nf = ints.shape[0]
    rows, rest = cos.shape[0], segr.shape[1]
    total = rows * (2 if regroup else nd)
    y, f, block = me[0], me[1], me[3]

    def slot(g):
        r = g ^ f
        return sum(((r >> b) & 1) << j for j, b in enumerate(bits))

    mine = slot((f & ~1) | y if regroup else f)
    starts, ends, at, first = [], [], 0, 0
    for u in range(utt):
        size = ints[mine, u]
        starts.append(at)
        first = jnp.where(size == long, at, first)
        at = at + size
        ends.append(at)
    idx[0], idx[1], idx[2] = block, first, me[2]
    kept = 0
    for g in range(nf):
        for u in range(utt):
            kept = kept + (1 - ints[g, utt + u])
    gs[0] = (nf * utt) / jnp.maximum(kept.astype(f32), 1.0)

    pos = block * rows + lax.broadcasted_iota(jnp.int32, (rows, LANES), 0)
    lane = lax.broadcasted_iota(jnp.int32, (rows, LANES), 1)
    offset = jnp.zeros((rows, LANES), jnp.int32)
    number = jnp.zeros((rows, LANES), jnp.int32)
    for u in range(1, utt):
        past = pos >= starts[u]
        offset = jnp.where(past, starts[u], offset)
        number = jnp.where(past, u, number)
    pick[...] = jnp.where((lane % utt == number) & (lane < 3 * utt), 1.0, 0.0).astype(bf16)
    half = HD // 2
    frequency = jnp.exp((lane[:1] % half).astype(f32) * (-math.log(10000.0) / half))
    angles = (pos - offset).astype(f32) * frequency
    cos[...] = jnp.cos(angles)
    sin[...] = jnp.where(lane[:1] % HD < half, -1.0, 1.0) * jnp.sin(angles)

    for ref, axis in ((segr, 1), (segc, 0)):
        p = first + long + lax.broadcasted_iota(jnp.int32, ref.shape, axis)
        p = jnp.where(p >= total, p - total, p)
        number = jnp.zeros(ref.shape, jnp.int32)
        for u in range(1, utt):
            number = jnp.where(p >= starts[u], u, number)
        ref[...] = number

    n, wide = smooth.shape
    d = wide * nd
    row = lax.broadcasted_iota(jnp.int32, (n, LANES), 0)
    when = jnp.zeros((n, LANES), jnp.int32)
    slots = [slot(g) for g in range(nf)]
    for j in range(n):
        k, u = divmod(j, utt)
        g = 2 * (k % (nf // 2)) + k // (nf // 2) if regroup else k
        when = jnp.where(row == j, ints[slots[g], 2 * utt + u], when)
    flow = 1000.0 * (when[:, :1].astype(f32) / STEPS)
    col = y * wide + lax.broadcasted_iota(jnp.int32, (1, wide), 1)
    low = col < d // 2
    at = jnp.where(low, col, col - d // 2).astype(f32)
    angles = flow * jnp.exp(at * (-math.log(10000.0) / (d // 2)))
    e = jnp.where(low, jnp.sin(angles), jnp.cos(angles))
    e = (e / (1.0 + jnp.exp(-e))).astype(bf16)
    smooth[...] = e
    part[...] = dot(e, w_mod[...], 1, 0)


def prep(net, ints, me, w_mod, rows, long, rest):
    utt = ints.shape[1] // 3
    n = net.nf * utt
    smem = pl.BlockSpec(memory_space=pltpu.SMEM)
    vmem = pl.BlockSpec(memory_space=pltpu.VMEM)
    return pl.pallas_call(
        partial(prep_kernel, nd=net.nd, utt=utt, long=long, regroup=net.regroup, bits=tuple(net.int_bits)),
        in_specs=[smem, smem, vmem],
        out_specs=[vmem] * 7 + [smem, smem],
        out_shape=[
            shape((rows, LANES), f32),
            shape((rows, LANES), f32),
            shape((rows, LANES), bf16),
            shape((8, rest), jnp.int32),
            shape((rest, LANES), jnp.int32),
            shape((n, w_mod.shape[0]), bf16),
            shape((n, w_mod.shape[1]), f32),
            shape((3,), jnp.int32),
            shape((1,), f32),
        ],
        compiler_params=params(32),
        cost_estimate=cost(2 * n * w_mod.size, 16 * rows * LANES, 4 * n * w_mod.shape[0]),
        name="prep",
    )(ints, me, w_mod)


def terms_kernel(*refs):
    out = refs[-1]
    x = refs[0][...]
    for ref in refs[1:-1]:
        x = x + ref[...]
    a = x.astype(bf16)
    b = (x - a.astype(f32)).astype(bf16)
    c = (x - a.astype(f32) - b.astype(f32)).astype(bf16)
    n = x.shape[0]
    out[...] = jnp.zeros_like(out)
    out[0 : 3 * n, :] = jnp.concatenate([a.astype(f32), b.astype(f32), c.astype(f32)], axis=0).astype(bf16)


def three_terms(*xs):
    return pl.pallas_call(
        terms_kernel,
        out_shape=shape((LANES, xs[0].shape[1]), bf16),
        compiler_params=params(16),
        cost_estimate=cost(0, 300 * xs[0].shape[1]),
        name="three_terms",
    )(*xs)


def scale_kernel(gs, x, out):
    out[...] = (x[...].astype(f32) * gs[0]).astype(bf16)


def scaled(x, gs):
    r, d = x.shape
    rb = min(256, r)
    row = pl.BlockSpec((rb, d), lambda i, s: (i, 0))
    return pl.pallas_call(
        scale_kernel,
        grid_spec=pltpu.PrefetchScalarGridSpec(num_scalar_prefetch=1, grid=(r // rb,), in_specs=[row], out_specs=row),
        out_shape=shape((r, d), bf16),
        compiler_params=params(16),
        cost_estimate=cost(r * d, 4 * r * d),
        name="scaled",
    )(gs, x)


def to_units(net, turned, w_down, y, f):
    nd, nf = net.nd, net.nf
    units = w_down.shape[0] // nf
    down = lax.all_to_all(w_down, "fsdp", split_axis=0, concat_axis=1, tiled=True)
    got = []
    for j in range(nd):
        perm = [(a * nf + b, nd * b + (a + j) % nd) for a in range(nd) for b in range(nf)]
        send = lax.dynamic_slice_in_dim(turned, (y + j) % nd * units, units, 0)
        got.append(move(net, send, perm, y, f))
    return got, down


def mix_kernel(idx, *refs, half, nd):
    ups, down, out = refs[:nd], refs[nd], refs[nd + 1]
    units, width = ups[0].shape
    own = lax.rem(idx[0], nd)
    for j, up in enumerate(ups):
        col = pl.multiple_of(lax.rem(own + nd - j, nd) * width, width)
        for at in range(0, units, half):
            out[2 * at : 2 * at + half, pl.ds(col, width)] = up[at : at + half, :]
    for at in range(0, units, half):
        out[2 * at + half : 2 * at + 2 * half, :] = down[at : at + half, :]


def own_units(net, ups, down, half, y, f):
    whole = pl.BlockSpec(memory_space=pltpu.VMEM)
    return pl.pallas_call(
        partial(mix_kernel, half=half, nd=net.nd),
        in_specs=[pl.BlockSpec(memory_space=pltpu.SMEM)] + [whole] * (net.nd + 1),
        out_specs=whole,
        out_shape=shape((2 * down.shape[0], down.shape[1]), bf16),
        compiler_params=params(16),
        cost_estimate=cost(0, 8 * down.size),
        name="own_units",
    )(jnp.stack([y * net.nf + f]).astype(jnp.int32), *ups, down)


def from_units(net, g_up, g_down, y, f):
    nd, nf = net.nd, net.nf
    grad_down = lax.all_to_all(g_down, "fsdp", split_axis=1, concat_axis=0, tiled=True)
    width = g_up.shape[1] // nd
    own = (y * nf + f) % nd
    got = []
    for j in range(nd):
        perm = [(nd * b + (a + j) % nd, a * nf + b) for a in range(nd) for b in range(nf)]
        send = lax.dynamic_slice_in_dim(g_up, (own - j) % nd * width, width, 1)
        got.append(move(net, send, perm, y, f))
    got = jnp.stack(got)
    rows = [lax.dynamic_index_in_dim(got, (h - y) % nd, 0, keepdims=False) for h in range(nd)]
    return jnp.concatenate(rows, axis=0).T.astype(f32), grad_down.astype(f32)


def move(net, x, perm, y, f):
    fixed = [a for a, b in perm if a == b]
    got = lax.ppermute(x, ("dp", "fsdp"), [(a, b) for a, b in perm if a != b])
    me = y * net.nf + f
    stays = False
    for a in fixed:
        stays = stays | (me == a)
    return jnp.where(stays, x, got) if fixed else got


def local(net, frames, skip_in, cond_in, lengths, drop_mask, time_index, w_skip, w_qkv, w_out, w_up, w_down, w_mod, d_out):
    frames, skip_in, cond_in, d_out = frames[0], skip_in[0], cond_in[0], d_out[0]
    rows, d = frames.shape
    nd, nf, na = net.nd, net.nf, net.na
    y, f = lax.axis_index("dp"), lax.axis_index("fsdp")
    utt = lengths.shape[1]
    group_len = rows * nd
    long = int(group_len * LONG_PART)
    rest = group_len - long
    core_bit = ("fsdp", 1)
    n_skip, n_qkv, n_out = w_skip.shape[1], w_qkv.shape[1], w_out.shape[1]
    part_of = lambda n, share: int(n * share) // 16 * 16
    block = net.attn_index()
    moved = ((f & 1) != y if net.regroup else y < 0).astype(jnp.int32)
    me = jnp.stack([y, f, moved, block]).astype(jnp.int32)
    cut = rows // 2
    cols = w_mod.shape[1]

    (skip_turned,) = flip(w_skip)
    qkv_turned, out_turned, up_turned = flip(w_qkv, w_out, w_up)
    g2 = Gather(net, jnp.concatenate([qkv_turned, out_turned], axis=0), part_of(n_qkv + n_out, 0.33))
    lens = jnp.concatenate([lengths, drop_mask], axis=0)
    ints = jnp.concatenate([lengths, drop_mask, time_index], axis=1)
    bits = net.int_bits[:]

    def more_ints():
        nonlocal ints
        if bits:
            ints = jnp.concatenate([ints, net.swap(ints, ("fsdp", 1 << bits.pop(0)))], axis=0)

    def step(g):
        if g.done < g.common:
            g.join()

    def start(g):
        if g.done < g.common:
            g.send()
        else:
            g.raw = []

    g1 = Gather(net, skip_turned, part_of(n_skip, 0.5))
    while g1.done < g1.common:
        g1.send()
        more_ints()
        g1.raw, (ints, lens, up_turned, w_down), g2.x = tie(g1.raw, [ints, lens, up_turned, w_down], g2.x)
        g1.join()
    g1.send()
    start(g2)
    while bits:
        more_ints()
    g1.raw, g2.raw, (ints, up_turned, w_down) = tie(g1.raw, g2.raw, [ints, up_turned, w_down])
    g1.join()
    step(g2)
    g1.send()
    start(g2)
    up_parts, down = to_units(net, up_turned, w_down, y, f)
    cos, sin, pick, segr, segc, smooth, part, idx, gs = prep(net, ints, me, w_mod, rows, long, rest)
    if net.regroup:
        part = part.reshape(2, nf // 2, utt, cols)
        mod_got = net.swap(lax.dynamic_index_in_dim(part, 1 - y, 0, keepdims=False), ("dp", 1))
        part = lax.dynamic_index_in_dim(part, y, 0, keepdims=False)
    else:
        for b in range(net.db):
            part = part + net.swap(part, ("dp", 1 << b))
        mod_got = part
    g1.raw, g2.raw, (ints, part, mod_got, down) = tie(g1.raw, g2.raw, [ints, part, mod_got, down])
    g1.join()
    theirs = g1.core(g1.x + g1.far)
    step(g2)
    g2.finish_common()
    g2.send()
    skip_t, = place(net, me, g1, theirs, [n_skip])
    (skip_t, lens, part, mod_got, down), up_parts = tie([skip_t, lens, part, mod_got, down], up_parts)
    units = down.shape[0]
    half = units // 2 if units // 2 % 16 == 0 else units
    g3 = Gather(net, own_units(net, up_parts, down, half, y, f), units * 2 if half == units else units)
    start(g3)
    hidden0, mixed = skip_fwd(me, lens, frames, skip_in, cond_in, skip_t)
    (hidden0, mixed, part, mod_got), g2.raw = tie([hidden0, mixed, part, mod_got], g2.raw)

    hidden_got = [net.trade(hidden0)]
    g2.join()
    g2.send()
    if net.regroup:
        part = jnp.broadcast_to((part + mod_got)[:, None], (nf // 2, 2, utt, cols))
    part = part.reshape(nf, utt, cols)
    mod = lax.all_to_all(part, "fsdp", split_axis=0, concat_axis=2, tiled=True)
    (hidden0, mod, d_out), g2.raw, g3.raw = tie([hidden0, mod, d_out], g2.raw, g3.raw)
    mods = three_terms(mod.reshape(utt, nf * cols))
    mod_a, mod_f = mods[:, : 2 * d], mods[:, 2 * d :]
    g2.join()
    theirs = g2.core(g2.x + g2.far)
    qkv_t, out_t = place(net, me, g2, theirs, [n_qkv, n_out])
    step(g3)
    (hidden0, qkv_t, out_t, d_out, mod_a, mod_f), hidden_got, g3.x = tie([hidden0, qkv_t, out_t, d_out, mod_a, mod_f], hidden_got, g3.x)

    start(g3)
    d_f0 = scaled(d_out, gs)
    d_f_got = [net.trade(d_f0[:cut])]
    hidden, normed_a, sent = qkv_fwd(net, idx, hidden0, hidden_got[0], pick, mod_a, qkv_t, cos, sin)
    sent, g3.raw, d_f_got, (d_f0,) = tie(list(sent), g3.raw, d_f_got, [d_f0])
    step(g3)
    g3.finish_common()
    pieces = [sent[0]] + [net.attn_swap(sent[r], r) for r in range(1, na)]
    pieces, (d_f0,), g3.x = tie(pieces, [d_f0], g3.x)
    g3.send()
    d_f_got.append(net.trade(d_f0[cut:]))
    attn_p, lse = attn_fwd(net, idx, pieces, segr, segc, long)
    (lse,), d_f_got, attn_p, g3.raw = tie([lse], d_f_got, list(attn_p), g3.raw)
    attn_p = [attn_p[0]] + [net.attn_swap(attn_p[r], r) for r in range(1, na)]
    g3.join()
    attn_p, near = tie(attn_p, g3.x)
    g3.send()
    near_core = g3.core(near)
    attn, hidden2, normed_f, d_f = out_fwd(net, idx, attn_p, hidden, pick, mod_f, out_t, d_f0, d_f_got)

    view = lambda x: x.reshape(x.shape[0], 2, x.shape[1] // 2, x.shape[2])
    acc, dx, *got1 = ffn(normed_f, d_f, hidden2, [view(x) for x in near_core + near])
    (acc, dx, mixed, skip_in), far, got1 = tie([acc, dx, mixed, skip_in], g3.raw, got1)
    far_core = g3.core(far)
    count = len(far)
    far_core, got1, (mixed, skip_in) = tie(far_core, got1, [mixed, skip_in])
    mixed_got, skip_got = net.trade(mixed), net.trade(skip_in)
    swapped1 = [net.swap(x, core_bit) for x in got1[:count]]
    out_b, dx, *got2 = ffn(normed_f, d_f, acc, [view(x) for x in far_core + far], dx)
    (out_b, dx, mixed_got), got2, swapped1 = tie([out_b, dx, mixed_got], got2, swapped1)
    swapped2 = [net.swap(x, core_bit) for x in got2[:count]]

    d_h2, d_att, sums_f, d_attn_p = out_bwd(net, idx, dx, hidden2, d_f, pick, mod_f[:, d:], out_t)
    (d_h2, d_att, skip_got), d_attn_p, swapped2 = tie([d_h2, d_att, skip_got], list(d_attn_p), swapped2)
    d_attn_p = [d_attn_p[0]] + [net.attn_swap(d_attn_p[r], r) for r in range(1, na)]
    sum_far = [plus(a, b) for a, b in zip(got2[count:], swapped2)]
    d_attn_p, sum_far, (d_att,) = tie(d_attn_p, sum_far, [d_att])
    came = [net.swap(x, o[-2]) for x, o in zip(sum_far, g3.orders)]
    into = outer(net, me, d_att, [attn], n_out, n_qkv + n_out, n_qkv)
    d_attn_p, into, (out_b,) = tie(d_attn_p, list(into), [out_b])

    def send_half(xs, bits):
        n = xs[0].shape[0] // 2
        return [x[:n] for x in xs], [net.swap(x[n:], b) for x, b in zip(xs, bits)]

    all_pairs = d // na // LANES
    pairs = max(1, all_pairs // 2)
    d_sent = attn_bwd(net, idx, pieces, d_attn_p, lse, segr, segc, long, 0, pairs)
    d_sent, came, d_attn_p = tie(list(d_sent), came, d_attn_p)
    d_pieces = [d_sent[0]] + [net.attn_swap(d_sent[r], r) for r in range(1, na)]
    ff = [plus(a, b, c) for a, b, c in zip(got1[count:], swapped1, came)]
    d_attn_p, ff, (out_b,) = tie(d_attn_p, ff, [out_b])
    kept, raw = send_half(ff, [o[-3] for o in g3.orders])
    output_got = net.trade(out_b)
    if all_pairs > pairs:
        d_sent = attn_bwd(net, idx, pieces, d_attn_p, lse, segr, segc, long, pairs, all_pairs - pairs)
        d_sent, raw, d_pieces = tie(list(d_sent), raw, d_pieces)
        d_pieces += [d_sent[0]] + [net.attn_swap(d_sent[r], r) for r in range(1, na)]
    ff = jnp.stack([plus(a, b) for a, b in zip(kept, raw)], axis=1)
    common = list(reversed(g3.orders[0][:-3]))
    d_pieces, (ff,) = tie(d_pieces, [ff])
    raw = []
    if common:
        kept, raw = send_half([ff], [common[0]])
    d_qkv = turn_back(net, idx, d_pieces, cos, sin, d)
    d_h, sums_a = qkv_bwd(d_qkv, hidden, d_h2, pick, mod_a[:, d:], qkv_t)
    (d_h, sums_a, d_qkv, output_got), raw = tie([d_h, sums_a, d_qkv, output_got], raw)
    if common:
        ff = plus(kept[0], raw[0])
    raw = []
    if len(common) > 1:
        kept, raw = send_half([ff], [common[1]])
    keep1, send1 = outer(net, me, d_h, [mixed, mixed_got, skip_in, skip_got], n_skip, n_skip, 0, choose=True)
    (keep1, send1, d_qkv, d_h), = tie([keep1, send1, d_qkv, d_h])
    got1 = net.swap(send1, core_bit)
    keep2, send2 = outer(net, me, d_qkv, [normed_a], n_qkv, n_qkv + n_out, 0, into)
    (keep2, send2, keep1, got1), = tie([keep2, send2, keep1, got1])
    got2 = net.swap(send2, core_bit)
    s1 = Sum(net, plus(keep1, got1))
    s1.send()
    (keep2, got2), = tie([keep2, got2])
    s2 = Sum(net, plus(keep2, got2))
    (s2.parts[0][0], s2.parts[1][0], sums_a, d_h, out_b), s1.raw = tie(
        [s2.parts[0][0], s2.parts[1][0], sums_a, d_h, out_b], s1.raw
    )
    s2.send()
    s1.join()
    s1.send()
    s1.raw, raw, (out_b, d_h) = tie(s1.raw, raw, [out_b, d_h])
    if len(common) > 1:
        ff = plus(kept[0], raw[0])
    for bit in common[2:]:
        kept, raw = send_half([ff], [bit])
        ff = plus(kept[0], raw[0])
    ff = ff.reshape(-1, 2, half, d)
    s1.join()
    s1.send()
    output = net.traded(out_b, output_got)
    grad_up, grad_down = from_units(net, ff[:, 0].reshape(units, d), ff[:, 1].reshape(units, d), y, f)
    s1.raw, s2.raw, (sums_a, output, grad_up, grad_down, d_h) = tie(s1.raw, s2.raw, [sums_a, output, grad_up, grad_down, d_h])
    d_h_got = [net.trade(d_h[:cut])]
    s2.join()
    s2.send()
    s1.join()
    if s1.left:
        s1.send()

    d_mod = jnp.concatenate([sums_a, sums_f], axis=1).reshape(utt, nf, cols).transpose(1, 0, 2)
    d_mod = lax.all_to_all(d_mod, "fsdp", split_axis=0, concat_axis=0, tiled=True)
    s1.raw, s2.raw, (d_mod, d_h), d_h_got = tie(s1.raw, s2.raw, [d_mod, d_h], d_h_got)
    d_h_got.append(net.trade(d_h[cut:]))
    if net.regroup:
        pair_sum = d_mod.reshape(nf // 2, 2, utt, cols).sum(axis=1)
        here = (jnp.arange(2) == y).astype(f32)
        d_mod = pair_sum[None] * here[:, None, None, None]
    d_mod = d_mod.reshape(nf * utt, cols)
    for b in range(net.db):
        d_mod = d_mod + net.swap(d_mod, ("dp", 1 << b))
    while s2.left:
        s2.join()
        if s1.left:
            s1.join()
        if s2.left:
            s2.send()
        if s1.left:
            s1.send()
        if s1.left and s2.left:
            s1.raw, s2.raw, d_h_got = tie(s1.raw, s2.raw, d_h_got)
        elif s2.left == 2:
            s2.raw, d_h_got = tie(s2.raw, d_h_got)
    d_frames, d_skip = skip_bwd(me, d_h, d_h_got, skip_t)
    g_two = s2.finish()
    grad_qkv = g_two[:n_qkv].T.astype(f32)
    grad_out = g_two[n_qkv:].T.astype(f32)
    grad_skip = s1.finish().T.astype(f32)
    grad_mod = jnp.dot(smooth.astype(f32).T, d_mod, precision=highest)

    return (output[None], d_frames[None], d_skip[None], grad_skip, grad_qkv, grad_out, grad_up, grad_down, grad_mod)


def solution(mesh):
    rows = P("fsdp", "dp", None)
    ints = P("fsdp", None)
    weight = P("dp", "fsdp")
    return jax.shard_map(
        partial(local, Net(mesh)),
        mesh=mesh,
        in_specs=(rows, rows, rows, ints, ints, ints, *([weight] * 6), rows),
        out_specs=(rows, rows, rows, *([weight] * 6)),
        check_vma=False,
    )
```
